32 devices in a mesh: seq: 8 (over z, y), row: 4 (over x, core).
Axes of the slice: x: 2, y: 2, z: 4, core: 2. Of those that a mesh axis runs over, the one named last changes fastest.
Arguments:
- tokens: bfloat16 [32, 2048, 512], P('row', 'seq'), may hold values from -6 to 6
- valid_count: int32 [32], P('row'), may hold values from 1024 to 2048, as said below
- norm_gain: bfloat16 [512], replicated, may hold values from 0.099609375 to 1.8984375
- value_weight: bfloat16 [512, 1024], replicated, may hold values from -0.25 to 0.25
- ema_forget: float32 [512, 16], replicated, may hold values from 5e-07 to 0.03
- ema_beta: float32 [512, 16], replicated, may hold values from -4 to 4
- ema_eta: float32 [512, 16], replicated, may hold values from -1.5 to 1.5
- ema_omega: float32 [512], replicated, may hold values from -4 to 4
- base_weight: bfloat16 [512, 2176], replicated, may hold values from -0.25 to 0.25
- qk_gain: bfloat16 [2, 128], replicated, may hold values from -8 to 8
- qk_bias: bfloat16 [2, 128], replicated, may hold values from -6 to 6
- output_weight: bfloat16 [1024, 512], replicated, may hold values from -0.5 to 0.5
- ffn_gain: bfloat16 [512], replicated, may hold values from 0.099609375 to 1.8984375
- ffn_in: bfloat16 [512, 1024], replicated, may hold values from -0.25 to 0.25
- ffn_out: bfloat16 [1024, 512], replicated, may hold values from -0.1875 to 0.1875
- cotangent: bfloat16 [32, 2048, 512], P('row', 'seq'), may hold values from -6 to 6
Outputs:
- block_out: bfloat16 [32, 2048, 512], P('row', 'seq')
- grad_tokens: bfloat16 [32, 2048, 512], P('row', 'seq')
- grad_norm_gain: float32 [512], replicated
- grad_value_weight: float32 [512, 1024], replicated
- grad_ema_forget: float32 [512, 16], replicated
- grad_ema_beta: float32 [512, 16], replicated
- grad_ema_eta: float32 [512, 16], replicated
- grad_ema_omega: float32 [512], replicated
- grad_base_weight: float32 [512, 2176], replicated
- grad_qk_gain: float32 [2, 128], replicated
- grad_qk_bias: float32 [2, 128], replicated
- grad_output_weight: float32 [1024, 512], replicated
- grad_ffn_gain: float32 [512], replicated
- grad_ffn_in: float32 [512, 1024], replicated
- grad_ffn_out: float32 [1024, 512], replicated
The draws below stay inside these ranges and needn't reach their ends.
Inputs may be any that keep to these rules, and one draw needn't show every extreme that they name: `valid_count`: each row's count of valid positions; positions at or past it are padding.
All inputs are finite; a program needn't handle non-finite values.
Results may differ from the reference program's by a relative error of at most 0.03.
Values sent between devices are 32-bit elements; how exact they have to be, the bound alone decides.
No kernel may reach another device: no remote copies, remote signals or barrier semaphores. Data moves between devices by JAX's collectives and lax.ppermute only.
A program may use at most 320 MiB of HBM per device.

```python
import math
import jax
import jax.numpy as jnp
from jax import lax

D = 512
ZDIM = 128
VDIM = 1024
NDIM = 16
GROUP = 128
FFN = 1024
ROWS = 32
LENGTH = 2048


def draw_valid_count(key, part):
    first_key, second_key = jax.random.split(key)
    counts = jax.random.randint(first_key, (ROWS,), LENGTH // 2, LENGTH + 1)
    shuffled = jax.random.permutation(second_key, ROWS)
    counts = counts.at[shuffled[0]].set(LENGTH)
    counts = counts.at[shuffled[1]].set(LENGTH // 2)
    return counts.astype(jnp.int32)


def shard_levels(rng, shape, shards, smallest, largest):
    def one(position, parts):
        heights = jax.random.uniform(jax.random.fold_in(jax.random.fold_in(rng, 6), position), (parts,), jnp.float32, smallest / len(shards), largest / len(shards))
        return jnp.repeat(jnp.exp(heights), shape[position] // parts).reshape((-1,) + (1,) * (len(shape) - position - 1))

    factor_of = one(*shards[0])
    for cut in shards[1:]:
        factor_of = factor_of * one(*cut)
    return factor_of


def bell_draw(key, shape, scale, reach, cuts=(), kind=jnp.bfloat16):
    gain = shard_levels(key, shape, cuts, -0.22, 0.18) if cuts else 1.0
    drawn = jax.random.normal(key, shape, jnp.float32) * scale * gain
    return jnp.minimum(jnp.maximum(drawn, -reach), reach).astype(kind)


def setup_inputs(seed: int = 0) -> dict:
    keys = jax.random.split(jax.random.key(seed), 17)
    return {
        "tokens": bell_draw(keys[0], (ROWS, LENGTH, D), 1.0, 6.0, ((0, 4), (1, 8))),
        "valid_count": draw_valid_count(jax.random.fold_in(keys[16], 71), 0),
        "norm_gain": jnp.clip(1.0 + 0.18 * jax.random.normal(keys[2], (D,), jnp.float32), 0.099609375, 1.8984375).astype(jnp.bfloat16),
        "value_weight": bell_draw(keys[3], (D, VDIM), D ** -0.5, 0.25),
        "ema_forget": jnp.clip(jnp.exp(jax.random.uniform(keys[4], (D, NDIM), jnp.float32, math.log(4.999999987376214e-07), math.log(0.03))), 4.999999987376214e-07, 0.03),
        "ema_beta": bell_draw(keys[5], (D, NDIM), 1.0, 4.0, (), jnp.float32),
        "ema_eta": bell_draw(keys[6], (D, NDIM), NDIM ** -0.5, 1.5, (), jnp.float32),
        "ema_omega": bell_draw(keys[7], (D,), 1.0, 4.0, (), jnp.float32),
        "base_weight": bell_draw(keys[8], (D, ZDIM + VDIM + 2 * D), D ** -0.5, 0.25),
        "qk_gain": bell_draw(keys[9], (2, ZDIM), 2.0, 8.0),
        "qk_bias": bell_draw(keys[10], (2, ZDIM), 1.5, 6.0),
        "output_weight": bell_draw(keys[11], (VDIM, D), (VDIM // 8) ** -0.5, 0.5),
        "ffn_gain": jnp.clip(1.0 + 0.18 * jax.random.normal(keys[12], (D,), jnp.float32), 0.099609375, 1.8984375).astype(jnp.bfloat16),
        "ffn_in": bell_draw(keys[13], (D, FFN), D ** -0.5, 0.25),
        "ffn_out": bell_draw(keys[14], (FFN, D), FFN ** -0.5, 0.1875),
        "cotangent": bell_draw(keys[15], (ROWS, LENGTH, D), 1.0, 6.0, ((0, 4), (1, 8))),
    }


epsilon = 1e-05
very_low = -1e+30
highest = lax.Precision.HIGHEST

@jax.custom_vjp
def low(v):
    return lax.optimization_barrier(v.astype(jnp.bfloat16)).astype(jnp.float32)

@jax.custom_vjp
def low_back(v):
    return v

def low_keep(v):
    return (low(v), None)

def low_pass(kept, grad):
    return (grad,)

def back_keep(v):
    return (v, None)

def back_low(kept, grad):
    return (low(grad),)
low.defvjp(low_keep, low_pass)
low_back.defvjp(back_keep, back_low)

def layer_norm(inputs, scales):
    centered = inputs - lax.optimization_barrier(jnp.mean(inputs, axis=-1, keepdims=True))
    spread = lax.optimization_barrier(jnp.mean(centered * centered, axis=-1, keepdims=True))
    return centered * lax.rsqrt(spread + epsilon) * scales

def mat_mul(first_op, second_op):
    return jnp.dot(first_op, second_op, precision=highest, preferred_element_type=jnp.float32)

def ema_scan(inputs, ema_forget, ema_beta, ema_eta):
    retain = 1.0 - ema_forget
    inflow = ema_beta * jnp.sqrt(ema_forget * (2.0 - ema_forget))
    row_count = inputs.shape[0]
    blocks = inputs.reshape(row_count, LENGTH // GROUP, GROUP, D).transpose(1, 2, 0, 3)

    def one_step(hidden, column):
        hidden = retain * hidden + inflow * column[:, :, None]
        return (hidden, lax.optimization_barrier(jnp.sum(ema_eta * hidden, axis=-1)))

    def one_block(hidden, block_in):
        return lax.scan(one_step, hidden, block_in)
    start_state = jnp.zeros((row_count, D, NDIM), jnp.float32)
    _, outputs = lax.scan(jax.checkpoint(one_block), start_state, blocks)
    return outputs.transpose(2, 0, 1, 3).reshape(row_count, LENGTH, D)

def forward(tokens, norm_gain, value_weight, ema_forget, ema_beta, ema_eta, ema_omega, base_weight, qk_gain, qk_bias, output_weight, ffn_gain, ffn_in, ffn_out, valid_mask):
    normed = layer_norm(tokens, norm_gain)
    value_pre = low_back(mat_mul(low(normed), value_weight))
    value_low = low(jax.nn.silu(value_pre))
    ema_y = ema_scan(normed * valid_mask[:, :, None], ema_forget, ema_beta, ema_eta)
    mixed = low(jax.nn.silu(ema_y + ema_omega * normed))
    base_proj = low_back(mat_mul(mixed, base_weight))
    shared_pre = base_proj[:, :, :ZDIM]
    reset_pre = base_proj[:, :, ZDIM:ZDIM + VDIM]
    update_pre = base_proj[:, :, ZDIM + VDIM:ZDIM + VDIM + D]
    candidate_pre = base_proj[:, :, ZDIM + VDIM + D:]
    shared_act = jax.nn.silu(shared_pre)
    query_low = low(shared_act * qk_gain[0] + qk_bias[0])
    key_low = low(shared_act * qk_gain[1] + qk_bias[1])
    block_count = ROWS * (LENGTH // GROUP)
    query_blocks = query_low.reshape(block_count, GROUP, ZDIM)
    key_blocks = key_low.reshape(block_count, GROUP, ZDIM)
    value_blocks = value_low.reshape(block_count, GROUP, VDIM)
    raw_scores = low_back(jnp.einsum('ntz,nsz->nts', query_blocks, key_blocks, precision=highest))
    scores = raw_scores * ZDIM ** (-0.5)
    places = jnp.arange(GROUP, dtype=jnp.int32)
    causal = places[:, None] >= places[None, :]
    diagonal = places[:, None] == places[None, :]
    block_valid = valid_mask.reshape(block_count, GROUP)
    allowed = causal[None] & ((block_valid[:, None, :] > 0.5) | diagonal[None])
    masked = jnp.where(allowed, scores, very_low)
    row_top = lax.optimization_barrier(jnp.max(masked, axis=-1, keepdims=True))
    log_total = row_top + jnp.log(lax.optimization_barrier(jnp.sum(jnp.exp(masked - row_top), axis=-1, keepdims=True)))
    probs_low = low(jnp.where(allowed, jnp.exp(masked - log_total), 0.0))
    attended = low_back(jnp.einsum('nts,nsv->ntv', probs_low, value_blocks, precision=highest))
    attended = attended.reshape(ROWS, LENGTH, VDIM)
    product_low = low(attended * jax.nn.silu(reset_pre))
    projected = low_back(mat_mul(product_low, output_weight))
    after_mix = tokens + jax.nn.sigmoid(update_pre) * (jax.nn.silu(candidate_pre + projected) - tokens)
    ffn_low = low(layer_norm(after_mix, ffn_gain))
    inner_pre = low_back(mat_mul(ffn_low, ffn_in))
    ffn_res = low_back(mat_mul(low(jax.nn.silu(inner_pre)), ffn_out))
    return after_mix + ffn_res

def reference(tokens, valid_count, norm_gain, value_weight, ema_forget, ema_beta, ema_eta, ema_omega, base_weight, qk_gain, qk_bias, output_weight, ffn_gain, ffn_in, ffn_out, cotangent):
    places = jnp.arange(LENGTH, dtype=jnp.int32)
    valid_mask = (places[None, :] < valid_count[:, None].astype(jnp.int32)).astype(jnp.float32)
    params = (tokens.astype(jnp.float32), norm_gain.astype(jnp.float32), value_weight.astype(jnp.float32), ema_forget.astype(jnp.float32), ema_beta.astype(jnp.float32), ema_eta.astype(jnp.float32), ema_omega.astype(jnp.float32), base_weight.astype(jnp.float32), qk_gain.astype(jnp.float32), qk_bias.astype(jnp.float32), output_weight.astype(jnp.float32), ffn_gain.astype(jnp.float32), ffn_in.astype(jnp.float32), ffn_out.astype(jnp.float32))

    def whole(*operands):
        return forward(*operands, valid_mask)
    block_out, pull_back = jax.vjp(whole, *params)
    grads = pull_back(cotangent.astype(jnp.float32))
    return (block_out.astype(jnp.bfloat16), grads[0].astype(jnp.bfloat16), grads[1], grads[2], grads[3], grads[4], grads[5], grads[6], grads[7], grads[8], grads[9], grads[10], grads[11], grads[12], grads[13])
```

```python
import functools

import jax
import jax.numpy as jnp
from jax import lax
from jax.experimental import pallas as pl
from jax.experimental.pallas import tpu as pltpu
from jax.sharding import PartitionSpec as P

GROUP = 128
STEPS = 32
LAG = 8
LANES = 128

epsilon = 1e-05
very_low = -1e30
scan_params = pltpu.CompilerParams(vmem_limit_bytes=48 * 2**20)


def lane_slices(width):
    return [slice(low, low + LANES) for low in range(0, width, LANES)]


def spread_rows(ref, index, lanes, rows):
    return jnp.broadcast_to(ref[index : index + 1, lanes], (rows, LANES))


def add_all(parts):
    while len(parts) > 1:
        parts = [
            parts[at] + parts[at + 1] if at + 1 < len(parts) else parts[at]
            for at in range(0, len(parts), 2)
        ]
    return parts[0]


def enter_body(count_ref, tokens_ref, gain_ref, retain_ref, low_ref, turned_ref, end_ref, state):
    step = pl.program_id(0)
    rows, steps, width = tokens_ref.shape
    states = retain_ref.shape[0]

    @pl.when(step == 0)
    def _():
        state[...] = jnp.zeros_like(state)

    values = tokens_ref[...].astype(jnp.float32)
    centered = values - jnp.mean(values, axis=-1, keepdims=True)
    spread = jnp.mean(centered * centered, axis=-1, keepdims=True)
    normed = centered * lax.rsqrt(spread + epsilon) * gain_ref[...]
    low_ref[...] = normed.astype(jnp.bfloat16)
    places = step * steps + lax.broadcasted_iota(jnp.int32, (steps, 1), 0)
    kept = jnp.stack([jnp.where(places < count_ref[row], normed[row], 0.0) for row in range(rows)])
    for lanes in lane_slices(width):
        for unit in range(steps // LAG):
            part = slice(unit * LAG, (unit + 1) * LAG)
            turned_ref[part, :, lanes] = jnp.swapaxes(kept[:, part, lanes], 0, 1)
    for lanes in lane_slices(width):
        retain = [spread_rows(retain_ref, j, lanes, rows) for j in range(states)]

        def unit_step(unit, hidden):
            for within in range(LAG):
                entry = turned_ref[unit * LAG + within, :, lanes]
                hidden = [retain[j] * hidden[j] + entry for j in range(states)]
            return hidden

        hidden = lax.fori_loop(
            0, steps // LAG, unit_step, [state[j, :, lanes] for j in range(states)]
        )
        for j in range(states):
            state[j, :, lanes] = hidden[j]

    @pl.when(step == pl.num_programs(0) - 1)
    def _():
        end_ref[...] = state[...]


def whole_spec(shape):
    return pl.BlockSpec(shape, lambda step: (0,) * len(shape))


def enter_call(counts, tokens, gain, retain):
    rows, length, width = tokens.shape
    states = retain.shape[0]
    natural = pl.BlockSpec((rows, STEPS, width), lambda step: (0, step, 0))
    return pl.pallas_call(
        enter_body,
        grid=(length // STEPS,),
        in_specs=[
            pl.BlockSpec(memory_space=pltpu.SMEM),
            natural,
            whole_spec((1, width)),
            whole_spec((states, width)),
        ],
        out_specs=(
            natural,
            pl.BlockSpec((STEPS, rows, width), lambda step: (step, 0, 0)),
            whole_spec((states, rows, width)),
        ),
        out_shape=(
            jax.ShapeDtypeStruct(tokens.shape, jnp.bfloat16),
            jax.ShapeDtypeStruct((length, rows, width), jnp.float32),
            jax.ShapeDtypeStruct((states, rows, width), jnp.float32),
        ),
        scratch_shapes=[pltpu.VMEM((states, rows, width), jnp.float32)],
        compiler_params=scan_params,
        name="enter",
    )(counts, tokens, gain, retain)


def average_body(turned_ref, retain_ref, mix_ref, start_ref, out_ref, end_ref, state):
    step = pl.program_id(0)
    steps, rows, width = turned_ref.shape
    states = retain_ref.shape[0]

    @pl.when(step == 0)
    def _():
        state[...] = start_ref[...]

    for lanes in lane_slices(width):
        retain = [spread_rows(retain_ref, j, lanes, rows) for j in range(states)]
        mix = [spread_rows(mix_ref, j, lanes, rows) for j in range(states)]

        def unit_step(unit, hidden):
            sums = []
            for within in range(LAG):
                entry = turned_ref[unit * LAG + within, :, lanes]
                hidden = [retain[j] * hidden[j] + entry for j in range(states)]
                sums.append(add_all([mix[j] * hidden[j] for j in range(states)]))
            out_ref[:, pl.ds(unit * LAG, LAG), lanes] = jnp.swapaxes(jnp.stack(sums), 0, 1)
            return hidden

        hidden = lax.fori_loop(
            0, steps // LAG, unit_step, [state[j, :, lanes] for j in range(states)]
        )
        for j in range(states):
            state[j, :, lanes] = hidden[j]

    @pl.when(step == pl.num_programs(0) - 1)
    def _():
        end_ref[...] = state[...]


def average_call(turned, retain, mix, start):
    length, rows, width = turned.shape
    states = retain.shape[0]
    held = (states, rows, width)
    return pl.pallas_call(
        average_body,
        grid=(length // STEPS,),
        in_specs=[
            pl.BlockSpec((STEPS, rows, width), lambda step: (step, 0, 0)),
            whole_spec((states, width)),
            whole_spec((states, width)),
            whole_spec(held),
        ],
        out_specs=(
            pl.BlockSpec((rows, STEPS, width), lambda step: (0, step, 0)),
            whole_spec(held),
        ),
        out_shape=(
            jax.ShapeDtypeStruct((rows, length, width), jnp.float32),
            jax.ShapeDtypeStruct(held, jnp.float32),
        ),
        scratch_shapes=[pltpu.VMEM(held, jnp.float32)],
        compiler_params=scan_params,
        name="average",
    )(turned, retain, mix, start)


def return_body(grad_ref, retain_ref, turned_ref, end_ref, state):
    step = pl.program_id(0)
    rows, steps, width = grad_ref.shape
    states = retain_ref.shape[0]

    @pl.when(step == 0)
    def _():
        state[...] = jnp.zeros_like(state)

    for lanes in lane_slices(width):
        retain = [spread_rows(retain_ref, j, lanes, rows) for j in range(states)]

        def unit_step(unit, hidden):
            part = pl.ds((steps // LAG - 1 - unit) * LAG, LAG)
            turned = jnp.swapaxes(grad_ref[:, part, lanes], 0, 1)
            turned_ref[part, :, lanes] = turned
            for within in reversed(range(LAG)):
                hidden = [retain[j] * hidden[j] + turned[within] for j in range(states)]
            return hidden

        hidden = lax.fori_loop(
            0, steps // LAG, unit_step, [state[j, :, lanes] for j in range(states)]
        )
        for j in range(states):
            state[j, :, lanes] = hidden[j]

    @pl.when(step == pl.num_programs(0) - 1)
    def _():
        end_ref[...] = state[...]


def return_call(grad, retain):
    rows, length, width = grad.shape
    states = retain.shape[0]
    last = length // STEPS - 1
    return pl.pallas_call(
        return_body,
        grid=(length // STEPS,),
        in_specs=[
            pl.BlockSpec((rows, STEPS, width), lambda step: (0, last - step, 0)),
            whole_spec((states, width)),
        ],
        out_specs=(
            pl.BlockSpec((STEPS, rows, width), lambda step: (last - step, 0, 0)),
            whole_spec((states, rows, width)),
        ),
        out_shape=(
            jax.ShapeDtypeStruct((length, rows, width), jnp.float32),
            jax.ShapeDtypeStruct((states, rows, width), jnp.float32),
        ),
        scratch_shapes=[pltpu.VMEM((states, rows, width), jnp.float32)],
        compiler_params=scan_params,
        name="back_enter",
    )(grad, retain)


def adjoint_body(
    grad_ref,
    turned_ref,
    retain_ref,
    inverse_ref,
    unit_ref,
    mix_ref,
    later_ref,
    end_ref,
    out_ref,
    cross_ref,
    border_ref,
    lag_ref,
    adjoint,
    state,
    kept,
):
    step = pl.program_id(0)
    steps, rows, width = grad_ref.shape
    states = retain_ref.shape[0]
    half = states // 2
    units = steps // LAG

    @pl.when(step == 0)
    def _():
        adjoint[...] = later_ref[...]
        state[...] = end_ref[...]
        cross_ref[...] = jnp.zeros_like(cross_ref)
        border_ref[...] = jnp.zeros_like(border_ref)
        lag_ref[...] = jnp.zeros_like(lag_ref)

    for lanes in lane_slices(width):
        for first in range(0, states, half):
            chosen = range(first, first + half)
            retain = [spread_rows(retain_ref, j, lanes, rows) for j in chosen]
            inverse = [spread_rows(inverse_ref, j, lanes, rows) for j in chosen]
            mix = [spread_rows(mix_ref, j, lanes, rows) for j in chosen]

            def unit_step(unit, carried):
                after, hidden, cross = carried
                unit = units - 1 - unit
                later = after
                sums = []
                for within in reversed(range(LAG)):
                    place = unit * LAG + within
                    entry = turned_ref[place, :, lanes]
                    grad = grad_ref[place, :, lanes]
                    after = [retain[m] * after[m] + grad for m in range(half)]
                    total = add_all([mix[m] * after[m] for m in range(half)])
                    if first == 0:
                        kept[place] = total
                    else:
                        sums.append(total + kept[place])
                    hidden = [(hidden[m] - entry) * inverse[m] for m in range(half)]
                    cross = [cross[m] + after[m] * hidden[m] for m in range(half)]
                for m, j in enumerate(chosen):
                    unit_decay = spread_rows(unit_ref, j, lanes, rows)
                    border_ref[j, :, lanes] += hidden[m] * (after[m] - unit_decay * later[m])
                if first > 0:
                    out_ref[:, pl.ds(unit * LAG, LAG), lanes] = jnp.swapaxes(
                        jnp.stack(sums[::-1]), 0, 1
                    )
                return after, hidden, cross

            after, hidden, cross = lax.fori_loop(
                0,
                units,
                unit_step,
                tuple(
                    [ref[j, :, lanes] for j in chosen] for ref in (adjoint, state, cross_ref)
                ),
            )
            for m, j in enumerate(chosen):
                adjoint[j, :, lanes] = after[m]
                state[j, :, lanes] = hidden[m]
                cross_ref[j, :, lanes] = cross[m]

        def lag_step(unit, lags):
            entries = [turned_ref[unit * LAG + at, :, lanes] for at in range(LAG)]
            grads = [grad_ref[unit * LAG + at, :, lanes] for at in range(LAG)]
            return [
                lags[lag] + add_all([grads[at] * entries[at - lag] for at in range(lag, LAG)])
                for lag in range(LAG)
            ]

        lags = lax.fori_loop(0, units, lag_step, [lag_ref[at, :, lanes] for at in range(LAG)])
        for at in range(LAG):
            lag_ref[at, :, lanes] = lags[at]


def adjoint_call(grad, turned, retain, inverse, unit_decay, mix, later, end):
    length, rows, width = grad.shape
    states = retain.shape[0]
    held = (states, rows, width)
    last = length // STEPS - 1
    turned_spec = pl.BlockSpec((STEPS, rows, width), lambda step: (last - step, 0, 0))
    param_spec = whole_spec((states, width))
    return pl.pallas_call(
        adjoint_body,
        grid=(length // STEPS,),
        in_specs=[turned_spec] * 2 + [param_spec] * 4 + [whole_spec(held)] * 2,
        out_specs=(
            pl.BlockSpec((rows, STEPS, width), lambda step: (0, last - step, 0)),
            whole_spec(held),
            whole_spec(held),
            whole_spec((LAG, rows, width)),
        ),
        out_shape=(
            jax.ShapeDtypeStruct((rows, length, width), jnp.float32),
            jax.ShapeDtypeStruct(held, jnp.float32),
            jax.ShapeDtypeStruct(held, jnp.float32),
            jax.ShapeDtypeStruct((LAG, rows, width), jnp.float32),
        ),
        scratch_shapes=[
            pltpu.VMEM(held, jnp.float32),
            pltpu.VMEM(held, jnp.float32),
            pltpu.VMEM((STEPS, rows, LANES), jnp.float32),
        ],
        compiler_params=scan_params,
        name="adjoint",
    )(grad, turned, retain, inverse, unit_decay, mix, later, end)


def carried_in(local, decay, axis, backward):
    count, mine = lax.axis_size(axis), lax.axis_index(axis)
    if backward:
        mine = count - 1 - mine

    def moved(value, hop):
        if backward:
            pairs = [(at, at - hop) for at in range(hop, count)]
        else:
            pairs = [(at, at + hop) for at in range(count - hop)]
        return lax.ppermute(value, axis, pairs)

    total = moved(local, 1)
    hop = 1
    while hop < count - 1:
        total = total + decay * moved(total, hop)
        decay = decay * decay
        hop *= 2
    return total


mesh_axes = ("seq", "row")


def device_total():
    return lax.axis_size("seq") * lax.axis_size("row")


def device_place():
    return lax.axis_index("seq") * lax.axis_size("row") + lax.axis_index("row")


def swapped(value, bit):
    return lax.ppermute(value, mesh_axes, [(at, at ^ bit) for at in range(device_total())])


def half_summed(value, bit):
    half = value.shape[0] // 2
    mine = (device_place() // bit) % 2
    sent = lax.dynamic_slice_in_dim(value, (1 - mine) * half, half, 0)
    kept = lax.dynamic_slice_in_dim(value, mine * half, half, 0)
    return kept + swapped(sent, bit)


def both_halves(value, bit):
    mine = (device_place() // bit) % 2 == 1
    other = swapped(value, bit)
    return jnp.concatenate([jnp.where(mine, other, value), jnp.where(mine, value, other)], axis=0)


def link_orders():
    total = device_total()
    bits = [1 << at for at in range(total.bit_length() - 1)]
    if (lax.axis_size("seq"), lax.axis_size("row")) == (8, 4):
        core, x, y, z_low, z_high = bits
        return (
            (core, x, y, z_low, z_high),
            (core, y, z_low, z_high, x),
            (core, z_low, z_high, x, y),
        )
    third = len(bits) // 3
    return tuple(bits[turn * third :] + bits[: turn * third] for turn in range(3))


def summed_everywhere(values, choices):
    orders = link_orders()
    for at in range(len(orders[0])):
        values = [half_summed(value, orders[pick][at]) for value, pick in zip(values, choices)]
    for at in reversed(range(len(orders[0]))):
        values = [both_halves(value, orders[pick][at]) for value, pick in zip(values, choices)]
    return values


def small_sum(value):
    bits = [1 << at for at in range(device_total().bit_length() - 1)]
    first = len(bits) % 2
    groups = [bits[:first]] if first else []
    groups += [bits[at : at + 2] for at in range(first, len(bits), 2)]
    for group in groups:
        partners = [group[0]] if len(group) == 1 else [group[0], group[1], group[0] + group[1]]
        arrived = [swapped(value, partner) for partner in partners]
        if len(arrived) == 1:
            value = value + arrived[0]
        else:
            value = (value + arrived[0]) + (arrived[1] + arrived[2])
    return value


def power_of(value, exponent):
    result = None
    while exponent:
        if exponent & 1:
            result = value if result is None else result * value
        value = value * value
        exponent >>= 1
    return result


def layer_norm(inputs, scales):
    centered = inputs - jnp.mean(inputs, axis=-1, keepdims=True)
    spread = jnp.mean(centered * centered, axis=-1, keepdims=True)
    return centered * lax.rsqrt(spread + epsilon) * scales


def plain_dot(first_op, second_op):
    return jnp.dot(first_op, second_op, preferred_element_type=jnp.float32)


def outer_dot(first_op, second_op):
    return lax.dot_general(
        first_op, second_op, (((0,), (0,)), ((), ())), preferred_element_type=jnp.float32
    )


def inner_dot(first_op, second_op):
    return lax.dot_general(
        first_op, second_op, (((1,), (1,)), ((), ())), preferred_element_type=jnp.float32
    )


def mix_piece(ema_flat, normed, ema_omega):
    return jax.nn.silu(ema_flat + ema_omega * normed)


def query_piece(shared_pre, gains, biases):
    shared_act = jax.nn.silu(shared_pre)
    return (shared_act * gains[0] + biases[0], shared_act * gains[1] + biases[1])


def merge_piece(candidate_pre, projected, update_pre, flat_in):
    return flat_in + jax.nn.sigmoid(update_pre) * (jax.nn.silu(candidate_pre + projected) - flat_in)


def per_device(
    tokens,
    valid_count,
    norm_gain,
    value_weight,
    ema_forget,
    ema_beta,
    ema_eta,
    ema_omega,
    base_weight,
    qk_gain,
    qk_bias,
    output_weight,
    ffn_gain,
    ffn_in,
    ffn_out,
    cotangent,
):
    row_count, seq_len, model_width = tokens.shape
    block_total = seq_len // GROUP
    query_width = qk_gain.shape[1]
    value_width = value_weight.shape[1]
    token_count = row_count * seq_len
    block_count = row_count * block_total
    score_scale = query_width ** (-0.5)
    device = lax.axis_index("seq")
    places = device * seq_len + jnp.arange(seq_len, dtype=jnp.int32)
    valid_mask = (places[None, :] < valid_count[:, None]).astype(jnp.float32)
    flat_in = tokens.astype(jnp.float32).reshape(token_count, model_width)
    normed, norm_back = jax.vjp(layer_norm, flat_in, norm_gain.astype(jnp.float32))
    normed_low = normed.astype(jnp.bfloat16)
    value_pre = plain_dot(normed_low, value_weight)
    value_act, value_back = jax.vjp(jax.nn.silu, value_pre)
    value_low = value_act.astype(jnp.bfloat16)
    forget, beta, eta = ema_forget.T, ema_beta.T, ema_eta.T
    retain = 1.0 - forget
    gate = jnp.sqrt(forget * (2.0 - forget))
    inflow = beta * gate
    mix = eta * inflow
    span_decay = power_of(retain, seq_len)[:, None, :]
    counts = valid_count - device * seq_len
    _, turned, device_end = enter_call(
        counts, tokens, norm_gain.astype(jnp.float32)[None], retain
    )
    incoming = carried_in(device_end, span_decay, "seq", False)
    ema_out, state_end = average_call(turned, retain, mix, incoming)
    ema_flat = ema_out.reshape(token_count, model_width)
    mixed, mix_back = jax.vjp(mix_piece, ema_flat, normed, ema_omega)
    mixed_low = mixed.astype(jnp.bfloat16)
    base_proj = plain_dot(mixed_low, base_weight)
    shared_pre = base_proj[:, :query_width]
    reset_pre = base_proj[:, query_width : query_width + value_width]
    update_pre = base_proj[:, query_width + value_width : query_width + value_width + model_width]
    candidate_pre = base_proj[:, query_width + value_width + model_width :]
    (query_vec, key_vec), query_back = jax.vjp(
        query_piece, shared_pre, qk_gain.astype(jnp.float32), qk_bias.astype(jnp.float32)
    )
    query_low = query_vec.astype(jnp.bfloat16).reshape(block_count, GROUP, query_width)
    key_low = key_vec.astype(jnp.bfloat16).reshape(block_count, GROUP, query_width)
    value_blocks = value_low.reshape(block_count, GROUP, value_width)
    positions = jnp.arange(GROUP, dtype=jnp.int32)
    causal = positions[:, None] >= positions[None, :]
    diagonal = positions[:, None] == positions[None, :]
    block_valid = valid_mask.reshape(block_count, GROUP)
    allowed = causal[None] & ((block_valid[:, None, :] > 0.5) | diagonal[None])
    scores = (
        jnp.einsum("ntz,nsz->nts", query_low, key_low, preferred_element_type=jnp.float32)
        * score_scale
    )
    masked = jnp.where(allowed, scores, very_low)
    row_top = jnp.max(masked, axis=-1, keepdims=True)
    log_total = row_top + jnp.log(jnp.sum(jnp.exp(masked - row_top), axis=-1, keepdims=True))
    probs_low = jnp.where(allowed, jnp.exp(masked - log_total), 0.0).astype(jnp.bfloat16)
    attended = jnp.einsum(
        "nts,nsv->ntv", probs_low, value_blocks, preferred_element_type=jnp.float32
    ).reshape(token_count, value_width)
    reset_act, reset_back = jax.vjp(jax.nn.silu, reset_pre)
    product_low = (attended * reset_act).astype(jnp.bfloat16)
    projected = plain_dot(product_low, output_weight)
    after_mix, merge_back = jax.vjp(merge_piece, candidate_pre, projected, update_pre, flat_in)
    ffn_normed, ffn_norm_back = jax.vjp(layer_norm, after_mix, ffn_gain.astype(jnp.float32))
    ffn_low = ffn_normed.astype(jnp.bfloat16)
    inner_pre = plain_dot(ffn_low, ffn_in)
    inner_act, act_back = jax.vjp(jax.nn.silu, inner_pre)
    act_low = inner_act.astype(jnp.bfloat16)
    ffn_res = plain_dot(act_low, ffn_out)
    block_out = (after_mix + ffn_res).astype(jnp.bfloat16).reshape(row_count, seq_len, model_width)
    grad_out = cotangent.astype(jnp.float32).reshape(token_count, model_width)
    grad_res_low = cotangent.reshape(token_count, model_width)
    grad_ffn_out = outer_dot(act_low, grad_res_low)
    grad_act = inner_dot(grad_res_low, ffn_out)
    grad_inner_low = act_back(grad_act)[0].astype(jnp.bfloat16)
    grad_ffn_in = outer_dot(ffn_low, grad_inner_low)
    grad_ffn_normed = inner_dot(grad_inner_low, ffn_in)
    grad_mix_add, grad_ffn_gain = ffn_norm_back(grad_ffn_normed)
    grad_after = grad_out + grad_mix_add
    grad_candidate, grad_projected, grad_update, grad_residual = merge_back(grad_after)
    grad_proj_low = grad_projected.astype(jnp.bfloat16)
    grad_output_weight = outer_dot(product_low, grad_proj_low)
    grad_product = inner_dot(grad_proj_low, output_weight)
    grad_attended = (
        (grad_product * reset_act).astype(jnp.bfloat16).reshape(block_count, GROUP, value_width)
    )
    grad_reset = reset_back(grad_product * attended)[0]
    again_scores = (
        jnp.einsum("ntz,nsz->nts", query_low, key_low, preferred_element_type=jnp.float32)
        * score_scale
    )
    soft_probs = jnp.where(
        allowed, jnp.exp(jnp.where(allowed, again_scores, very_low) - log_total), 0.0
    )
    soft_low = soft_probs.astype(jnp.bfloat16)
    grad_probs = jnp.einsum(
        "ntv,nsv->nts", grad_attended, value_blocks, preferred_element_type=jnp.float32
    )
    grad_value = jnp.einsum(
        "nts,ntv->nsv", soft_low, grad_attended, preferred_element_type=jnp.float32
    ).reshape(token_count, value_width)
    grad_scores = soft_probs * (
        grad_probs - jnp.sum(grad_probs * soft_probs, axis=-1, keepdims=True)
    )
    grad_raw_low = (grad_scores * score_scale).astype(jnp.bfloat16)
    grad_query = jnp.einsum(
        "nts,nsz->ntz", grad_raw_low, key_low, preferred_element_type=jnp.float32
    ).reshape(token_count, query_width)
    grad_key = jnp.einsum(
        "nts,ntz->nsz", grad_raw_low, query_low, preferred_element_type=jnp.float32
    ).reshape(token_count, query_width)
    grad_shared, grad_qk_gain, grad_qk_bias = query_back((grad_query, grad_key))
    grad_base_low = jnp.concatenate(
        [grad_shared, grad_reset, grad_update, grad_candidate], axis=1
    ).astype(jnp.bfloat16)
    grad_base_weight = outer_dot(mixed_low, grad_base_low)
    grad_mixed = inner_dot(grad_base_low, base_weight)
    grad_ema_flat, grad_normed_mix, grad_omega = mix_back(grad_mixed)
    grad_turned, device_start = return_call(
        grad_ema_flat.reshape(row_count, seq_len, model_width), retain
    )
    later = carried_in(device_start, span_decay, "seq", True)
    grad_ema_total, cross, border, lags = adjoint_call(
        grad_turned,
        turned,
        retain,
        1.0 / retain,
        power_of(retain, LAG),
        mix,
        later,
        state_end,
    )
    cross = jnp.sum(cross, axis=1)
    lags = jnp.sum(lags, axis=1)
    paired = retain * jnp.sum(border, axis=1)
    decay = jnp.ones_like(retain)
    for lag in range(LAG):
        paired = paired + decay * lags[lag]
        decay = decay * retain
    grad_ema_total = grad_ema_total * valid_mask[:, :, None]
    grad_vpre_low = value_back(grad_value)[0].astype(jnp.bfloat16)
    grad_value_weight = outer_dot(normed_low, grad_vpre_low)
    grad_normed = (
        grad_normed_mix
        + grad_ema_total.reshape(token_count, model_width)
        + inner_dot(grad_vpre_low, value_weight)
    )
    grad_flat, grad_norm_gain = norm_back(grad_normed)
    grad_tokens = (
        (grad_flat + grad_residual).astype(jnp.bfloat16).reshape(row_count, seq_len, model_width)
    )
    width = model_width
    small = jnp.concatenate(
        [
            paired,
            cross,
            grad_norm_gain[None],
            grad_omega[None],
            grad_ffn_gain[None],
            jnp.concatenate([grad_qk_gain, grad_qk_bias], axis=0).reshape(-1, width),
        ],
        axis=0,
    )
    states = retain.shape[0]
    padding = -small.shape[0] % 8
    small = small_sum(jnp.pad(small, ((0, padding), (0, 0))))
    paired, cross = small[:states], small[states : 2 * states]
    grad_norm_gain, grad_omega, grad_ffn_gain = (small[2 * states + at] for at in range(3))
    grad_query_key = small[2 * states + 3 : small.shape[0] - padding].reshape(4, query_width)
    grad_qk_gain, grad_qk_bias = grad_query_key[:2], grad_query_key[2:]
    grad_eta = (inflow * paired).T
    grad_beta = (eta * paired * gate).T
    grad_forget = (eta * paired * beta * (1.0 - forget) / gate - mix * cross).T
    middle = grad_base_weight.shape[0] // 2
    (
        grad_ffn_out,
        grad_ffn_in,
        grad_output_weight,
        base_top,
        base_bottom,
        grad_value_weight,
    ) = summed_everywhere(
        [
            grad_ffn_out,
            grad_ffn_in,
            grad_output_weight,
            grad_base_weight[:middle],
            grad_base_weight[middle:],
            grad_value_weight,
        ],
        (0, 1, 0, 0, 1, 2),
    )
    grad_base_weight = jnp.concatenate([base_top, base_bottom], axis=0)
    return (
        block_out,
        grad_tokens,
        grad_norm_gain,
        grad_value_weight,
        grad_forget,
        grad_beta,
        grad_eta,
        grad_omega,
        grad_base_weight,
        grad_qk_gain,
        grad_qk_bias,
        grad_output_weight,
        grad_ffn_gain,
        grad_ffn_in,
        grad_ffn_out,
    )


def solution(mesh):
    return jax.shard_map(
        per_device,
        mesh=mesh,
        in_specs=(
            P("row", "seq", None),
            P("row"),
            P(),
            P(),
            P(),
            P(),
            P(),
            P(),
            P(),
            P(),
            P(),
            P(),
            P(),
            P(),
            P(),
            P("row", "seq", None),
        ),
        out_specs=(
            P("row", "seq", None),
            P("row", "seq", None),
            P(),
            P(),
            P(),
            P(),
            P(),
            P(),
            P(),
            P(),
            P(),
            P(),
            P(),
            P(),
            P(),
        ),
        check_vma=False,
    )
```

```python
import functools

import jax
import jax.numpy as jnp
from jax import lax
from jax.experimental import pallas as pl
from jax.experimental.pallas import tpu as pltpu
from jax.sharding import PartitionSpec as P

GROUP = 128
STEPS = 32
LAG = 8
LANES = 128

epsilon = 1e-05
very_low = -1e30
scan_params = pltpu.CompilerParams(vmem_limit_bytes=48 * 2**20)
dense_params = pltpu.CompilerParams(vmem_limit_bytes=56 * 2**20)


def work_cost(flops, seconds):
    return pl.CostEstimate(flops=int(flops), bytes_accessed=int(seconds * 3.0e12), transcendentals=0)


def sigmoid(value):
    return 0.5 * jnp.tanh(0.5 * value) + 0.5


def unit_norm(values):
    centered = values - jnp.mean(values, axis=-1, keepdims=True)
    spread = jnp.mean(centered * centered, axis=-1, keepdims=True)
    scale = lax.rsqrt(spread + epsilon)
    return centered * scale, scale


def norm_backward(grad, unit_values, scale):
    along = jnp.mean(grad * unit_values, axis=-1, keepdims=True)
    return scale * (grad - jnp.mean(grad, axis=-1, keepdims=True) - unit_values * along)


def whole_spec(shape):
    return pl.BlockSpec(shape, lambda step: (0,) * len(shape))


def lane_slices(width):
    return [slice(low, low + LANES) for low in range(0, width, LANES)]


def spread_rows(ref, index, lanes, rows):
    return jnp.broadcast_to(ref[index : index + 1, lanes], (rows, LANES))


def add_all(parts):
    while len(parts) > 1:
        parts = [
            parts[at] + parts[at + 1] if at + 1 < len(parts) else parts[at]
            for at in range(0, len(parts), 2)
        ]
    return parts[0]


def enter_body(count_ref, tokens_ref, gain_ref, retain_ref, low_ref, turned_ref, end_ref, state):
    step = pl.program_id(0)
    rows, steps, width = tokens_ref.shape
    states = retain_ref.shape[0]

    @pl.when(step == 0)
    def _():
        state[...] = jnp.zeros_like(state)

    values = tokens_ref[...].astype(jnp.float32)
    centered = values - jnp.mean(values, axis=-1, keepdims=True)
    spread = jnp.mean(centered * centered, axis=-1, keepdims=True)
    normed = centered * lax.rsqrt(spread + epsilon) * gain_ref[...]
    low_ref[...] = normed.astype(jnp.bfloat16)
    places = step * steps + lax.broadcasted_iota(jnp.int32, (steps, 1), 0)
    kept = jnp.stack([jnp.where(places < count_ref[row], normed[row], 0.0) for row in range(rows)])
    for lanes in lane_slices(width):
        for unit in range(steps // LAG):
            part = slice(unit * LAG, (unit + 1) * LAG)
            turned_ref[part, :, lanes] = jnp.swapaxes(kept[:, part, lanes], 0, 1)
    for lanes in lane_slices(width):
        retain = [spread_rows(retain_ref, j, lanes, rows) for j in range(states)]

        def unit_step(unit, hidden):
            for within in range(LAG):
                entry = turned_ref[unit * LAG + within, :, lanes]
                hidden = [retain[j] * hidden[j] + entry for j in range(states)]
            return hidden

        hidden = lax.fori_loop(
            0, steps // LAG, unit_step, [state[j, :, lanes] for j in range(states)]
        )
        for j in range(states):
            state[j, :, lanes] = hidden[j]

    @pl.when(step == pl.num_programs(0) - 1)
    def _():
        end_ref[...] = state[...]


def enter_call(counts, tokens, gain, retain):
    rows, length, width = tokens.shape
    states = retain.shape[0]
    natural = pl.BlockSpec((rows, STEPS, width), lambda step: (0, step, 0))
    return pl.pallas_call(
        enter_body,
        grid=(length // STEPS,),
        in_specs=[
            pl.BlockSpec(memory_space=pltpu.SMEM),
            natural,
            whole_spec((1, width)),
            whole_spec((states, width)),
        ],
        out_specs=(
            natural,
            pl.BlockSpec((STEPS, rows, width), lambda step: (step, 0, 0)),
            whole_spec((states, rows, width)),
        ),
        out_shape=(
            jax.ShapeDtypeStruct(tokens.shape, jnp.bfloat16),
            jax.ShapeDtypeStruct((length, rows, width), jnp.float32),
            jax.ShapeDtypeStruct((states, rows, width), jnp.float32),
        ),
        scratch_shapes=[pltpu.VMEM((states, rows, width), jnp.float32)],
        compiler_params=scan_params,
        cost_estimate=work_cost(0.0, 9e-6),
        name="enter",
    )(counts, tokens, gain, retain)


def average_body(turned_ref, retain_ref, mix_ref, start_ref, out_ref, end_ref, state):
    step = pl.program_id(0)
    steps, rows, width = turned_ref.shape
    states = retain_ref.shape[0]

    @pl.when(step == 0)
    def _():
        state[...] = start_ref[...]

    for lanes in lane_slices(width):
        retain = [spread_rows(retain_ref, j, lanes, rows) for j in range(states)]
        mix = [spread_rows(mix_ref, j, lanes, rows) for j in range(states)]

        def unit_step(unit, hidden):
            sums = []
            for within in range(LAG):
                entry = turned_ref[unit * LAG + within, :, lanes]
                hidden = [retain[j] * hidden[j] + entry for j in range(states)]
                sums.append(add_all([mix[j] * hidden[j] for j in range(states)]))
            out_ref[:, pl.ds(unit * LAG, LAG), lanes] = jnp.swapaxes(jnp.stack(sums), 0, 1)
            return hidden

        hidden = lax.fori_loop(
            0, steps // LAG, unit_step, [state[j, :, lanes] for j in range(states)]
        )
        for j in range(states):
            state[j, :, lanes] = hidden[j]

    @pl.when(step == pl.num_programs(0) - 1)
    def _():
        end_ref[...] = state[...]


def average_call(turned, retain, mix, start):
    length, rows, width = turned.shape
    states = retain.shape[0]
    held = (states, rows, width)
    return pl.pallas_call(
        average_body,
        grid=(length // STEPS,),
        in_specs=[
            pl.BlockSpec((STEPS, rows, width), lambda step: (step, 0, 0)),
            whole_spec((states, width)),
            whole_spec((states, width)),
            whole_spec(held),
        ],
        out_specs=(
            pl.BlockSpec((rows, STEPS, width), lambda step: (0, step, 0)),
            whole_spec(held),
        ),
        out_shape=(
            jax.ShapeDtypeStruct((rows, length, width), jnp.float32),
            jax.ShapeDtypeStruct(held, jnp.float32),
        ),
        scratch_shapes=[pltpu.VMEM(held, jnp.float32)],
        compiler_params=scan_params,
        cost_estimate=work_cost(0.0, 12e-6),
        name="average",
    )(turned, retain, mix, start)


def return_body(grad_ref, retain_ref, turned_ref, end_ref, state):
    step = pl.program_id(0)
    rows, steps, width = grad_ref.shape
    states = retain_ref.shape[0]

    @pl.when(step == 0)
    def _():
        state[...] = jnp.zeros_like(state)

    for lanes in lane_slices(width):
        retain = [spread_rows(retain_ref, j, lanes, rows) for j in range(states)]

        def unit_step(unit, hidden):
            part = pl.ds((steps // LAG - 1 - unit) * LAG, LAG)
            turned = jnp.swapaxes(grad_ref[:, part, lanes], 0, 1)
            turned_ref[part, :, lanes] = turned
            for within in reversed(range(LAG)):
                hidden = [retain[j] * hidden[j] + turned[within] for j in range(states)]
            return hidden

        hidden = lax.fori_loop(
            0, steps // LAG, unit_step, [state[j, :, lanes] for j in range(states)]
        )
        for j in range(states):
            state[j, :, lanes] = hidden[j]

    @pl.when(step == pl.num_programs(0) - 1)
    def _():
        end_ref[...] = state[...]


def return_call(grad, retain):
    rows, length, width = grad.shape
    states = retain.shape[0]
    last = length // STEPS - 1
    return pl.pallas_call(
        return_body,
        grid=(length // STEPS,),
        in_specs=[
            pl.BlockSpec((rows, STEPS, width), lambda step: (0, last - step, 0)),
            whole_spec((states, width)),
        ],
        out_specs=(
            pl.BlockSpec((STEPS, rows, width), lambda step: (last - step, 0, 0)),
            whole_spec((states, rows, width)),
        ),
        out_shape=(
            jax.ShapeDtypeStruct((length, rows, width), jnp.float32),
            jax.ShapeDtypeStruct((states, rows, width), jnp.float32),
        ),
        scratch_shapes=[pltpu.VMEM((states, rows, width), jnp.float32)],
        compiler_params=scan_params,
        cost_estimate=work_cost(0.0, 8e-6),
        name="back_enter",
    )(grad, retain)


def sums_body(
    grad_ref,
    turned_ref,
    retain_ref,
    inverse_ref,
    unit_ref,
    held_ref,
    lag_in_ref,
    carry_ref,
    lag_ref,
):
    step = pl.program_id(0)
    steps, rows, width = grad_ref.shape
    states = retain_ref.shape[0]
    half = states // 2
    units = steps // LAG

    @pl.when(step == 0)
    def _():
        carry_ref[...] = held_ref[...]
        lag_ref[...] = lag_in_ref[...]

    for lanes in lane_slices(width):
        for first in range(0, states, half):
            chosen = range(first, first + half)
            retain = [spread_rows(retain_ref, j, lanes, rows) for j in chosen]
            inverse = [spread_rows(inverse_ref, j, lanes, rows) for j in chosen]

            def unit_step(unit, carried):
                after, hidden, cross = carried
                unit = units - 1 - unit
                later = after
                for within in reversed(range(LAG)):
                    place = unit * LAG + within
                    entry = turned_ref[place, :, lanes]
                    grad = grad_ref[place, :, lanes]
                    after = [retain[m] * after[m] + grad for m in range(half)]
                    hidden = [(hidden[m] - entry) * inverse[m] for m in range(half)]
                    cross = [cross[m] + after[m] * hidden[m] for m in range(half)]
                for m, j in enumerate(chosen):
                    unit_decay = spread_rows(unit_ref, j, lanes, rows)
                    carry_ref[3, j, :, lanes] += hidden[m] * (after[m] - unit_decay * later[m])
                return after, hidden, cross

            results = lax.fori_loop(
                0,
                units,
                unit_step,
                tuple([carry_ref[kind, j, :, lanes] for j in chosen] for kind in range(3)),
            )
            for kind in range(3):
                for m, j in enumerate(chosen):
                    carry_ref[kind, j, :, lanes] = results[kind][m]

        def lag_step(unit, lags):
            entries = [turned_ref[unit * LAG + at, :, lanes] for at in range(LAG)]
            grads = [grad_ref[unit * LAG + at, :, lanes] for at in range(LAG)]
            return [
                lags[lag] + add_all([grads[at] * entries[at - lag] for at in range(lag, LAG)])
                for lag in range(LAG)
            ]

        lags = lax.fori_loop(0, units, lag_step, [lag_ref[at, :, lanes] for at in range(LAG)])
        for at in range(LAG):
            lag_ref[at, :, lanes] = lags[at]


def sums_call(low_end, high_end, grad, turned, params, carried):
    rows, width = grad.shape[1:]
    states = params[0].shape[0]
    last = high_end // STEPS - 1
    turned_spec = pl.BlockSpec((STEPS, rows, width), lambda step: (last - step, 0, 0))
    carried_specs = [whole_spec(value.shape) for value in carried]
    return pl.pallas_call(
        sums_body,
        grid=((high_end - low_end) // STEPS,),
        in_specs=[turned_spec] * 2 + [whole_spec((states, width))] * 3 + carried_specs,
        out_specs=carried_specs,
        out_shape=[jax.ShapeDtypeStruct(value.shape, jnp.float32) for value in carried],
        compiler_params=scan_params,
        cost_estimate=work_cost(0.0, 8e-6),
        name="adjoint_sums",
    )(grad, turned, *params, *carried)


def leave_body(
    count_ref,
    tokens_ref,
    gain_ref,
    part_ref,
    residual_ref,
    grad_ref,
    retain_ref,
    mix_ref,
    held_ref,
    _,
    carry_ref,
    out_ref,
    path,
    *,
    places_before,
):
    step = pl.program_id(0)
    steps, rows, width = grad_ref.shape
    states = retain_ref.shape[0]
    units = steps // LAG

    @pl.when(step == 0)
    def _():
        carry_ref[...] = held_ref[...]

    for lanes in lane_slices(width):
        retain = [spread_rows(retain_ref, j, lanes, rows) for j in range(states)]
        mix = [spread_rows(mix_ref, j, lanes, rows) for j in range(states)]

        def unit_step(unit, after):
            unit = units - 1 - unit
            sums = []
            for within in reversed(range(LAG)):
                grad = grad_ref[unit * LAG + within, :, lanes]
                after = [retain[j] * after[j] + grad for j in range(states)]
                sums.append(add_all([mix[j] * after[j] for j in range(states)]))
            path[:, pl.ds(unit * LAG, LAG), lanes] = jnp.swapaxes(jnp.stack(sums[::-1]), 0, 1)
            return after

        after = lax.fori_loop(
            0, units, unit_step, [carry_ref[j, :, lanes] for j in range(states)]
        )
        for j in range(states):
            carry_ref[j, :, lanes] = after[j]

    first_place = places_before + (pl.num_programs(0) - 1 - step) * steps
    places = first_place + lax.broadcasted_iota(jnp.int32, (steps, 1), 0)
    gain = gain_ref[...]
    for row in range(rows):
        unit_values, scale = unit_norm(tokens_ref[row].astype(jnp.float32))
        grad = part_ref[row].astype(jnp.float32)
        grad = grad + jnp.where(places < count_ref[row], path[row], 0.0)
        out = norm_backward(grad * gain, unit_values, scale)
        out_ref[row] = (out + residual_ref[row].astype(jnp.float32)).astype(jnp.bfloat16)


def leave_call(
    low_end, high_end, counts, tokens, gain, part, grad, retain, mix, carried
):
    rows, length, width = tokens.shape
    held = carried[0].shape
    last = high_end // STEPS - 1
    natural = pl.BlockSpec((rows, STEPS, width), lambda step: (0, last - step, 0))
    return pl.pallas_call(
        functools.partial(leave_body, places_before=low_end),
        grid=((high_end - low_end) // STEPS,),
        in_specs=[
            pl.BlockSpec(memory_space=pltpu.SMEM),
            natural,
            whole_spec((1, width)),
            natural,
            natural,
            pl.BlockSpec((STEPS, rows, width), lambda step: (last - step, 0, 0)),
            whole_spec(retain.shape),
            whole_spec(mix.shape),
            whole_spec(held),
            pl.BlockSpec(memory_space=pl.ANY),
        ],
        out_specs=[whole_spec(held), natural],
        out_shape=[
            jax.ShapeDtypeStruct(held, jnp.float32),
            jax.ShapeDtypeStruct((rows, length, width), jnp.bfloat16),
        ],
        input_output_aliases={9: 1},
        scratch_shapes=[pltpu.VMEM((rows, STEPS, width), jnp.float32)],
        compiler_params=scan_params,
        cost_estimate=work_cost(0.0, 8e-6),
        name="leave",
    )(counts, tokens, gain, part, carried[1], grad, retain, mix, *carried)


class Exchange:
    def __init__(self, local, decay, axis, backward):
        self.axis, self.backward = axis, backward
        self.count = lax.axis_size(axis)
        place = lax.axis_index(axis)
        self.place = self.count - 1 - place if backward else place
        self.low = self.place % 2
        self.half = local.shape[-1] // 2
        self.local = local
        self.decay = self.part(decay, self.low)

    def part(self, value, which):
        return lax.dynamic_slice_in_dim(value, which * self.half, self.half, value.ndim - 1)

    def moved(self, value, pairs):
        last = self.count - 1
        if self.backward:
            pairs = [(last - source, last - target) for source, target in pairs]
        return lax.ppermute(value, self.axis, pairs)

    def swapped(self, value):
        return self.moved(value, [(at, at ^ 1) for at in range(self.count)])

    def later(self, value, hop):
        return self.moved(value, [(at, at + 2 * hop) for at in range(self.count - 2 * hop)])

    def share(self):
        own = self.part(self.local, self.low)
        other = self.swapped(self.part(self.local, 1 - self.low))
        self.first = jnp.where(self.low == 0, own, other)
        self.pair = self.decay * self.first + jnp.where(self.low == 0, other, own)

    def cross(self):
        pairs = self.count // 2
        decay = self.decay * self.decay
        if pairs <= 4:
            arrived = [self.later(self.pair, hop) for hop in range(1, pairs)]
            total = arrived[-1]
            for value in arrived[-2::-1]:
                total = decay * total + value
        else:
            total, hop = self.later(self.pair, 1), 1
            while hop < pairs - 1:
                total = total + decay * self.later(total, hop)
                decay = decay * decay
                hop *= 2
        self.start = total

    def give(self):
        second = self.decay * self.start + self.first
        kept = jnp.where(self.low == 0, self.start, second)
        got = self.swapped(jnp.where(self.low == 0, second, self.start))
        return jnp.concatenate(
            [jnp.where(self.low == 0, kept, got), jnp.where(self.low == 0, got, kept)], axis=-1
        )


mesh_axes = ("seq", "row")


def device_total():
    return lax.axis_size("seq") * lax.axis_size("row")


def device_place():
    return lax.axis_index("seq") * lax.axis_size("row") + lax.axis_index("row")


def swapped(value, bit):
    return lax.ppermute(value, mesh_axes, [(at, at ^ bit) for at in range(device_total())])


def half_summed(value, bit):
    half = value.shape[0] // 2
    mine = (device_place() // bit) % 2
    sent = lax.dynamic_slice_in_dim(value, (1 - mine) * half, half, 0)
    kept = lax.dynamic_slice_in_dim(value, mine * half, half, 0)
    return kept + swapped(sent, bit)


def both_halves(value, bit):
    mine = (device_place() // bit) % 2 == 1
    other = swapped(value, bit)
    return jnp.concatenate([jnp.where(mine, other, value), jnp.where(mine, value, other)], axis=0)


def link_orders():
    total = device_total()
    bits = [1 << at for at in range(total.bit_length() - 1)]
    if (lax.axis_size("seq"), lax.axis_size("row")) == (8, 4):
        core, x, y, z_low, z_high = bits
        return (
            (core, x, y, z_low, z_high),
            (core, y, z_low, z_high, x),
            (core, z_low, z_high, x, y),
        )
    third = len(bits) // 3
    return tuple(bits[turn * third :] + bits[: turn * third] for turn in range(3))


def summed_everywhere(values):
    orders = link_orders()
    for at in range(len(orders[0])):
        values = [half_summed(v, orders[n % 3][at]) for n, v in enumerate(values)]
    for at in reversed(range(len(orders[0]))):
        values = [both_halves(v, orders[n % 3][at]) for n, v in enumerate(values)]
    return values


def paired_sum(value, group):
    partners = [group[0]] if len(group) == 1 else [group[0], group[1], group[0] + group[1]]
    arrived = [swapped(value, partner) for partner in partners]
    if len(arrived) == 1:
        return value + arrived[0]
    return (value + arrived[0]) + (arrived[1] + arrived[2])


def small_sum(value):
    bits = [1 << at for at in range(device_total().bit_length() - 1)]
    for at in range(0, len(bits), 2):
        value = paired_sum(value, bits[at : at + 2])
    return value


def power_of(value, exponent):
    result = None
    while exponent:
        if exponent & 1:
            result = value if result is None else result * value
        value = value * value
        exponent >>= 1
    return result


def dot(first_op, second_op):
    return jnp.dot(first_op, second_op, preferred_element_type=jnp.float32)


def dot_back(first_op, second_op):
    return lax.dot_general(
        first_op, second_op, (((1,), (1,)), ((), ())), preferred_element_type=jnp.float32
    )


def dot_outer(first_op, second_op):
    return lax.dot_general(
        first_op, second_op, (((0,), (0,)), ((), ())), preferred_element_type=jnp.float32
    )


def low(value):
    return value.astype(jnp.bfloat16)


def chunks(low_end, high_end, size):
    return [slice(at, min(at + size, high_end)) for at in range(low_end, high_end, size)]


def forward_body(
    count_ref,
    tokens_ref,
    cotangent_ref,
    average_ref,
    normed_ref,
    omega_ref,
    value_weight_ref,
    base_weight_ref,
    gains_ref,
    biases_ref,
    output_weight_ref,
    ffn_gain_ref,
    ffn_in_ref,
    ffn_out_ref,
    out_ref,
    mixed_ref,
    mixed_slope_ref,
    value_ref,
    value_slope_ref,
    probs_ref,
    query_ref,
    key_ref,
    shared_ref,
    shared_slope_ref,
    product_ref,
    ffn_low_ref,
    act_ref,
    grad_inner_ref,
    grad_proj_ref,
    grad_attended_ref,
    grad_main_ref,
    residual_ref,
    ffn_gain_grad_ref,
    reset_ref,
    reset_slope_ref,
):
    row = pl.program_id(0)
    length, width = tokens_ref.shape
    zdim = query_ref.shape[1]
    vdim = value_ref.shape[1]
    inner = act_ref.shape[1]

    @pl.when(row == 0)
    def _():
        ffn_gain_grad_ref[...] = jnp.zeros_like(ffn_gain_grad_ref)

    normed = normed_ref[...]
    sums = average_ref[...] + omega_ref[...] * normed.astype(jnp.float32)
    gate = sigmoid(sums)
    mixed = sums * gate
    mixed_ref[...] = low(mixed)
    mixed_slope_ref[...] = low(gate + mixed * (1.0 - gate))
    mixed_low = mixed_ref[...]

    shared = dot(mixed_low, base_weight_ref[:, :zdim])
    gate = sigmoid(shared)
    shared_act = shared * gate
    shared_ref[...] = shared_act
    shared_slope_ref[...] = gate + shared_act * (1.0 - gate)
    query_ref[...] = low(shared_act * gains_ref[0:1] + biases_ref[0:1])
    key_ref[...] = low(shared_act * gains_ref[1:2] + biases_ref[1:2])

    for part in chunks(0, vdim, 256):
        value_pre = dot(normed, value_weight_ref[:, part])
        gate = sigmoid(value_pre)
        value = value_pre * gate
        value_ref[:, part] = low(value)
        value_slope_ref[:, part] = low(gate + value * (1.0 - gate))

    to_place = lax.broadcasted_iota(jnp.int32, (GROUP, GROUP), 0)
    from_place = lax.broadcasted_iota(jnp.int32, (GROUP, GROUP), 1)
    for block in chunks(0, length, GROUP):
        allowed = (from_place <= to_place) & (
            (from_place < count_ref[row] - block.start) | (from_place == to_place)
        )
        scores = dot_back(query_ref[block], key_ref[block]) * zdim**-0.5
        scores = jnp.where(allowed, scores, very_low)
        weights = jnp.exp(scores - jnp.max(scores, axis=-1, keepdims=True))
        weights = jnp.where(allowed, weights, 0.0)
        probs_ref[block] = weights / jnp.sum(weights, axis=-1, keepdims=True)

    for part in chunks(0, vdim, 256):
        base_part = slice(zdim + part.start, zdim + part.stop)
        reset = dot(mixed_low, base_weight_ref[:, base_part])
        gate = sigmoid(reset)
        reset_act = reset * gate
        reset_slope = gate + reset_act * (1.0 - gate)
        reset_ref[:, part] = low(reset_act)
        for block in chunks(0, length, GROUP):
            attended = dot(low(probs_ref[block]), value_ref[block, part])
            product_ref[block, part] = low(attended * reset_act[block])
            reset_slope_ref[block, part] = low(attended * reset_slope[block])

    update_gate = sigmoid(dot(mixed_low, base_weight_ref[:, zdim + vdim : zdim + vdim + width]))
    candidate = dot(mixed_low, base_weight_ref[:, zdim + vdim + width :])
    candidate = candidate + dot(product_ref[...], output_weight_ref[...])
    candidate_gate = sigmoid(candidate)
    candidate_act = candidate * candidate_gate
    candidate_slope = candidate_gate + candidate_act * (1.0 - candidate_gate)
    tokens = tokens_ref[...].astype(jnp.float32)
    change = candidate_act - tokens
    after = tokens + update_gate * change
    unit_values, scale = unit_norm(after)
    ffn_low_ref[...] = low(unit_values * ffn_gain_ref[...])
    ffn_low = ffn_low_ref[...]
    cotangent = cotangent_ref[...]

    out = after
    grad_normed = jnp.zeros_like(after)
    for part in chunks(0, inner, 256):
        inner_pre = dot(ffn_low, ffn_in_ref[:, part])
        gate = sigmoid(inner_pre)
        act = inner_pre * gate
        slope = gate + act * (1.0 - gate)
        act_ref[:, part] = low(act)
        grad_act = dot_back(cotangent, ffn_out_ref[part])
        grad_inner_ref[:, part] = low(grad_act * slope)
    out = after + dot(act_ref[...], ffn_out_ref[...])
    out_ref[...] = low(out)
    grad_normed = dot_back(grad_inner_ref[...], ffn_in_ref[...])
    ffn_gain_grad_ref[...] += jnp.sum(grad_normed * unit_values, axis=0, keepdims=True)
    grad_after = cotangent.astype(jnp.float32) + norm_backward(
        grad_normed * ffn_gain_ref[...], unit_values, scale
    )
    grad_change = grad_after * update_gate
    grad_proj = low(grad_change * candidate_slope)
    grad_proj_ref[...] = grad_proj
    grad_main_ref[:, vdim : vdim + width] = low(grad_change * change * (1.0 - update_gate))
    grad_main_ref[:, vdim + width :] = grad_proj
    for part in chunks(0, vdim, 256):
        grad_product = dot_back(grad_proj, output_weight_ref[part])
        grad_attended_ref[:, part] = low(grad_product * reset_ref[:, part].astype(jnp.float32))
        grad_main_ref[:, part] = low(grad_product * reset_slope_ref[:, part].astype(jnp.float32))
    residual_ref[...] = low(grad_after - grad_change)


def row_spec(length, width):
    return pl.BlockSpec((None, length, width), lambda row: (row, 0, 0))


def once_spec(shape):
    return pl.BlockSpec(shape, lambda row: (0,) * len(shape), pipeline_mode=pl.Buffered(1))


def forward_call(
    counts,
    tokens,
    cotangent,
    average,
    normed,
    omega,
    value_weight,
    base_weight,
    gains,
    biases,
    output_weight,
    ffn_gain,
    ffn_in,
    ffn_out,
):
    rows, length, width = tokens.shape
    zdim, vdim, inner = gains.shape[1], value_weight.shape[1], ffn_in.shape[1]
    half, full = jnp.bfloat16, jnp.float32
    outs = [
        (width, half),
        (width, half),
        (width, half),
        (vdim, half),
        (vdim, half),
        (GROUP, full),
        (zdim, half),
        (zdim, half),
        (zdim, full),
        (zdim, full),
        (vdim, half),
        (width, half),
        (inner, half),
        (inner, half),
        (width, half),
        (vdim, half),
        (vdim + 2 * width, half),
        (width, half),
    ]
    tied = [
        omega,
        value_weight,
        base_weight,
        gains,
        biases,
        output_weight,
        ffn_gain,
        ffn_in,
        ffn_out,
    ]
    return pl.pallas_call(
        forward_body,
        grid=(rows,),
        in_specs=[pl.BlockSpec(memory_space=pltpu.SMEM)]
        + [row_spec(length, width)] * 4
        + [once_spec(value.shape) for value in tied],
        out_specs=[row_spec(length, size) for size, _ in outs] + [whole_spec((1, width))],
        out_shape=[jax.ShapeDtypeStruct((rows, length, size), kind) for size, kind in outs]
        + [jax.ShapeDtypeStruct((1, width), full)],
        scratch_shapes=[pltpu.VMEM((length, vdim), half)] * 2,
        compiler_params=dense_params,
        cost_estimate=work_cost(18e9, 40e-6),
        name="dense_forward",
    )(counts, tokens, cotangent, average, normed, *tied)


def backward_body(
    grad_attended_ref,
    grad_main_ref,
    normed_ref,
    mixed_slope_ref,
    value_ref,
    value_slope_ref,
    probs_ref,
    query_ref,
    key_ref,
    shared_ref,
    shared_slope_ref,
    omega_ref,
    gains_ref,
    value_weight_ref,
    base_weight_ref,
    grad_shared_ref,
    grad_vpre_ref,
    grad_average_ref,
    part_ref,
    grad_gains_ref,
    grad_omega_ref,
    grad_gain_ref,
):
    row = pl.program_id(0)
    length = grad_attended_ref.shape[0]
    zdim = query_ref.shape[1]
    vdim = value_ref.shape[1]

    @pl.when(row == 0)
    def _():
        grad_gains_ref[...] = jnp.zeros_like(grad_gains_ref)
        grad_omega_ref[...] = jnp.zeros_like(grad_omega_ref)
        grad_gain_ref[...] = jnp.zeros_like(grad_gain_ref)

    grad_gains = jnp.zeros(grad_gains_ref.shape, jnp.float32)
    for block in chunks(0, length, GROUP):
        probs = probs_ref[block]
        probs_low = low(probs)
        grad_probs = dot_back(grad_attended_ref[block], value_ref[block])
        for part in chunks(0, vdim, 512):
            grad_value = dot_outer(probs_low, grad_attended_ref[block, part])
            grad_vpre_ref[block, part] = low(
                grad_value * value_slope_ref[block, part].astype(jnp.float32)
            )
        total = jnp.sum(grad_probs * probs, axis=-1, keepdims=True)
        grad_raw = low(probs * (grad_probs - total) * zdim**-0.5)
        grad_query = dot(grad_raw, key_ref[block])
        grad_key = dot_outer(grad_raw, query_ref[block])
        shared = shared_ref[block]
        grad_gains = grad_gains + jnp.concatenate(
            [
                jnp.sum(value, axis=0, keepdims=True)
                for value in (grad_query * shared, grad_key * shared, grad_query, grad_key)
            ],
            axis=0,
        )
        grad_shared = grad_query * gains_ref[0:1] + grad_key * gains_ref[1:2]
        grad_shared_ref[block] = low(grad_shared * shared_slope_ref[block])
    grad_gains_ref[...] += grad_gains
    grad_average = dot_back(grad_main_ref[...], base_weight_ref[:, zdim:])
    grad_average = grad_average + dot_back(grad_shared_ref[...], base_weight_ref[:, :zdim])
    grad_average = grad_average * mixed_slope_ref[...].astype(jnp.float32)
    grad_average_ref[...] = grad_average
    part = dot_back(grad_vpre_ref[...], value_weight_ref[...]) + grad_average * omega_ref[...]
    part_ref[...] = part
    normed = normed_ref[...].astype(jnp.float32)
    grad_omega_ref[...] += jnp.sum(grad_average * normed, axis=0, keepdims=True)
    grad_gain_ref[...] += jnp.sum(part * normed, axis=0, keepdims=True)


def backward_call(inputs, tied_inputs):
    rows, length, vdim = inputs[0].shape
    omega, gains, _, _ = tied_inputs
    width, zdim = omega.shape[1], gains.shape[1]
    outs = [
        (zdim, jnp.bfloat16),
        (vdim, jnp.bfloat16),
        (width, jnp.float32),
        (width, jnp.float32),
    ]
    return pl.pallas_call(
        backward_body,
        grid=(rows,),
        in_specs=[row_spec(length, value.shape[2]) for value in inputs]
        + [once_spec(value.shape) for value in tied_inputs],
        out_specs=[row_spec(length, size) for size, _ in outs]
        + [whole_spec((4, zdim))]
        + [whole_spec((1, width))] * 2,
        out_shape=[jax.ShapeDtypeStruct((rows, length, size), kind) for size, kind in outs]
        + [
            jax.ShapeDtypeStruct((4, zdim), jnp.float32),
            jax.ShapeDtypeStruct((1, width), jnp.float32),
            jax.ShapeDtypeStruct((1, width), jnp.float32),
        ],
        compiler_params=dense_params,
        cost_estimate=work_cost(10e9, 25e-6),
        name="dense_backward",
    )(*inputs, *tied_inputs)


def joined_body(*refs, widths, split):
    refs = refs[1:] if split else refs
    outs_per_chain = 2 if split else 1
    outs = refs[len(refs) - outs_per_chain * len(widths) :]
    at = 0
    for chain, parts in enumerate(widths):
        for side in range(outs_per_chain):
            column = 0
            for width in parts:
                total = refs[at][...] + refs[at + 1][...]
                outs[chain * outs_per_chain + side][:, column : column + width] = total
                column += width
                at += 2


def joined(chains):
    split = chains[0][2] is not None
    sides = 2 if split else 1
    widths = [[value.shape[1] for value in kept] for kept, _, _ in chains]
    sizes = [kept[0].shape[0] // sides for kept, _, _ in chains]
    steps = 4
    while any(size % (8 * steps) for size in sizes):
        steps //= 2
    operands, in_specs, out_specs, out_shape = [], [], [], []
    for chain, (kept, arrived, _) in enumerate(chains):
        block = sizes[chain] // steps
        for side in range(sides):

            def place(step, *held, chain=chain, side=side):
                if not held:
                    return step, 0
                mine = held[0][chain]
                return (1 - mine if side else mine) * steps + step, 0

            for pair in zip(kept, arrived):
                for value in pair:
                    operands.append(value)
                    in_specs.append(pl.BlockSpec((block, value.shape[1]), place))
            total = sum(widths[chain])
            out_specs.append(pl.BlockSpec((block, total), lambda step, *held: (step, 0)))
            out_shape.append(jax.ShapeDtypeStruct((sizes[chain], total), jnp.float32))
    if split:
        mine = [(device_place() // bit) % 2 for _, _, bit in chains]
        operands.insert(0, jnp.stack(mine).astype(jnp.int32))
    outs = pl.pallas_call(
        functools.partial(joined_body, widths=widths, split=split),
        grid_spec=pltpu.PrefetchScalarGridSpec(
            num_scalar_prefetch=1 if split else 0,
            grid=(steps,),
            in_specs=in_specs,
            out_specs=out_specs,
        ),
        out_shape=out_shape,
        compiler_params=scan_params,
        cost_estimate=work_cost(0.0, 2e-6),
        name="joined",
    )(*operands)
    return [tuple(outs[at : at + sides]) for at in range(0, len(outs), sides)]


def placed_body(*refs, copies, sources):
    mine, refs = refs[0], refs[1:]
    half = pl.program_id(0)
    for own, arrived, which, taken, result, column in copies:
        there = slice(column, column + taken.stop - taken.start)

        @pl.when(half == mine[which])
        def _(own=own, taken=taken, result=result, there=there):
            refs[sources + result][:, there] = refs[own][:, taken]

        @pl.when(half != mine[which])
        def _(arrived=arrived, taken=taken, result=result, there=there):
            refs[sources + result][:, there] = refs[arrived][:, taken]


def placed(values, bits, copies, shapes):
    steps = 4
    while any(value.shape[0] % (8 * steps) for value in values):
        steps //= 2
    in_specs = []
    for at, value in enumerate(values):

        def place(half, step, mine, which=at // 2, other=at % 2):
            wanted = (half == mine[which]) != bool(other)
            return jnp.where(wanted, step, jnp.where(half == 0, 0, steps - 1)), 0

        in_specs.append(pl.BlockSpec((value.shape[0] // steps, value.shape[1]), place))
    mine = jnp.stack([(device_place() // bit) % 2 for bit in bits]).astype(jnp.int32)
    return pl.pallas_call(
        functools.partial(placed_body, copies=copies, sources=len(values)),
        grid_spec=pltpu.PrefetchScalarGridSpec(
            num_scalar_prefetch=1,
            grid=(2, steps),
            in_specs=in_specs,
            out_specs=[
                pl.BlockSpec(
                    (shape[0] // (2 * steps), shape[1]),
                    lambda half, step, mine: (half * steps + step, 0),
                )
                for shape in shapes
            ],
        ),
        out_shape=[jax.ShapeDtypeStruct(shape, jnp.float32) for shape in shapes],
        compiler_params=scan_params,
        cost_estimate=work_cost(0.0, 2e-6),
        name="placed",
    )(mine, *values)


def gathered_body(*refs, copies):
    where, refs = refs[0], refs[1:]
    results = refs[len(refs) - 1 - max(result for _, _, result, _ in copies) :]
    turn = pl.program_id(0)
    for chain, taken, result, column in copies:
        there = slice(column, column + taken.stop - taken.start)
        for piece in range(2):

            @pl.when(turn == where[2 * chain + piece])
            def _(source=2 * chain + piece, taken=taken, result=result, there=there):
                results[result][:, there] = refs[source][:, taken]


def gathered(chains, copies, shapes, before=None):
    values, where = [], []
    for one in chains:
        low = (device_place() // one.order[1]) % 2
        values += one.held if before is None else one.arrived
        where += [low, 1 - low]
    core = (device_place() // chains[0].order[0]) % 2
    where.append(core if before is None else 1 - core)
    steps = 2
    in_specs = []
    for at, value in enumerate(values):

        def place(turn, step, where, at=at):
            early = jnp.where(turn < where[at], 0, steps - 1)
            return jnp.where(turn == where[at], step, early), 0

        in_specs.append(pl.BlockSpec((value.shape[0] // steps, value.shape[1]), place))
    aliases = {}
    if before is not None:
        aliases = {1 + len(values) + at: at for at in range(len(shapes))}
        in_specs += [pl.BlockSpec(memory_space=pl.ANY)] * len(shapes)
    side = len(where) - 1
    return pl.pallas_call(
        functools.partial(gathered_body, copies=copies),
        grid_spec=pltpu.PrefetchScalarGridSpec(
            num_scalar_prefetch=1,
            grid=(2, steps),
            in_specs=in_specs,
            out_specs=[
                pl.BlockSpec(
                    (shape[0] // (4 * steps), shape[1]),
                    lambda turn, step, where: ((2 * where[side] + turn) * steps + step, 0),
                )
                for shape in shapes
            ],
        ),
        out_shape=[jax.ShapeDtypeStruct(shape, jnp.float32) for shape in shapes],
        input_output_aliases=aliases,
        compiler_params=scan_params,
        cost_estimate=work_cost(0.0, 4e-6),
        name="gathered",
    )(jnp.stack(where).astype(jnp.int32), *values, *(before or ()))


class Chain:
    def __init__(self, order, sent, kept):
        self.order, self.at = order, 0
        self.sent, self.kept, self.arrived = list(sent), list(kept), []

    def state(self):
        return self.sent, self.kept, self.arrived

    def set_state(self, state):
        self.sent, self.kept, self.arrived = state

    def send(self):
        total = len(self.order)
        bit = self.order[self.at if self.at < total else 2 * total - 1 - self.at]
        self.arrived = [swapped(value, bit) for value in self.sent]

    def give(self):
        self.held = self.sent + self.arrived
        self.arrived = [swapped(value, self.order[0]) for value in self.held]

    def pieces(self):
        return self.held + self.arrived


def join(*chains):
    total = len(chains[0].order)
    if chains[0].at < total:
        last = chains[0].at == total - 1
        results = joined(
            [
                (one.kept, one.arrived, None if last else one.order[one.at + 1])
                for one in chains
            ]
        )
        for one, result in zip(chains, results):
            if last:
                one.sent, one.kept = [result[0]], []
            else:
                one.sent, one.kept = [result[1]], [result[0]]
    else:
        values, copies, shapes = [], [], []
        for at, one in enumerate(chains):
            rows, columns = one.sent[0].shape
            values += [one.sent[0], one.arrived[0]]
            copies.append((2 * at, 2 * at + 1, at, slice(0, columns), at, 0))
            shapes.append((2 * rows, columns))
        bits = [one.order[2 * total - 1 - one.at] for one in chains]
        for one, result in zip(chains, placed(values, bits, copies, shapes)):
            one.sent = [result]
    for one in chains:
        one.arrived = []
        one.at += 1


def tied(value, *chains):
    value, states = lax.optimization_barrier((value, [one.state() for one in chains]))
    for one, state in zip(chains, states):
        one.set_state(state)
    return value


def weight_halves(first_op, second_op, bit):
    first_op = first_op.reshape(-1, first_op.shape[-1])
    second_op = second_op.reshape(-1, second_op.shape[-1])
    half = first_op.shape[1] // 2
    mine = (device_place() // bit) % 2
    return [
        dot_outer(lax.dynamic_slice_in_dim(first_op, which * half, half, 1), second_op)
        for which in (1 - mine, mine)
    ]


def weight_grad(first_op, second_op):
    return dot_outer(
        first_op.reshape(-1, first_op.shape[-1]), second_op.reshape(-1, second_op.shape[-1])
    )


def per_device(
    tokens,
    valid_count,
    norm_gain,
    value_weight,
    ema_forget,
    ema_beta,
    ema_eta,
    ema_omega,
    base_weight,
    qk_gain,
    qk_bias,
    output_weight,
    ffn_gain,
    ffn_in,
    ffn_out,
    cotangent,
):
    length, width = tokens.shape[1:]
    counts = valid_count - lax.axis_index("seq") * length
    norm_gain = norm_gain.astype(jnp.float32)[None]
    ffn_gain = ffn_gain.astype(jnp.float32)[None]
    omega = ema_omega[None]
    gains, biases = qk_gain.astype(jnp.float32), qk_bias.astype(jnp.float32)
    forget, beta, eta = ema_forget.T, ema_beta.T, ema_eta.T
    retain = 1.0 - forget
    gate = jnp.sqrt(forget * (2.0 - forget))
    inflow = beta * gate
    mix = eta * inflow
    span_decay = power_of(retain, length)[:, None, :]

    normed, turned, device_end = enter_call(counts, tokens, norm_gain, retain)
    ahead = Exchange(device_end, span_decay, "seq", False)
    ahead.share()
    ahead.cross()
    incoming = ahead.give()
    average, state_end = average_call(turned, retain, mix, incoming)
    (
        block_out,
        mixed,
        mixed_slope,
        value,
        value_slope,
        probs,
        query,
        key,
        shared,
        shared_slope,
        product,
        ffn_low,
        act,
        grad_inner,
        grad_proj,
        grad_attended,
        grad_main,
        residual,
        grad_ffn_gain,
    ) = forward_call(
        counts,
        tokens,
        cotangent,
        average,
        normed,
        omega,
        value_weight,
        base_weight,
        gains,
        biases,
        output_weight,
        ffn_gain,
        ffn_in,
        ffn_out,
    )
    back_inputs = [
        grad_attended,
        grad_main,
        normed,
        mixed_slope,
        value,
        value_slope,
        probs,
        query,
        key,
        shared,
        shared_slope,
    ]
    orders = link_orders()
    chained = device_total() == 32
    early, late, chains = [], None, []
    if chained:
        core = orders[0][0]
        sums = [
            weight_halves(act, cotangent, core),
            weight_halves(product, grad_proj, core),
            weight_halves(mixed, grad_main, core),
            weight_halves(ffn_low, grad_inner, core),
        ]
        outs = Chain(orders[0], [sums[0][0], sums[1][0]], [sums[0][1], sums[1][1]])
        main = Chain(orders[1], [sums[2][0]], [sums[2][1]])
        inner = Chain(orders[2], [sums[3][0]], [sums[3][1]])
        early = [outs, main, inner]
        for one in early:
            one.send()
        join(*early)
        back_inputs = tied(back_inputs, *early)
        for one in early:
            one.send()
    back_outputs = backward_call(back_inputs, [omega, gains, value_weight, base_weight])
    if chained:
        back_outputs = tied(back_outputs, *early)
        join(*early)
        back_outputs = tied(back_outputs, *early)
        for one in early:
            one.send()
    grad_shared, grad_vpre, grad_average, part, grad_query_key, grad_omega, grad_gain = (
        back_outputs
    )
    if chained:
        sums = [weight_halves(normed, grad_vpre, core), weight_halves(mixed, grad_shared, core)]
        late = Chain(orders[0], [sums[0][0], sums[1][0]], [sums[0][1], sums[1][1]])
        chains = [late, *early]
        grad_average = tied(grad_average, late)
        late.send()

    def halve(value, *moving):
        if chained:
            value = tied(value, *chains)
            if early[0] in moving:
                join(*early)
            join(late)
            value = tied(value, *chains)
            for one in moving:
                one.send()
        return value

    grad_turned, device_start = return_call(grad_average, retain)
    behind = Exchange(device_start, span_decay, "seq", True)
    behind.local = halve(behind.local, late, *early)
    behind.share()
    behind.pair = halve(behind.pair, late)
    behind.cross()
    behind.start = halve(behind.start, late, *early)
    later = behind.give()
    states = retain.shape[0]
    carried = [
        jnp.stack([later, state_end, jnp.zeros_like(later), jnp.zeros_like(later)]),
        jnp.zeros((LAG,) + later.shape[1:], jnp.float32),
    ]
    parts = length // STEPS
    inverse, unit_decay = 1.0 / retain, power_of(retain, LAG)
    ends = [at * STEPS for at in (parts, 5 * parts // 8, 2 * parts // 8, 0)]
    for high_end, low_end in zip(ends, ends[1:]):
        carried = halve(carried, late, *early)
        carried = sums_call(
            low_end, high_end, grad_turned, turned, [retain, inverse, unit_decay], carried
        )
    (_, _, cross, border), lags = carried
    left = [later, residual]
    if chained:
        left = halve([left, cross], late, *early)
        left, cross = left
    cross = jnp.sum(cross, axis=1)
    lags = jnp.sum(lags, axis=1)
    paired = retain * jnp.sum(border, axis=1)
    decay = jnp.ones_like(retain)
    for lag in range(LAG):
        paired = paired + decay * lags[lag]
        decay = decay * retain
    small = jnp.concatenate(
        [
            paired,
            cross,
            grad_gain,
            grad_omega,
            grad_ffn_gain,
            grad_query_key.reshape(-1, width),
        ],
        axis=0,
    )
    used = small.shape[0]
    small = jnp.pad(small, ((0, -used % 8), (0, 0)))
    ends = [at * STEPS for at in (parts, 5 * parts // 8, 3 * parts // 8, 0)]
    if chained:
        core, _, _, z_low, z_high = orders[0]
        first_bits = [core, z_high, z_low]
    for turn, (high_end, low_end) in enumerate(zip(ends, ends[1:])):
        if chained:
            left, small = lax.optimization_barrier((left, small))
            small = small + swapped(small, first_bits[turn])
        left = leave_call(
            low_end, high_end, counts, tokens, norm_gain, part, grad_turned, retain, mix, left
        )
    if chained:
        left, small = tied((left, small), *chains)
        for one in early:
            one.give()
        join(late)
        late.send()
        small = paired_sum(small, orders[0][1:3])
    else:
        small = small_sum(small)
    grad_tokens = left[1]
    paired, cross = small[:states], small[states : 2 * states]
    grad_gain, grad_omega, grad_ffn_gain = (small[2 * states + at] for at in range(3))
    grad_norm_gain = (grad_gain + jnp.sum(mix * paired, axis=0)) / norm_gain[0]
    grad_query_key = small[2 * states + 3 : used].reshape(grad_query_key.shape)
    grad_eta = (inflow * paired).T
    grad_beta = (eta * paired * gate).T
    grad_forget = (eta * paired * beta * (1.0 - forget) / gate - mix * cross).T
    vdim = value_weight.shape[1]
    if chained:
        outs, main, inner = early
        zdim = gains.shape[1]
        groups = [
            (
                [outs, inner],
                [
                    (0, slice(0, width), 0, 0),
                    (0, slice(width, 2 * width), 1, 0),
                    (1, slice(0, ffn_in.shape[1]), 2, 0),
                ],
                [ffn_out.shape, output_weight.shape, ffn_in.shape],
            ),
            (
                [main, late],
                [
                    (0, slice(0, grad_main.shape[-1]), 0, zdim),
                    (1, slice(0, vdim), 1, 0),
                    (1, slice(vdim, vdim + zdim), 0, 0),
                ],
                [base_weight.shape, value_weight.shape],
            ),
        ]
        first = gathered(*groups[0])
        late.give()
        second = gathered(*groups[1])
        grad_ffn_out, grad_output_weight, grad_ffn_in = gathered(*groups[0], first)
        grad_base_weight, grad_value_weight = gathered(*groups[1], second)
    else:
        grad_base = jnp.concatenate([grad_shared, grad_main], axis=-1)
        (
            grad_ffn_out,
            grad_output_weight,
            grad_base_weight,
            grad_ffn_in,
            grad_value_weight,
        ) = summed_everywhere(
            [
                weight_grad(act, cotangent),
                weight_grad(product, grad_proj),
                weight_grad(mixed, grad_base),
                weight_grad(ffn_low, grad_inner),
                weight_grad(normed, grad_vpre),
            ]
        )
    return (
        block_out,
        grad_tokens,
        grad_norm_gain,
        grad_value_weight,
        grad_forget,
        grad_beta,
        grad_eta,
        grad_omega,
        grad_base_weight,
        grad_query_key[:2],
        grad_query_key[2:],
        grad_output_weight,
        grad_ffn_gain,
        grad_ffn_in,
        grad_ffn_out,
    )


def solution(mesh):
    return jax.shard_map(
        per_device,
        mesh=mesh,
        in_specs=(
            P("row", "seq", None),
            P("row"),
            P(),
            P(),
            P(),
            P(),
            P(),
            P(),
            P(),
            P(),
            P(),
            P(),
            P(),
            P(),
            P(),
            P("row", "seq", None),
        ),
        out_specs=(
            P("row", "seq", None),
            P("row", "seq", None),
            P(),
            P(),
            P(),
            P(),
            P(),
            P(),
            P(),
            P(),
            P(),
            P(),
            P(),
            P(),
            P(),
        ),
        check_vma=False,
    )
```

```python
import functools

import jax
import jax.numpy as jnp
from jax import lax
from jax.experimental import pallas as pl
from jax.experimental.pallas import tpu as pltpu
from jax.sharding import PartitionSpec as P

GROUP = 128
STEPS = 32
LAG = 8
LANES = 128

epsilon = 1e-05
very_low = -1e30
scan_params = pltpu.CompilerParams(vmem_limit_bytes=20 * 2**20)
front_params = pltpu.CompilerParams(vmem_limit_bytes=52 * 2**20)
dense_params = pltpu.CompilerParams(vmem_limit_bytes=36 * 2**20)


def work_cost(flops, seconds):
    return pl.CostEstimate(flops=int(flops), bytes_accessed=int(seconds * 3.0e12), transcendentals=0)


def sigmoid(value):
    return 0.5 * jnp.tanh(0.5 * value) + 0.5


def unit_norm(values):
    centered = values - jnp.mean(values, axis=-1, keepdims=True)
    spread = jnp.mean(centered * centered, axis=-1, keepdims=True)
    scale = lax.rsqrt(spread + epsilon)
    return centered * scale, scale


def norm_backward(grad, unit_values, scale):
    along = jnp.mean(grad * unit_values, axis=-1, keepdims=True)
    return scale * (grad - jnp.mean(grad, axis=-1, keepdims=True) - unit_values * along)


def whole_spec(shape):
    return pl.BlockSpec(shape, lambda step: (0,) * len(shape))


def lane_slices(width):
    return [slice(low, low + LANES) for low in range(0, width, LANES)]


def spread_rows(ref, index, lanes, rows):
    return jnp.broadcast_to(ref[index : index + 1, lanes], (rows, LANES))


def add_all(parts):
    while len(parts) > 1:
        parts = [
            parts[at] + parts[at + 1] if at + 1 < len(parts) else parts[at]
            for at in range(0, len(parts), 2)
        ]
    return parts[0]


def enter_body(count_ref, tokens_ref, gain_ref, retain_ref, low_ref, turned_ref, end_ref, state):
    step = pl.program_id(0)
    rows, steps, width = tokens_ref.shape
    states = retain_ref.shape[0]

    @pl.when(step == 0)
    def _():
        state[...] = jnp.zeros_like(state)

    values = tokens_ref[...].astype(jnp.float32)
    centered = values - jnp.mean(values, axis=-1, keepdims=True)
    spread = jnp.mean(centered * centered, axis=-1, keepdims=True)
    normed = centered * lax.rsqrt(spread + epsilon) * gain_ref[...]
    low_ref[...] = normed.astype(jnp.bfloat16)
    places = step * steps + lax.broadcasted_iota(jnp.int32, (steps, 1), 0)
    kept = jnp.stack([jnp.where(places < count_ref[row], normed[row], 0.0) for row in range(rows)])
    for lanes in lane_slices(width):
        for unit in range(steps // LAG):
            part = slice(unit * LAG, (unit + 1) * LAG)
            turned_ref[part, :, lanes] = jnp.swapaxes(kept[:, part, lanes], 0, 1)
    for lanes in lane_slices(width):
        retain = [spread_rows(retain_ref, j, lanes, rows) for j in range(states)]

        def unit_step(unit, hidden):
            for within in range(LAG):
                entry = turned_ref[unit * LAG + within, :, lanes]
                hidden = [retain[j] * hidden[j] + entry for j in range(states)]
            return hidden

        hidden = lax.fori_loop(
            0, steps // LAG, unit_step, [state[j, :, lanes] for j in range(states)]
        )
        for j in range(states):
            state[j, :, lanes] = hidden[j]

    @pl.when(step == pl.num_programs(0) - 1)
    def _():
        end_ref[...] = state[...]


def enter_call(counts, tokens, gain, retain):
    rows, length, width = tokens.shape
    states = retain.shape[0]
    natural = pl.BlockSpec((rows, STEPS, width), lambda step: (0, step, 0))
    return pl.pallas_call(
        enter_body,
        grid=(length // STEPS,),
        in_specs=[
            pl.BlockSpec(memory_space=pltpu.SMEM),
            natural,
            whole_spec((1, width)),
            whole_spec((states, width)),
        ],
        out_specs=(
            natural,
            pl.BlockSpec((STEPS, rows, width), lambda step: (step, 0, 0)),
            whole_spec((states, rows, width)),
        ),
        out_shape=(
            jax.ShapeDtypeStruct(tokens.shape, jnp.bfloat16),
            jax.ShapeDtypeStruct((length, rows, width), jnp.float32),
            jax.ShapeDtypeStruct((states, rows, width), jnp.float32),
        ),
        scratch_shapes=[pltpu.VMEM((states, rows, width), jnp.float32)],
        compiler_params=front_params,
        cost_estimate=work_cost(0.0, 9e-6),
        name="enter",
    )(counts, tokens, gain, retain)


def average_body(turned_ref, retain_ref, mix_ref, held_ref, state, out_ref):
    step = pl.program_id(0)
    steps, rows, width = turned_ref.shape
    states = retain_ref.shape[0]

    @pl.when(step == 0)
    def _():
        state[...] = held_ref[...]

    for lanes in lane_slices(width):
        retain = [spread_rows(retain_ref, j, lanes, rows) for j in range(states)]
        mix = [spread_rows(mix_ref, j, lanes, rows) for j in range(states)]

        def unit_step(unit, hidden):
            sums = []
            for within in range(LAG):
                entry = turned_ref[unit * LAG + within, :, lanes]
                hidden = [retain[j] * hidden[j] + entry for j in range(states)]
                sums.append(add_all([mix[j] * hidden[j] for j in range(states)]))
            out_ref[:, pl.ds(unit * LAG, LAG), lanes] = jnp.swapaxes(jnp.stack(sums), 0, 1)
            return hidden

        hidden = lax.fori_loop(
            0, steps // LAG, unit_step, [state[j, :, lanes] for j in range(states)]
        )
        for j in range(states):
            state[j, :, lanes] = hidden[j]


def average_call(turned, retain, mix, start):
    length, rows, width = turned.shape
    states = retain.shape[0]
    held = (states, rows, width)
    return pl.pallas_call(
        average_body,
        grid=(length // STEPS,),
        in_specs=[
            pl.BlockSpec((STEPS, rows, width), lambda step: (step, 0, 0)),
            whole_spec((states, width)),
            whole_spec((states, width)),
            whole_spec(held),
        ],
        out_specs=(
            whole_spec(held),
            pl.BlockSpec((rows, STEPS, width), lambda step: (0, step, 0)),
        ),
        out_shape=(
            jax.ShapeDtypeStruct(held, jnp.float32),
            jax.ShapeDtypeStruct((rows, length, width), jnp.float32),
        ),
        compiler_params=front_params,
        cost_estimate=work_cost(0.0, 12e-6),
        name="average",
    )(turned, retain, mix, start)


def return_body(grad_ref, retain_ref, turned_ref, end_ref, state):
    step = pl.program_id(0)
    rows, steps, width = grad_ref.shape
    states = retain_ref.shape[0]

    @pl.when(step == 0)
    def _():
        state[...] = jnp.zeros_like(state)

    for lanes in lane_slices(width):
        retain = [spread_rows(retain_ref, j, lanes, rows) for j in range(states)]

        def unit_step(unit, hidden):
            part = pl.ds((steps // LAG - 1 - unit) * LAG, LAG)
            turned = jnp.swapaxes(grad_ref[:, part, lanes], 0, 1)
            turned_ref[part, :, lanes] = turned
            for within in reversed(range(LAG)):
                hidden = [retain[j] * hidden[j] + turned[within] for j in range(states)]
            return hidden

        hidden = lax.fori_loop(
            0, steps // LAG, unit_step, [state[j, :, lanes] for j in range(states)]
        )
        for j in range(states):
            state[j, :, lanes] = hidden[j]

    @pl.when(step == pl.num_programs(0) - 1)
    def _():
        end_ref[...] = state[...]


def return_call(grad, retain):
    rows, length, width = grad.shape
    states = retain.shape[0]
    last = length // STEPS - 1
    return pl.pallas_call(
        return_body,
        grid=(length // STEPS,),
        in_specs=[
            pl.BlockSpec((rows, STEPS, width), lambda step: (0, last - step, 0)),
            whole_spec((states, width)),
        ],
        out_specs=(
            pl.BlockSpec((STEPS, rows, width), lambda step: (last - step, 0, 0)),
            whole_spec((states, rows, width)),
        ),
        out_shape=(
            jax.ShapeDtypeStruct((length, rows, width), jnp.float32),
            jax.ShapeDtypeStruct((states, rows, width), jnp.float32),
        ),
        scratch_shapes=[pltpu.VMEM((states, rows, width), jnp.float32)],
        compiler_params=scan_params,
        cost_estimate=work_cost(0.0, 8e-6),
        name="back_enter",
    )(grad, retain)


def sums_body(
    grad_ref,
    turned_ref,
    retain_ref,
    inverse_ref,
    unit_ref,
    held_ref,
    lag_in_ref,
    carry_ref,
    lag_ref,
):
    step = pl.program_id(0)
    steps, rows, width = grad_ref.shape
    states = retain_ref.shape[0]
    half = states // 2
    units = steps // LAG

    @pl.when(step == 0)
    def _():
        carry_ref[...] = held_ref[...]
        lag_ref[...] = lag_in_ref[...]

    for lanes in lane_slices(width):
        for first in range(0, states, half):
            chosen = range(first, first + half)
            retain = [spread_rows(retain_ref, j, lanes, rows) for j in chosen]
            inverse = [spread_rows(inverse_ref, j, lanes, rows) for j in chosen]

            def unit_step(unit, carried):
                after, hidden, cross = carried
                unit = units - 1 - unit
                later = after
                for within in reversed(range(LAG)):
                    place = unit * LAG + within
                    entry = turned_ref[place, :, lanes]
                    grad = grad_ref[place, :, lanes]
                    after = [retain[m] * after[m] + grad for m in range(half)]
                    hidden = [(hidden[m] - entry) * inverse[m] for m in range(half)]
                    cross = [cross[m] + after[m] * hidden[m] for m in range(half)]
                for m, j in enumerate(chosen):
                    unit_decay = spread_rows(unit_ref, j, lanes, rows)
                    carry_ref[3, j, :, lanes] += hidden[m] * (after[m] - unit_decay * later[m])
                return after, hidden, cross

            results = lax.fori_loop(
                0,
                units,
                unit_step,
                tuple([carry_ref[kind, j, :, lanes] for j in chosen] for kind in range(3)),
            )
            for kind in range(3):
                for m, j in enumerate(chosen):
                    carry_ref[kind, j, :, lanes] = results[kind][m]

        def lag_step(unit, lags):
            entries = [turned_ref[unit * LAG + at, :, lanes] for at in range(LAG)]
            grads = [grad_ref[unit * LAG + at, :, lanes] for at in range(LAG)]
            return [
                lags[lag] + add_all([grads[at] * entries[at - lag] for at in range(lag, LAG)])
                for lag in range(LAG)
            ]

        lags = lax.fori_loop(0, units, lag_step, [lag_ref[at, :, lanes] for at in range(LAG)])
        for at in range(LAG):
            lag_ref[at, :, lanes] = lags[at]


def sums_call(low_end, high_end, grad, turned, params, carried):
    rows, width = grad.shape[1:]
    states = params[0].shape[0]
    last = high_end // STEPS - 1
    turned_spec = pl.BlockSpec((STEPS, rows, width), lambda step: (last - step, 0, 0))
    carried_specs = [whole_spec(value.shape) for value in carried]
    return pl.pallas_call(
        sums_body,
        grid=((high_end - low_end) // STEPS,),
        in_specs=[turned_spec] * 2 + [whole_spec((states, width))] * 3 + carried_specs,
        out_specs=carried_specs,
        out_shape=[jax.ShapeDtypeStruct(value.shape, jnp.float32) for value in carried],
        compiler_params=scan_params,
        cost_estimate=work_cost(0.0, 8e-6),
        name="adjoint_sums",
    )(grad, turned, *params, *carried)


def leave_body(
    count_ref,
    tokens_ref,
    gain_ref,
    part_ref,
    residual_ref,
    grad_ref,
    retain_ref,
    mix_ref,
    held_ref,
    *others,
    places_before,
):
    carry_ref, out_ref, path = others[-3:]
    step = pl.program_id(0)
    steps, rows, width = grad_ref.shape
    states = retain_ref.shape[0]
    units = steps // LAG

    @pl.when(step == 0)
    def _():
        carry_ref[...] = held_ref[...]

    for lanes in lane_slices(width):
        retain = [spread_rows(retain_ref, j, lanes, rows) for j in range(states)]
        mix = [spread_rows(mix_ref, j, lanes, rows) for j in range(states)]

        def unit_step(unit, after):
            unit = units - 1 - unit
            sums = []
            for within in reversed(range(LAG)):
                grad = grad_ref[unit * LAG + within, :, lanes]
                after = [retain[j] * after[j] + grad for j in range(states)]
                sums.append(add_all([mix[j] * after[j] for j in range(states)]))
            path[:, pl.ds(unit * LAG, LAG), lanes] = jnp.swapaxes(jnp.stack(sums[::-1]), 0, 1)
            return after

        after = lax.fori_loop(
            0, units, unit_step, [carry_ref[j, :, lanes] for j in range(states)]
        )
        for j in range(states):
            carry_ref[j, :, lanes] = after[j]

    first_place = places_before + (pl.num_programs(0) - 1 - step) * steps
    places = first_place + lax.broadcasted_iota(jnp.int32, (steps, 1), 0)
    gain = gain_ref[...]
    for row in range(rows):
        unit_values, scale = unit_norm(tokens_ref[row].astype(jnp.float32))
        grad = part_ref[row].astype(jnp.float32)
        grad = grad + jnp.where(places < count_ref[row], path[row], 0.0)
        out = norm_backward(grad * gain, unit_values, scale)
        out_ref[row] = (out + residual_ref[row].astype(jnp.float32)).astype(jnp.bfloat16)


def leave_call(
    low_end, high_end, counts, tokens, gain, part, residual, grad, retain, mix, carried
):
    rows, length, width = tokens.shape
    held = carried[0].shape
    last = high_end // STEPS - 1
    going_on = len(carried) > 1
    natural = pl.BlockSpec((rows, STEPS, width), lambda step: (0, last - step, 0))
    return pl.pallas_call(
        functools.partial(leave_body, places_before=low_end),
        grid=((high_end - low_end) // STEPS,),
        in_specs=[
            pl.BlockSpec(memory_space=pltpu.SMEM),
            natural,
            whole_spec((1, width)),
            natural,
            natural,
            pl.BlockSpec((STEPS, rows, width), lambda step: (last - step, 0, 0)),
            whole_spec(retain.shape),
            whole_spec(mix.shape),
            whole_spec(held),
        ]
        + [pl.BlockSpec(memory_space=pl.ANY)] * going_on,
        out_specs=[whole_spec(held), natural],
        out_shape=[
            jax.ShapeDtypeStruct(held, jnp.float32),
            jax.ShapeDtypeStruct((rows, length, width), jnp.bfloat16),
        ],
        input_output_aliases={9: 1} if going_on else {},
        scratch_shapes=[pltpu.VMEM((rows, STEPS, width), jnp.float32)],
        compiler_params=scan_params,
        cost_estimate=work_cost(0.0, 8e-6),
        name="leave",
    )(counts, tokens, gain, part, residual, grad, retain, mix, *carried)


class Exchange:
    def __init__(self, local, decay, axis, backward):
        self.axis, self.backward = axis, backward
        self.count = lax.axis_size(axis)
        place = lax.axis_index(axis)
        self.place = self.count - 1 - place if backward else place
        self.low = self.place % 2
        self.half = local.shape[-1] // 2
        self.local = local
        self.decay = self.part(decay, self.low)

    def part(self, value, which):
        return lax.dynamic_slice_in_dim(value, which * self.half, self.half, value.ndim - 1)

    def moved(self, value, pairs):
        last = self.count - 1
        if self.backward:
            pairs = [(last - source, last - target) for source, target in pairs]
        return lax.ppermute(value, self.axis, pairs)

    def swapped(self, value):
        return self.moved(value, [(at, at ^ 1) for at in range(self.count)])

    def later(self, value, hop):
        return self.moved(value, [(at, at + 2 * hop) for at in range(self.count - 2 * hop)])

    def share(self):
        own = self.part(self.local, self.low)
        other = self.swapped(self.part(self.local, 1 - self.low))
        self.first = jnp.where(self.low == 0, own, other)
        self.pair = self.decay * self.first + jnp.where(self.low == 0, other, own)

    def cross(self):
        pairs = self.count // 2
        decay = self.decay * self.decay
        if pairs <= 4:
            arrived = [self.later(self.pair, hop) for hop in range(1, pairs)]
            total = arrived[-1]
            for value in arrived[-2::-1]:
                total = decay * total + value
        else:
            total, hop = self.later(self.pair, 1), 1
            while hop < pairs - 1:
                total = total + decay * self.later(total, hop)
                decay = decay * decay
                hop *= 2
        self.start = total

    def give(self):
        second = self.decay * self.start + self.first
        kept = jnp.where(self.low == 0, self.start, second)
        got = self.swapped(jnp.where(self.low == 0, second, self.start))
        return jnp.concatenate(
            [jnp.where(self.low == 0, kept, got), jnp.where(self.low == 0, got, kept)], axis=-1
        )


mesh_axes = ("seq", "row")


def device_total():
    return lax.axis_size("seq") * lax.axis_size("row")


def device_place():
    return lax.axis_index("seq") * lax.axis_size("row") + lax.axis_index("row")


def swapped(value, bit):
    return lax.ppermute(value, mesh_axes, [(at, at ^ bit) for at in range(device_total())])


def half_summed(value, bit):
    half = value.shape[0] // 2
    mine = (device_place() // bit) % 2
    sent = lax.dynamic_slice_in_dim(value, (1 - mine) * half, half, 0)
    kept = lax.dynamic_slice_in_dim(value, mine * half, half, 0)
    return kept + swapped(sent, bit)


def both_halves(value, bit):
    mine = (device_place() // bit) % 2 == 1
    other = swapped(value, bit)
    return jnp.concatenate([jnp.where(mine, other, value), jnp.where(mine, value, other)], axis=0)


def link_orders():
    total = device_total()
    bits = [1 << at for at in range(total.bit_length() - 1)]
    if (lax.axis_size("seq"), lax.axis_size("row")) == (8, 4):
        core, x, y, z_low, z_high = bits
        return (
            (core, x, y, z_low, z_high),
            (core, y, z_low, x, z_high),
            (core, z_low, x, y, z_high),
        )
    third = len(bits) // 3
    return tuple(bits[turn * third :] + bits[: turn * third] for turn in range(3))


def summed_everywhere(values):
    orders = link_orders()
    for at in range(len(orders[0])):
        values = [half_summed(v, orders[n % 3][at]) for n, v in enumerate(values)]
    for at in reversed(range(len(orders[0]))):
        values = [both_halves(v, orders[n % 3][at]) for n, v in enumerate(values)]
    return values


def paired_sum(value, group):
    partners = [group[0]] if len(group) == 1 else [group[0], group[1], group[0] + group[1]]
    arrived = [swapped(value, partner) for partner in partners]
    if len(arrived) == 1:
        return value + arrived[0]
    return (value + arrived[0]) + (arrived[1] + arrived[2])


def small_sum(value):
    bits = [1 << at for at in range(device_total().bit_length() - 1)]
    for at in range(0, len(bits), 2):
        value = paired_sum(value, bits[at : at + 2])
    return value


def power_of(value, exponent):
    result = None
    while exponent:
        if exponent & 1:
            result = value if result is None else result * value
        value = value * value
        exponent >>= 1
    return result


def dot(first_op, second_op):
    return jnp.dot(first_op, second_op, preferred_element_type=jnp.float32)


def dot_back(first_op, second_op):
    return lax.dot_general(
        first_op, second_op, (((1,), (1,)), ((), ())), preferred_element_type=jnp.float32
    )


def dot_outer(first_op, second_op):
    return lax.dot_general(
        first_op, second_op, (((0,), (0,)), ((), ())), preferred_element_type=jnp.float32
    )


def low(value):
    return value.astype(jnp.bfloat16)


def chunks(low_end, high_end, size):
    return [slice(at, min(at + size, high_end)) for at in range(low_end, high_end, size)]


def gated(value):
    half = 0.5 * value
    turn = jnp.tanh(half)
    gate = 0.5 * turn + 0.5
    act = half * turn + half
    return act, gate + act * (1.0 - gate)


def value_body(normed_ref, value_weight_ref, value_ref, value_slope_ref):
    for part in chunks(0, value_ref.shape[1], 256):
        value, slope = gated(low(dot(normed_ref[...], value_weight_ref[:, part])))
        value_ref[:, part] = low(value)
        value_slope_ref[:, part] = low(slope)


def value_call(normed, value_weight):
    rows, length, width = normed.shape
    vdim = value_weight.shape[1]
    return pl.pallas_call(
        value_body,
        grid=(rows,),
        in_specs=[row_spec(length, width), once_spec(value_weight.shape)],
        out_specs=[row_spec(length, vdim)] * 2,
        out_shape=[jax.ShapeDtypeStruct((rows, length, vdim), jnp.bfloat16)] * 2,
        compiler_params=front_params,
        cost_estimate=work_cost(2e9, 5e-6),
        name="value",
    )(normed, value_weight)


def forward_body(
    count_ref,
    tokens_ref,
    cotangent_ref,
    average_ref,
    normed_ref,
    value_ref,
    value_slope_ref,
    omega_ref,
    base_weight_ref,
    gains_ref,
    biases_ref,
    output_weight_ref,
    ffn_gain_ref,
    ffn_in_ref,
    ffn_out_ref,
    out_ref,
    mixed_ref,
    mixed_slope_ref,
    product_ref,
    ffn_low_ref,
    act_ref,
    grad_inner_ref,
    grad_proj_ref,
    grad_main_ref,
    grad_shared_ref,
    grad_vpre_ref,
    residual_ref,
    ffn_gain_grad_ref,
    grad_gains_ref,
    reset_ref,
    reset_slope_ref,
    grad_attended_ref,
    probs_ref,
    query_ref,
    key_ref,
    shared_ref,
    shared_slope_ref,
):
    row = pl.program_id(0)
    length, width = tokens_ref.shape
    zdim = query_ref.shape[1]
    vdim = value_ref.shape[1]
    inner = act_ref.shape[1]

    @pl.when(row == 0)
    def _():
        ffn_gain_grad_ref[...] = jnp.zeros_like(ffn_gain_grad_ref)
        grad_gains_ref[...] = jnp.zeros_like(grad_gains_ref)

    normed = normed_ref[...]
    sums = average_ref[...] + omega_ref[...] * normed.astype(jnp.float32)
    gate = sigmoid(sums)
    mixed = sums * gate
    mixed_ref[...] = low(mixed)
    mixed_slope_ref[...] = low(gate + mixed * (1.0 - gate))
    mixed_low = mixed_ref[...]

    shared = dot(mixed_low, base_weight_ref[:, :zdim])
    gate = sigmoid(shared)
    shared_act = shared * gate
    shared_ref[...] = shared_act
    shared_slope_ref[...] = gate + shared_act * (1.0 - gate)
    query_ref[...] = low(shared_act * gains_ref[0:1] + biases_ref[0:1])
    key_ref[...] = low(shared_act * gains_ref[1:2] + biases_ref[1:2])

    to_place = lax.broadcasted_iota(jnp.int32, (GROUP, GROUP), 0)
    from_place = lax.broadcasted_iota(jnp.int32, (GROUP, GROUP), 1)
    for block in chunks(0, length, GROUP):
        allowed = (from_place <= to_place) & (
            (from_place < count_ref[row] - block.start) | (from_place == to_place)
        )
        scores = dot_back(query_ref[block], key_ref[block]) * zdim**-0.5
        scores = jnp.where(allowed, scores, very_low)
        weights = jnp.exp(scores - jnp.max(scores, axis=-1, keepdims=True))
        weights = jnp.where(allowed, weights, 0.0)
        probs_ref[block] = weights / jnp.sum(weights, axis=-1, keepdims=True)

    for part in chunks(0, vdim, 256):
        base_part = slice(zdim + part.start, zdim + part.stop)
        reset_act, reset_slope = gated(low(dot(mixed_low, base_weight_ref[:, base_part])))
        reset_ref[:, part] = low(reset_act)
        for block in chunks(0, length, GROUP):
            attended = low(dot(low(probs_ref[block]), value_ref[block, part]))
            product_ref[block, part] = low(attended * reset_act[block])
            reset_slope_ref[block, part] = low(attended * reset_slope[block])

    update_gate = sigmoid(dot(mixed_low, base_weight_ref[:, zdim + vdim : zdim + vdim + width]))
    candidate = dot(mixed_low, base_weight_ref[:, zdim + vdim + width :])
    candidate = candidate + dot(product_ref[...], output_weight_ref[...])
    candidate_gate = sigmoid(candidate)
    candidate_act = candidate * candidate_gate
    candidate_slope = candidate_gate + candidate_act * (1.0 - candidate_gate)
    tokens = tokens_ref[...].astype(jnp.float32)
    change = candidate_act - tokens
    after = tokens + update_gate * change
    unit_values, scale = unit_norm(after)
    ffn_low_ref[...] = low(unit_values * ffn_gain_ref[...])
    ffn_low = ffn_low_ref[...]
    cotangent = cotangent_ref[...]

    out = after
    grad_normed = jnp.zeros_like(after)
    for part in chunks(0, inner, 256):
        act, slope = gated(low(dot(ffn_low, ffn_in_ref[:, part])))
        act_ref[:, part] = low(act)
        grad_act = low(dot_back(cotangent, ffn_out_ref[part]))
        grad_inner_ref[:, part] = low(grad_act * slope)
    out = after + dot(act_ref[...], ffn_out_ref[...])
    out_ref[...] = low(out)
    grad_normed = dot_back(grad_inner_ref[...], ffn_in_ref[...])
    ffn_gain_grad_ref[...] += jnp.sum(grad_normed * unit_values, axis=0, keepdims=True)
    grad_after = cotangent.astype(jnp.float32) + norm_backward(
        grad_normed * ffn_gain_ref[...], unit_values, scale
    )
    grad_change = grad_after * update_gate
    grad_proj = low(grad_change * candidate_slope)
    grad_proj_ref[...] = grad_proj
    grad_main_ref[:, vdim : vdim + width] = low(grad_change * change * (1.0 - update_gate))
    grad_main_ref[:, vdim + width :] = grad_proj
    for part in chunks(0, vdim, 256):
        grad_product = low(dot_back(grad_proj, output_weight_ref[part]))
        grad_attended_ref[:, part] = low(grad_product * reset_ref[:, part])
        grad_main_ref[:, part] = low(grad_product * reset_slope_ref[:, part])

    grad_gains = jnp.zeros(grad_gains_ref.shape, jnp.float32)
    for block in chunks(0, length, GROUP):
        probs = probs_ref[block]
        probs_low = low(probs)
        grad_probs = dot_back(grad_attended_ref[block], value_ref[block])
        for part in chunks(0, vdim, 512):
            grad_value = dot_outer(probs_low, grad_attended_ref[block, part])
            grad_vpre_ref[block, part] = low(low(grad_value) * value_slope_ref[block, part])
        total = jnp.sum(grad_probs * probs, axis=-1, keepdims=True)
        grad_raw = low(probs * (grad_probs - total) * zdim**-0.5)
        grad_query = dot(grad_raw, key_ref[block])
        grad_key = dot_outer(grad_raw, query_ref[block])
        shared = shared_ref[block]
        grad_gains = grad_gains + jnp.concatenate(
            [
                jnp.sum(value, axis=0, keepdims=True)
                for value in (grad_query * shared, grad_key * shared, grad_query, grad_key)
            ],
            axis=0,
        )
        grad_shared = grad_query * gains_ref[0:1] + grad_key * gains_ref[1:2]
        grad_shared_ref[block] = low(grad_shared * shared_slope_ref[block])
    grad_gains_ref[...] += grad_gains
    residual_ref[...] = low(grad_after - grad_change)


def row_spec(length, width):
    return pl.BlockSpec((None, length, width), lambda row: (row, 0, 0))


def once_spec(shape):
    return pl.BlockSpec(shape, lambda row: (0,) * len(shape), pipeline_mode=pl.Buffered(1))


def forward_call(
    counts,
    tokens,
    cotangent,
    average,
    normed,
    value,
    value_slope,
    omega,
    base_weight,
    gains,
    biases,
    output_weight,
    ffn_gain,
    ffn_in,
    ffn_out,
):
    rows, length, width = tokens.shape
    zdim, vdim, inner = gains.shape[1], value.shape[2], ffn_in.shape[1]
    half, full = jnp.bfloat16, jnp.float32
    outs = [
        (width, half),
        (width, half),
        (width, half),
        (vdim, half),
        (width, half),
        (inner, half),
        (inner, half),
        (width, half),
        (vdim + 2 * width, half),
        (zdim, half),
        (vdim, half),
        (width, half),
    ]
    tied = [
        omega,
        base_weight,
        gains,
        biases,
        output_weight,
        ffn_gain,
        ffn_in,
        ffn_out,
    ]
    return pl.pallas_call(
        forward_body,
        grid=(rows,),
        in_specs=[pl.BlockSpec(memory_space=pltpu.SMEM)]
        + [row_spec(length, width)] * 4
        + [row_spec(length, vdim)] * 2
        + [once_spec(weight.shape) for weight in tied],
        out_specs=[row_spec(length, size) for size, _ in outs]
        + [whole_spec((1, width)), whole_spec((4, zdim))],
        out_shape=[jax.ShapeDtypeStruct((rows, length, size), kind) for size, kind in outs]
        + [jax.ShapeDtypeStruct((1, width), full), jax.ShapeDtypeStruct((4, zdim), full)],
        scratch_shapes=[pltpu.VMEM((length, vdim), half)] * 3
        + [pltpu.VMEM((length, GROUP), full)]
        + [pltpu.VMEM((length, zdim), half)] * 2
        + [pltpu.VMEM((length, zdim), full)] * 2,
        compiler_params=dense_params,
        cost_estimate=work_cost(18e9, 40e-6),
        name="dense_forward",
    )(counts, tokens, cotangent, average, normed, value, value_slope, *tied)


def backward_body(
    grad_main_ref,
    grad_shared_ref,
    grad_vpre_ref,
    normed_ref,
    mixed_slope_ref,
    omega_ref,
    value_weight_ref,
    base_weight_ref,
    grad_average_ref,
    part_ref,
    grad_omega_ref,
    grad_gain_ref,
):
    zdim = grad_shared_ref.shape[1]

    @pl.when(pl.program_id(0) == 0)
    def _():
        grad_omega_ref[...] = jnp.zeros_like(grad_omega_ref)
        grad_gain_ref[...] = jnp.zeros_like(grad_gain_ref)

    grad_average = dot_back(grad_main_ref[...], base_weight_ref[:, zdim:])
    grad_average = grad_average + dot_back(grad_shared_ref[...], base_weight_ref[:, :zdim])
    grad_average = grad_average * mixed_slope_ref[...].astype(jnp.float32)
    grad_average_ref[...] = grad_average
    part = dot_back(grad_vpre_ref[...], value_weight_ref[...]) + grad_average * omega_ref[...]
    part_ref[...] = part
    normed = normed_ref[...].astype(jnp.float32)
    grad_omega_ref[...] += jnp.sum(grad_average * normed, axis=0, keepdims=True)
    grad_gain_ref[...] += jnp.sum(part * normed, axis=0, keepdims=True)


def backward_call(inputs, tied_inputs):
    rows, length, _ = inputs[0].shape
    width = tied_inputs[0].shape[1]
    return pl.pallas_call(
        backward_body,
        grid=(rows,),
        in_specs=[row_spec(length, value.shape[2]) for value in inputs]
        + [once_spec(value.shape) for value in tied_inputs],
        out_specs=[row_spec(length, width)] * 2 + [whole_spec((1, width))] * 2,
        out_shape=[jax.ShapeDtypeStruct((rows, length, width), jnp.float32)] * 2
        + [jax.ShapeDtypeStruct((1, width), jnp.float32)] * 2,
        compiler_params=dense_params,
        cost_estimate=work_cost(7e9, 12e-6),
        name="dense_backward",
    )(*inputs, *tied_inputs)


def joined_body(*refs, widths, split):
    refs = refs[1:] if split else refs
    outs_per_chain = 2 if split else 1
    outs = refs[len(refs) - outs_per_chain * len(widths) :]
    at = 0
    for chain, parts in enumerate(widths):
        for side in range(outs_per_chain):
            column = 0
            for width in parts:
                total = refs[at][...] + refs[at + 1][...]
                outs[chain * outs_per_chain + side][:, column : column + width] = total
                column += width
                at += 2


def joined(chains):
    split = chains[0][2] is not None
    sides = 2 if split else 1
    widths = [[value.shape[1] for value in kept] for kept, _, _ in chains]
    sizes = [kept[0].shape[0] // sides for kept, _, _ in chains]
    steps = 4
    while any(size % (8 * steps) for size in sizes):
        steps //= 2
    operands, in_specs, out_specs, out_shape = [], [], [], []
    for chain, (kept, arrived, _) in enumerate(chains):
        block = sizes[chain] // steps
        for side in range(sides):

            def place(step, *held, chain=chain, side=side):
                if not held:
                    return step, 0
                mine = held[0][chain]
                return (1 - mine if side else mine) * steps + step, 0

            for pair in zip(kept, arrived):
                for value in pair:
                    operands.append(value)
                    in_specs.append(pl.BlockSpec((block, value.shape[1]), place))
            total = sum(widths[chain])
            out_specs.append(pl.BlockSpec((block, total), lambda step, *held: (step, 0)))
            out_shape.append(jax.ShapeDtypeStruct((sizes[chain], total), jnp.float32))
    if split:
        mine = [(device_place() // bit) % 2 for _, _, bit in chains]
        operands.insert(0, jnp.stack(mine).astype(jnp.int32))
    outs = pl.pallas_call(
        functools.partial(joined_body, widths=widths, split=split),
        grid_spec=pltpu.PrefetchScalarGridSpec(
            num_scalar_prefetch=1 if split else 0,
            grid=(steps,),
            in_specs=in_specs,
            out_specs=out_specs,
        ),
        out_shape=out_shape,
        compiler_params=scan_params,
        cost_estimate=work_cost(0.0, 2e-6),
        name="joined",
    )(*operands)
    return [tuple(outs[at : at + sides]) for at in range(0, len(outs), sides)]


def placed_body(*refs, copies, sources):
    mine, refs = refs[0], refs[1:]
    half = pl.program_id(0)
    for own, arrived, which, taken, result, column in copies:
        there = slice(column, column + taken.stop - taken.start)

        @pl.when(half == mine[which])
        def _(own=own, taken=taken, result=result, there=there):
            refs[sources + result][:, there] = refs[own][:, taken]

        @pl.when(half != mine[which])
        def _(arrived=arrived, taken=taken, result=result, there=there):
            refs[sources + result][:, there] = refs[arrived][:, taken]


def placed(values, bits, copies, shapes):
    steps = 4
    while any(value.shape[0] % (8 * steps) for value in values):
        steps //= 2
    in_specs = []
    for at, value in enumerate(values):

        def place(half, step, mine, which=at // 2, other=at % 2):
            wanted = (half == mine[which]) != bool(other)
            return jnp.where(wanted, step, jnp.where(half == 0, 0, steps - 1)), 0

        in_specs.append(pl.BlockSpec((value.shape[0] // steps, value.shape[1]), place))
    mine = jnp.stack([(device_place() // bit) % 2 for bit in bits]).astype(jnp.int32)
    return pl.pallas_call(
        functools.partial(placed_body, copies=copies, sources=len(values)),
        grid_spec=pltpu.PrefetchScalarGridSpec(
            num_scalar_prefetch=1,
            grid=(2, steps),
            in_specs=in_specs,
            out_specs=[
                pl.BlockSpec(
                    (shape[0] // (2 * steps), shape[1]),
                    lambda half, step, mine: (half * steps + step, 0),
                )
                for shape in shapes
            ],
        ),
        out_shape=[jax.ShapeDtypeStruct(shape, jnp.float32) for shape in shapes],
        compiler_params=scan_params,
        cost_estimate=work_cost(0.0, 2e-6),
        name="placed",
    )(mine, *values)


def gathered_body(*refs, copies):
    where, refs = refs[0], refs[1:]
    results = refs[len(refs) - 1 - max(result for _, _, result, _ in copies) :]
    turn = pl.program_id(0)
    for chain, taken, result, column in copies:
        there = slice(column, column + taken.stop - taken.start)
        for piece in range(2):

            @pl.when(turn == where[2 * chain + piece])
            def _(source=2 * chain + piece, taken=taken, result=result, there=there):
                results[result][:, there] = refs[source][:, taken]


def gathered(chains, copies, shapes, before=None):
    values, where = [], []
    for one in chains:
        low = (device_place() // one.order[1]) % 2
        values += one.held if before is None else one.arrived
        where += [low, 1 - low]
    core = (device_place() // chains[0].order[0]) % 2
    where.append(core if before is None else 1 - core)
    steps = 4
    in_specs = []
    for at, value in enumerate(values):

        def place(turn, step, where, at=at):
            early = jnp.where(turn < where[at], 0, steps - 1)
            return jnp.where(turn == where[at], step, early), 0

        in_specs.append(pl.BlockSpec((value.shape[0] // steps, value.shape[1]), place))
    aliases = {}
    if before is not None:
        aliases = {1 + len(values) + at: at for at in range(len(shapes))}
        in_specs += [pl.BlockSpec(memory_space=pl.ANY)] * len(shapes)
    side = len(where) - 1
    return pl.pallas_call(
        functools.partial(gathered_body, copies=copies),
        grid_spec=pltpu.PrefetchScalarGridSpec(
            num_scalar_prefetch=1,
            grid=(2, steps),
            in_specs=in_specs,
            out_specs=[
                pl.BlockSpec(
                    (shape[0] // (4 * steps), shape[1]),
                    lambda turn, step, where: ((2 * where[side] + turn) * steps + step, 0),
                )
                for shape in shapes
            ],
        ),
        out_shape=[jax.ShapeDtypeStruct(shape, jnp.float32) for shape in shapes],
        input_output_aliases=aliases,
        compiler_params=scan_params,
        cost_estimate=work_cost(0.0, 4e-6),
        name="gathered",
    )(jnp.stack(where).astype(jnp.int32), *values, *(before or ()))


class Chain:
    def __init__(self, order, sent, kept):
        self.order, self.at = order, 0
        self.sent, self.kept, self.arrived = list(sent), list(kept), []

    def state(self):
        return self.sent, self.kept, self.arrived

    def set_state(self, state):
        self.sent, self.kept, self.arrived = state

    def send(self):
        total = len(self.order)
        bit = self.order[self.at if self.at < total else 2 * total - 1 - self.at]
        self.arrived = [swapped(value, bit) for value in self.sent]

    def give(self):
        self.held = self.sent + self.arrived
        self.arrived = [swapped(value, self.order[0]) for value in self.held]

    def pieces(self):
        return self.held + self.arrived


def join(*chains):
    total = len(chains[0].order)
    if chains[0].at < total:
        last = chains[0].at == total - 1
        results = joined(
            [
                (one.kept, one.arrived, None if last else one.order[one.at + 1])
                for one in chains
            ]
        )
        for one, result in zip(chains, results):
            if last:
                one.sent, one.kept = [result[0]], []
            else:
                one.sent, one.kept = [result[1]], [result[0]]
    else:
        values, copies, shapes = [], [], []
        for at, one in enumerate(chains):
            rows, columns = one.sent[0].shape
            values += [one.sent[0], one.arrived[0]]
            copies.append((2 * at, 2 * at + 1, at, slice(0, columns), at, 0))
            shapes.append((2 * rows, columns))
        bits = [one.order[2 * total - 1 - one.at] for one in chains]
        for one, result in zip(chains, placed(values, bits, copies, shapes)):
            one.sent = [result]
    for one in chains:
        one.arrived = []
        one.at += 1


def tied(value, *chains):
    value, states = lax.optimization_barrier((value, [one.state() for one in chains]))
    for one, state in zip(chains, states):
        one.set_state(state)
    return value


def weight_halves(first_op, second_op, bit):
    first_op = first_op.reshape(-1, first_op.shape[-1])
    second_op = second_op.reshape(-1, second_op.shape[-1])
    half = first_op.shape[1] // 2
    mine = (device_place() // bit) % 2
    return [
        dot_outer(lax.dynamic_slice_in_dim(first_op, which * half, half, 1), second_op)
        for which in (1 - mine, mine)
    ]


def weight_grad(first_op, second_op):
    return dot_outer(
        first_op.reshape(-1, first_op.shape[-1]), second_op.reshape(-1, second_op.shape[-1])
    )


def per_device(
    tokens,
    valid_count,
    norm_gain,
    value_weight,
    ema_forget,
    ema_beta,
    ema_eta,
    ema_omega,
    base_weight,
    qk_gain,
    qk_bias,
    output_weight,
    ffn_gain,
    ffn_in,
    ffn_out,
    cotangent,
):
    length, width = tokens.shape[1:]
    counts = valid_count - lax.axis_index("seq") * length
    norm_gain = norm_gain.astype(jnp.float32)[None]
    ffn_gain = ffn_gain.astype(jnp.float32)[None]
    omega = ema_omega[None]
    gains, biases = qk_gain.astype(jnp.float32), qk_bias.astype(jnp.float32)
    forget, beta, eta = ema_forget.T, ema_beta.T, ema_eta.T
    retain = 1.0 - forget
    gate = jnp.sqrt(forget * (2.0 - forget))
    inflow = beta * gate
    mix = eta * inflow
    span_decay = power_of(retain, length)[:, None, :]

    normed, turned, device_end = enter_call(counts, tokens, norm_gain, retain)
    ahead = Exchange(device_end, span_decay, "seq", False)
    ahead.share()
    ahead.cross()
    value, value_slope = value_call(normed, value_weight)
    ahead.start, value, value_slope = lax.optimization_barrier((ahead.start, value, value_slope))
    incoming = ahead.give()
    state_end, average = average_call(turned, retain, mix, incoming)
    unit_decay = power_of(retain, LAG)
    (
        block_out,
        mixed,
        mixed_slope,
        product,
        ffn_low,
        act,
        grad_inner,
        grad_proj,
        grad_main,
        grad_shared,
        grad_vpre,
        residual,
        grad_ffn_gain,
        grad_query_key,
    ) = forward_call(
        counts,
        tokens,
        cotangent,
        average,
        normed,
        value,
        value_slope,
        omega,
        base_weight,
        gains,
        biases,
        output_weight,
        ffn_gain,
        ffn_in,
        ffn_out,
    )
    orders = link_orders()
    core = orders[0][0]
    chained = device_total() == 32
    chains = []
    back_inputs = [grad_main, grad_shared, grad_vpre, normed, mixed_slope]
    if chained:
        products = [
            [(act, cotangent), (product, grad_proj)],
            [(mixed, grad_main)],
            [(ffn_low, grad_inner), (normed, grad_vpre), (mixed, grad_shared)],
        ]
        halves = [[weight_halves(*pair, core) for pair in pairs] for pairs in products]
        for order, pairs in zip(orders, halves):
            chains.append(Chain(order, [pair[0] for pair in pairs], [pair[1] for pair in pairs]))
            chains[-1].send()
        join(*chains)
        back_inputs = tied(back_inputs, *chains)
        for one in chains:
            one.send()
    grad_average, part, grad_omega, grad_gain = backward_call(
        back_inputs, [omega, value_weight, base_weight]
    )

    def halve(value):
        if chained:
            value = tied(value, *chains)
            join(*chains)
            value = tied(value, *chains)
            for one in chains:
                one.send()
        return value

    grad_turned, device_start = return_call(grad_average, retain)
    behind = Exchange(device_start, span_decay, "seq", True)
    behind.share()
    behind.pair = halve(behind.pair)
    behind.cross()
    behind.start = halve(behind.start)
    later = behind.give()
    states = retain.shape[0]
    carried = [
        jnp.stack([later, state_end, jnp.zeros_like(later), jnp.zeros_like(later)]),
        jnp.zeros((LAG,) + later.shape[1:], jnp.float32),
    ]
    parts = length // STEPS
    inverse = 1.0 / retain
    ends = [at * STEPS // 8 for at in (8 * parts, 5 * parts, 2 * parts, 0)]
    ends = [at // STEPS * STEPS for at in ends]
    for high_end, low_end in zip(ends, ends[1:]):
        carried = halve(carried)
        carried = sums_call(
            low_end, high_end, grad_turned, turned, [retain, inverse, unit_decay], carried
        )
    carry, lags = carried
    ends = [at * STEPS for at in (parts, 5 * parts // 8, 0)]
    left = [later]
    for high_end, low_end in zip(ends, ends[1:]):
        left, carry, lags = halve((left, carry, lags))
        left = leave_call(
            low_end,
            high_end,
            counts,
            tokens,
            norm_gain,
            part,
            residual,
            grad_turned,
            retain,
            mix,
            left,
        )
    left, carry, lags = lax.optimization_barrier((left, carry, lags))
    cross, border = jnp.sum(carry[2:], axis=2)
    lags = jnp.sum(lags, axis=1)
    paired = retain * border
    decay = jnp.ones_like(retain)
    for lag in range(LAG):
        paired = paired + decay * lags[lag]
        decay = decay * retain
    small = jnp.concatenate(
        [
            paired,
            cross,
            grad_gain,
            grad_omega,
            grad_ffn_gain,
            grad_query_key.reshape(-1, width),
        ],
        axis=0,
    )
    used = small.shape[0]
    small = jnp.pad(small, ((0, -used % 8), (0, 0)))
    grad_tokens = left[1]
    if chained:
        small = tied(small, *chains)
        small = small + swapped(small, core)
        for one in chains:
            one.give()
        small = paired_sum(small, orders[0][1:3])
        small = paired_sum(small, orders[0][3:5])
    else:
        small = small_sum(small)
    paired, cross = small[:states], small[states : 2 * states]
    grad_gain, grad_omega, grad_ffn_gain = (small[2 * states + at] for at in range(3))
    grad_norm_gain = (grad_gain + jnp.sum(mix * paired, axis=0)) / norm_gain[0]
    grad_query_key = small[2 * states + 3 : used].reshape(grad_query_key.shape)
    grad_eta = (inflow * paired).T
    grad_beta = (eta * paired * gate).T
    grad_forget = (eta * paired * beta * (1.0 - forget) / gate - mix * cross).T
    vdim = value_weight.shape[1]
    if chained:
        zdim, main_end, inner_dim = gains.shape[1], grad_main.shape[-1], ffn_in.shape[1]
        copies = [
            (0, slice(0, width), 0, 0),
            (0, slice(width, 2 * width), 1, 0),
            (1, slice(0, main_end), 2, zdim),
            (2, slice(inner_dim + vdim, inner_dim + vdim + zdim), 2, 0),
            (2, slice(0, inner_dim), 3, 0),
            (2, slice(inner_dim, inner_dim + vdim), 4, 0),
        ]
        shapes = [
            ffn_out.shape,
            output_weight.shape,
            base_weight.shape,
            ffn_in.shape,
            value_weight.shape,
        ]
        (
            grad_ffn_out,
            grad_output_weight,
            grad_base_weight,
            grad_ffn_in,
            grad_value_weight,
        ) = gathered(chains, copies, shapes, gathered(chains, copies, shapes))
    else:
        grad_base = jnp.concatenate([grad_shared, grad_main], axis=-1)
        (
            grad_ffn_out,
            grad_output_weight,
            grad_base_weight,
            grad_ffn_in,
            grad_value_weight,
        ) = summed_everywhere(
            [
                weight_grad(act, cotangent),
                weight_grad(product, grad_proj),
                weight_grad(mixed, grad_base),
                weight_grad(ffn_low, grad_inner),
                weight_grad(normed, grad_vpre),
            ]
        )
    return (
        block_out,
        grad_tokens,
        grad_norm_gain,
        grad_value_weight,
        grad_forget,
        grad_beta,
        grad_eta,
        grad_omega,
        grad_base_weight,
        grad_query_key[:2],
        grad_query_key[2:],
        grad_output_weight,
        grad_ffn_gain,
        grad_ffn_in,
        grad_ffn_out,
    )


def solution(mesh):
    return jax.shard_map(
        per_device,
        mesh=mesh,
        in_specs=(
            P("row", "seq", None),
            P("row"),
            P(),
            P(),
            P(),
            P(),
            P(),
            P(),
            P(),
            P(),
            P(),
            P(),
            P(),
            P(),
            P(),
            P("row", "seq", None),
        ),
        out_specs=(
            P("row", "seq", None),
            P("row", "seq", None),
            P(),
            P(),
            P(),
            P(),
            P(),
            P(),
            P(),
            P(),
            P(),
            P(),
            P(),
            P(),
            P(),
        ),
        check_vma=False,
    )
```

```python
import functools

import jax
import jax.numpy as jnp
from jax import lax
from jax.experimental import pallas as pl
from jax.experimental.pallas import tpu as pltpu
from jax.sharding import PartitionSpec as P

GROUP = 128
STEPS = 32
LAG = 8
LANES = 128

epsilon = 1e-05
very_low = -1e30
scan_params = pltpu.CompilerParams(vmem_limit_bytes=20 * 2**20)
front_params = pltpu.CompilerParams(vmem_limit_bytes=52 * 2**20)
dense_params = pltpu.CompilerParams(vmem_limit_bytes=36 * 2**20)


def work_cost(flops, seconds):
    return pl.CostEstimate(flops=int(flops), bytes_accessed=int(seconds * 3.0e12), transcendentals=0)


def sigmoid(value):
    return 0.5 * jnp.tanh(0.5 * value) + 0.5


def unit_norm(values):
    centered = values - jnp.mean(values, axis=-1, keepdims=True)
    spread = jnp.mean(centered * centered, axis=-1, keepdims=True)
    scale = lax.rsqrt(spread + epsilon)
    return centered * scale, scale


def norm_backward(grad, unit_values, scale):
    along = jnp.mean(grad * unit_values, axis=-1, keepdims=True)
    return scale * (grad - jnp.mean(grad, axis=-1, keepdims=True) - unit_values * along)


def whole_spec(shape):
    return pl.BlockSpec(shape, lambda step: (0,) * len(shape))


def lane_slices(width):
    return [slice(low, low + LANES) for low in range(0, width, LANES)]


def spread_rows(ref, index, lanes, rows):
    return jnp.broadcast_to(ref[index : index + 1, lanes], (rows, LANES))


def add_all(parts):
    while len(parts) > 1:
        parts = [
            parts[at] + parts[at + 1] if at + 1 < len(parts) else parts[at]
            for at in range(0, len(parts), 2)
        ]
    return parts[0]


def enter_body(count_ref, tokens_ref, gain_ref, retain_ref, low_ref, turned_ref, end_ref, state):
    step = pl.program_id(0)
    rows, steps, width = tokens_ref.shape
    states = retain_ref.shape[0]

    @pl.when(step == 0)
    def _():
        state[...] = jnp.zeros_like(state)

    values = tokens_ref[...].astype(jnp.float32)
    centered = values - jnp.mean(values, axis=-1, keepdims=True)
    spread = jnp.mean(centered * centered, axis=-1, keepdims=True)
    normed = centered * lax.rsqrt(spread + epsilon) * gain_ref[...]
    low_ref[...] = normed.astype(jnp.bfloat16)
    places = step * steps + lax.broadcasted_iota(jnp.int32, (steps, 1), 0)
    kept = jnp.stack([jnp.where(places < count_ref[row], normed[row], 0.0) for row in range(rows)])
    for lanes in lane_slices(width):
        for unit in range(steps // LAG):
            part = slice(unit * LAG, (unit + 1) * LAG)
            turned_ref[part, :, lanes] = jnp.swapaxes(kept[:, part, lanes], 0, 1)
    for lanes in lane_slices(width):
        retain = [spread_rows(retain_ref, j, lanes, rows) for j in range(states)]

        def unit_step(unit, hidden):
            for within in range(LAG):
                entry = turned_ref[unit * LAG + within, :, lanes]
                hidden = [retain[j] * hidden[j] + entry for j in range(states)]
            return hidden

        hidden = lax.fori_loop(
            0, steps // LAG, unit_step, [state[j, :, lanes] for j in range(states)]
        )
        for j in range(states):
            state[j, :, lanes] = hidden[j]

    @pl.when(step == pl.num_programs(0) - 1)
    def _():
        end_ref[...] = state[...]


def enter_call(counts, tokens, gain, retain):
    rows, length, width = tokens.shape
    states = retain.shape[0]
    natural = pl.BlockSpec((rows, STEPS, width), lambda step: (0, step, 0))
    return pl.pallas_call(
        enter_body,
        grid=(length // STEPS,),
        in_specs=[
            pl.BlockSpec(memory_space=pltpu.SMEM),
            natural,
            whole_spec((1, width)),
            whole_spec((states, width)),
        ],
        out_specs=(
            natural,
            pl.BlockSpec((STEPS, rows, width), lambda step: (step, 0, 0)),
            whole_spec((states, rows, width)),
        ),
        out_shape=(
            jax.ShapeDtypeStruct(tokens.shape, jnp.bfloat16),
            jax.ShapeDtypeStruct((length, rows, width), jnp.float32),
            jax.ShapeDtypeStruct((states, rows, width), jnp.float32),
        ),
        scratch_shapes=[pltpu.VMEM((states, rows, width), jnp.float32)],
        compiler_params=front_params,
        cost_estimate=work_cost(0.0, 9e-6),
        name="enter",
    )(counts, tokens, gain, retain)


def average_body(turned_ref, retain_ref, mix_ref, held_ref, state, out_ref):
    step = pl.program_id(0)
    steps, rows, width = turned_ref.shape
    states = retain_ref.shape[0]

    @pl.when(step == 0)
    def _():
        state[...] = held_ref[...]

    for lanes in lane_slices(width):
        retain = [spread_rows(retain_ref, j, lanes, rows) for j in range(states)]
        mix = [spread_rows(mix_ref, j, lanes, rows) for j in range(states)]

        def unit_step(unit, hidden):
            sums = []
            for within in range(LAG):
                entry = turned_ref[unit * LAG + within, :, lanes]
                hidden = [retain[j] * hidden[j] + entry for j in range(states)]
                sums.append(add_all([mix[j] * hidden[j] for j in range(states)]))
            out_ref[:, pl.ds(unit * LAG, LAG), lanes] = jnp.swapaxes(jnp.stack(sums), 0, 1)
            return hidden

        hidden = lax.fori_loop(
            0, steps // LAG, unit_step, [state[j, :, lanes] for j in range(states)]
        )
        for j in range(states):
            state[j, :, lanes] = hidden[j]


def average_call(turned, retain, mix, start):
    length, rows, width = turned.shape
    states = retain.shape[0]
    held = (states, rows, width)
    return pl.pallas_call(
        average_body,
        grid=(length // STEPS,),
        in_specs=[
            pl.BlockSpec((STEPS, rows, width), lambda step: (step, 0, 0)),
            whole_spec((states, width)),
            whole_spec((states, width)),
            whole_spec(held),
        ],
        out_specs=(
            whole_spec(held),
            pl.BlockSpec((rows, STEPS, width), lambda step: (0, step, 0)),
        ),
        out_shape=(
            jax.ShapeDtypeStruct(held, jnp.float32),
            jax.ShapeDtypeStruct((rows, length, width), jnp.float32),
        ),
        compiler_params=front_params,
        cost_estimate=work_cost(0.0, 12e-6),
        name="average",
    )(turned, retain, mix, start)


def return_body(grad_ref, retain_ref, turned_ref, end_ref, state):
    step = pl.program_id(0)
    rows, steps, width = grad_ref.shape
    states = retain_ref.shape[0]

    @pl.when(step == 0)
    def _():
        state[...] = jnp.zeros_like(state)

    for lanes in lane_slices(width):
        retain = [spread_rows(retain_ref, j, lanes, rows) for j in range(states)]

        def unit_step(unit, hidden):
            part = pl.ds((steps // LAG - 1 - unit) * LAG, LAG)
            turned = jnp.swapaxes(grad_ref[:, part, lanes], 0, 1)
            turned_ref[part, :, lanes] = turned
            for within in reversed(range(LAG)):
                hidden = [retain[j] * hidden[j] + turned[within] for j in range(states)]
            return hidden

        hidden = lax.fori_loop(
            0, steps // LAG, unit_step, [state[j, :, lanes] for j in range(states)]
        )
        for j in range(states):
            state[j, :, lanes] = hidden[j]

    @pl.when(step == pl.num_programs(0) - 1)
    def _():
        end_ref[...] = state[...]


def return_call(grad, retain):
    rows, length, width = grad.shape
    states = retain.shape[0]
    last = length // STEPS - 1
    return pl.pallas_call(
        return_body,
        grid=(length // STEPS,),
        in_specs=[
            pl.BlockSpec((rows, STEPS, width), lambda step: (0, last - step, 0)),
            whole_spec((states, width)),
        ],
        out_specs=(
            pl.BlockSpec((STEPS, rows, width), lambda step: (last - step, 0, 0)),
            whole_spec((states, rows, width)),
        ),
        out_shape=(
            jax.ShapeDtypeStruct((length, rows, width), jnp.float32),
            jax.ShapeDtypeStruct((states, rows, width), jnp.float32),
        ),
        scratch_shapes=[pltpu.VMEM((states, rows, width), jnp.float32)],
        compiler_params=scan_params,
        cost_estimate=work_cost(0.0, 8e-6),
        name="back_enter",
    )(grad, retain)


def sums_body(
    grad_ref,
    turned_ref,
    retain_ref,
    inverse_ref,
    unit_ref,
    held_ref,
    lag_in_ref,
    carry_ref,
    lag_ref,
):
    step = pl.program_id(0)
    steps, rows, width = grad_ref.shape
    states = retain_ref.shape[0]
    half = states // 2
    units = steps // LAG

    @pl.when(step == 0)
    def _():
        carry_ref[...] = held_ref[...]
        lag_ref[...] = lag_in_ref[...]

    for lanes in lane_slices(width):
        for first in range(0, states, half):
            chosen = range(first, first + half)
            retain = [spread_rows(retain_ref, j, lanes, rows) for j in chosen]
            inverse = [spread_rows(inverse_ref, j, lanes, rows) for j in chosen]

            def unit_step(unit, carried):
                after, hidden, cross = carried
                unit = units - 1 - unit
                later = after
                for within in reversed(range(LAG)):
                    place = unit * LAG + within
                    entry = turned_ref[place, :, lanes]
                    grad = grad_ref[place, :, lanes]
                    after = [retain[m] * after[m] + grad for m in range(half)]
                    hidden = [(hidden[m] - entry) * inverse[m] for m in range(half)]
                    cross = [cross[m] + after[m] * hidden[m] for m in range(half)]
                for m, j in enumerate(chosen):
                    unit_decay = spread_rows(unit_ref, j, lanes, rows)
                    carry_ref[3, j, :, lanes] += hidden[m] * (after[m] - unit_decay * later[m])
                return after, hidden, cross

            results = lax.fori_loop(
                0,
                units,
                unit_step,
                tuple([carry_ref[kind, j, :, lanes] for j in chosen] for kind in range(3)),
            )
            for kind in range(3):
                for m, j in enumerate(chosen):
                    carry_ref[kind, j, :, lanes] = results[kind][m]

        def lag_step(unit, lags):
            entries = [turned_ref[unit * LAG + at, :, lanes] for at in range(LAG)]
            grads = [grad_ref[unit * LAG + at, :, lanes] for at in range(LAG)]
            return [
                lags[lag] + add_all([grads[at] * entries[at - lag] for at in range(lag, LAG)])
                for lag in range(LAG)
            ]

        lags = lax.fori_loop(0, units, lag_step, [lag_ref[at, :, lanes] for at in range(LAG)])
        for at in range(LAG):
            lag_ref[at, :, lanes] = lags[at]


def sums_call(low_end, high_end, grad, turned, params, carried):
    rows, width = grad.shape[1:]
    states = params[0].shape[0]
    last = high_end // STEPS - 1
    turned_spec = pl.BlockSpec((STEPS, rows, width), lambda step: (last - step, 0, 0))
    carried_specs = [whole_spec(value.shape) for value in carried]
    return pl.pallas_call(
        sums_body,
        grid=((high_end - low_end) // STEPS,),
        in_specs=[turned_spec] * 2 + [whole_spec((states, width))] * 3 + carried_specs,
        out_specs=carried_specs,
        out_shape=[jax.ShapeDtypeStruct(value.shape, jnp.float32) for value in carried],
        compiler_params=scan_params,
        cost_estimate=work_cost(0.0, 8e-6),
        name="adjoint_sums",
    )(grad, turned, *params, *carried)


def leave_body(
    count_ref,
    tokens_ref,
    gain_ref,
    part_ref,
    residual_ref,
    grad_ref,
    retain_ref,
    mix_ref,
    held_ref,
    *others,
    places_before,
):
    carry_ref, out_ref, path = others[-3:]
    step = pl.program_id(0)
    steps, rows, width = grad_ref.shape
    states = retain_ref.shape[0]
    units = steps // LAG

    @pl.when(step == 0)
    def _():
        carry_ref[...] = held_ref[...]

    for lanes in lane_slices(width):
        retain = [spread_rows(retain_ref, j, lanes, rows) for j in range(states)]
        mix = [spread_rows(mix_ref, j, lanes, rows) for j in range(states)]

        def unit_step(unit, after):
            unit = units - 1 - unit
            sums = []
            for within in reversed(range(LAG)):
                grad = grad_ref[unit * LAG + within, :, lanes]
                after = [retain[j] * after[j] + grad for j in range(states)]
                sums.append(add_all([mix[j] * after[j] for j in range(states)]))
            path[:, pl.ds(unit * LAG, LAG), lanes] = jnp.swapaxes(jnp.stack(sums[::-1]), 0, 1)
            return after

        after = lax.fori_loop(
            0, units, unit_step, [carry_ref[j, :, lanes] for j in range(states)]
        )
        for j in range(states):
            carry_ref[j, :, lanes] = after[j]

    first_place = places_before + (pl.num_programs(0) - 1 - step) * steps
    places = first_place + lax.broadcasted_iota(jnp.int32, (steps, 1), 0)
    gain = gain_ref[...]
    for row in range(rows):
        unit_values, scale = unit_norm(tokens_ref[row].astype(jnp.float32))
        grad = part_ref[row].astype(jnp.float32)
        grad = grad + jnp.where(places < count_ref[row], path[row], 0.0)
        out = norm_backward(grad * gain, unit_values, scale)
        out_ref[row] = (out + residual_ref[row].astype(jnp.float32)).astype(jnp.bfloat16)


def leave_call(
    low_end, high_end, counts, tokens, gain, part, residual, grad, retain, mix, carried
):
    rows, length, width = tokens.shape
    held = carried[0].shape
    last = high_end // STEPS - 1
    going_on = len(carried) > 1
    natural = pl.BlockSpec((rows, STEPS, width), lambda step: (0, last - step, 0))
    return pl.pallas_call(
        functools.partial(leave_body, places_before=low_end),
        grid=((high_end - low_end) // STEPS,),
        in_specs=[
            pl.BlockSpec(memory_space=pltpu.SMEM),
            natural,
            whole_spec((1, width)),
            natural,
            natural,
            pl.BlockSpec((STEPS, rows, width), lambda step: (last - step, 0, 0)),
            whole_spec(retain.shape),
            whole_spec(mix.shape),
            whole_spec(held),
        ]
        + [pl.BlockSpec(memory_space=pl.ANY)] * going_on,
        out_specs=[whole_spec(held), natural],
        out_shape=[
            jax.ShapeDtypeStruct(held, jnp.float32),
            jax.ShapeDtypeStruct((rows, length, width), jnp.bfloat16),
        ],
        input_output_aliases={9: 1} if going_on else {},
        scratch_shapes=[pltpu.VMEM((rows, STEPS, width), jnp.float32)],
        compiler_params=scan_params,
        cost_estimate=work_cost(0.0, 8e-6),
        name="leave",
    )(counts, tokens, gain, part, residual, grad, retain, mix, *carried)


class Exchange:
    def __init__(self, local, decay, axis, backward):
        self.axis, self.backward = axis, backward
        self.count = lax.axis_size(axis)
        place = lax.axis_index(axis)
        self.place = self.count - 1 - place if backward else place
        self.low = self.place % 2
        self.half = local.shape[-1] // 2
        self.local = local
        self.decay = self.part(decay, self.low)

    def part(self, value, which):
        return lax.dynamic_slice_in_dim(value, which * self.half, self.half, value.ndim - 1)

    def moved(self, value, pairs):
        last = self.count - 1
        if self.backward:
            pairs = [(last - source, last - target) for source, target in pairs]
        return lax.ppermute(value, self.axis, pairs)

    def swapped(self, value):
        return self.moved(value, [(at, at ^ 1) for at in range(self.count)])

    def later(self, value, hop):
        return self.moved(value, [(at, at + 2 * hop) for at in range(self.count - 2 * hop)])

    def share(self):
        own = self.part(self.local, self.low)
        other = self.swapped(self.part(self.local, 1 - self.low))
        self.first = jnp.where(self.low == 0, own, other)
        self.pair = self.decay * self.first + jnp.where(self.low == 0, other, own)

    def cross(self):
        pairs = self.count // 2
        decay = self.decay * self.decay
        if pairs <= 4:
            arrived = [self.later(self.pair, hop) for hop in range(1, pairs)]
            total = arrived[-1]
            for value in arrived[-2::-1]:
                total = decay * total + value
        else:
            total, hop = self.later(self.pair, 1), 1
            while hop < pairs - 1:
                total = total + decay * self.later(total, hop)
                decay = decay * decay
                hop *= 2
        self.start = total

    def give(self):
        second = self.decay * self.start + self.first
        kept = jnp.where(self.low == 0, self.start, second)
        got = self.swapped(jnp.where(self.low == 0, second, self.start))
        return jnp.concatenate(
            [jnp.where(self.low == 0, kept, got), jnp.where(self.low == 0, got, kept)], axis=-1
        )


mesh_axes = ("seq", "row")


def device_total():
    return lax.axis_size("seq") * lax.axis_size("row")


def device_place():
    return lax.axis_index("seq") * lax.axis_size("row") + lax.axis_index("row")


def swapped(value, bit):
    return lax.ppermute(value, mesh_axes, [(at, at ^ bit) for at in range(device_total())])


def half_summed(value, bit):
    half = value.shape[0] // 2
    mine = (device_place() // bit) % 2
    sent = lax.dynamic_slice_in_dim(value, (1 - mine) * half, half, 0)
    kept = lax.dynamic_slice_in_dim(value, mine * half, half, 0)
    return kept + swapped(sent, bit)


def both_halves(value, bit):
    mine = (device_place() // bit) % 2 == 1
    other = swapped(value, bit)
    return jnp.concatenate([jnp.where(mine, other, value), jnp.where(mine, value, other)], axis=0)


def link_orders():
    total = device_total()
    bits = [1 << at for at in range(total.bit_length() - 1)]
    if (lax.axis_size("seq"), lax.axis_size("row")) == (8, 4):
        core, x, y, z_low, z_high = bits
        return (
            (core, x, y, z_low, z_high),
            (core, y, z_low, x, z_high),
            (core, z_low, x, y, z_high),
        )
    third = len(bits) // 3
    return tuple(bits[turn * third :] + bits[: turn * third] for turn in range(3))


def summed_everywhere(values):
    orders = link_orders()
    for at in range(len(orders[0])):
        values = [half_summed(v, orders[n % 3][at]) for n, v in enumerate(values)]
    for at in reversed(range(len(orders[0]))):
        values = [both_halves(v, orders[n % 3][at]) for n, v in enumerate(values)]
    return values


def paired_sum(value, group):
    partners = [group[0]] if len(group) == 1 else [group[0], group[1], group[0] + group[1]]
    arrived = [swapped(value, partner) for partner in partners]
    if len(arrived) == 1:
        return value + arrived[0]
    return (value + arrived[0]) + (arrived[1] + arrived[2])


def small_sum(value):
    bits = [1 << at for at in range(device_total().bit_length() - 1)]
    for at in range(0, len(bits), 2):
        value = paired_sum(value, bits[at : at + 2])
    return value


def power_of(value, exponent):
    result = None
    while exponent:
        if exponent & 1:
            result = value if result is None else result * value
        value = value * value
        exponent >>= 1
    return result


def dot(first_op, second_op):
    return jnp.dot(first_op, second_op, preferred_element_type=jnp.float32)


def dot_back(first_op, second_op):
    return lax.dot_general(
        first_op, second_op, (((1,), (1,)), ((), ())), preferred_element_type=jnp.float32
    )


def dot_outer(first_op, second_op):
    return lax.dot_general(
        first_op, second_op, (((0,), (0,)), ((), ())), preferred_element_type=jnp.float32
    )


def low(value):
    return value.astype(jnp.bfloat16)


def chunks(low_end, high_end, size):
    return [slice(at, min(at + size, high_end)) for at in range(low_end, high_end, size)]


def gated(value):
    half = 0.5 * value
    turn = jnp.tanh(half)
    gate = 0.5 * turn + 0.5
    act = half * turn + half
    return act, gate + act * (1.0 - gate)


def value_body(normed_ref, value_weight_ref, value_ref, value_slope_ref):
    for part in chunks(0, value_ref.shape[1], 256):
        value, slope = gated(low(dot(normed_ref[...], value_weight_ref[:, part])))
        value_ref[:, part] = low(value)
        value_slope_ref[:, part] = low(slope)


def value_call(normed, value_weight):
    rows, length, width = normed.shape
    vdim = value_weight.shape[1]
    return pl.pallas_call(
        value_body,
        grid=(rows,),
        in_specs=[row_spec(length, width), once_spec(value_weight.shape)],
        out_specs=[row_spec(length, vdim)] * 2,
        out_shape=[jax.ShapeDtypeStruct((rows, length, vdim), jnp.bfloat16)] * 2,
        compiler_params=front_params,
        cost_estimate=work_cost(2e9, 5e-6),
        name="value",
    )(normed, value_weight)


def forward_body(
    count_ref,
    tokens_ref,
    cotangent_ref,
    average_ref,
    normed_ref,
    value_ref,
    value_slope_ref,
    omega_ref,
    base_weight_ref,
    gains_ref,
    biases_ref,
    output_weight_ref,
    ffn_gain_ref,
    ffn_in_ref,
    ffn_out_ref,
    out_ref,
    mixed_ref,
    mixed_slope_ref,
    product_ref,
    ffn_low_ref,
    act_ref,
    grad_inner_ref,
    grad_proj_ref,
    grad_main_ref,
    grad_shared_ref,
    grad_vpre_ref,
    residual_ref,
    ffn_gain_grad_ref,
    grad_gains_ref,
    reset_ref,
    reset_slope_ref,
    grad_attended_ref,
    probs_ref,
    query_ref,
    key_ref,
    shared_ref,
    shared_slope_ref,
):
    row = pl.program_id(0)
    length, width = tokens_ref.shape
    zdim = query_ref.shape[1]
    vdim = value_ref.shape[1]
    inner = act_ref.shape[1]

    @pl.when(row == 0)
    def _():
        ffn_gain_grad_ref[...] = jnp.zeros_like(ffn_gain_grad_ref)
        grad_gains_ref[...] = jnp.zeros_like(grad_gains_ref)

    normed = normed_ref[...]
    sums = average_ref[...] + omega_ref[...] * normed.astype(jnp.float32)
    gate = sigmoid(sums)
    mixed = sums * gate
    mixed_ref[...] = low(mixed)
    mixed_slope_ref[...] = low(gate + mixed * (1.0 - gate))
    mixed_low = mixed_ref[...]

    shared = dot(mixed_low, base_weight_ref[:, :zdim])
    gate = sigmoid(shared)
    shared_act = shared * gate
    shared_ref[...] = shared_act
    shared_slope_ref[...] = gate + shared_act * (1.0 - gate)
    query_ref[...] = low(shared_act * gains_ref[0:1] + biases_ref[0:1])
    key_ref[...] = low(shared_act * gains_ref[1:2] + biases_ref[1:2])

    to_place = lax.broadcasted_iota(jnp.int32, (GROUP, GROUP), 0)
    from_place = lax.broadcasted_iota(jnp.int32, (GROUP, GROUP), 1)
    for block in chunks(0, length, GROUP):
        allowed = (from_place <= to_place) & (
            (from_place < count_ref[row] - block.start) | (from_place == to_place)
        )
        scores = dot_back(query_ref[block], key_ref[block]) * zdim**-0.5
        scores = jnp.where(allowed, scores, very_low)
        weights = jnp.exp(scores - jnp.max(scores, axis=-1, keepdims=True))
        weights = jnp.where(allowed, weights, 0.0)
        probs_ref[block] = weights / jnp.sum(weights, axis=-1, keepdims=True)

    for part in chunks(0, vdim, 256):
        base_part = slice(zdim + part.start, zdim + part.stop)
        reset_act, reset_slope = gated(low(dot(mixed_low, base_weight_ref[:, base_part])))
        reset_ref[:, part] = low(reset_act)
        for block in chunks(0, length, GROUP):
            attended = low(dot(low(probs_ref[block]), value_ref[block, part]))
            product_ref[block, part] = low(attended * reset_act[block])
            reset_slope_ref[block, part] = low(attended * reset_slope[block])

    update_gate = sigmoid(dot(mixed_low, base_weight_ref[:, zdim + vdim : zdim + vdim + width]))
    candidate = dot(mixed_low, base_weight_ref[:, zdim + vdim + width :])
    candidate = candidate + dot(product_ref[...], output_weight_ref[...])
    candidate_gate = sigmoid(candidate)
    candidate_act = candidate * candidate_gate
    candidate_slope = candidate_gate + candidate_act * (1.0 - candidate_gate)
    tokens = tokens_ref[...].astype(jnp.float32)
    change = candidate_act - tokens
    after = tokens + update_gate * change
    unit_values, scale = unit_norm(after)
    ffn_low_ref[...] = low(unit_values * ffn_gain_ref[...])
    ffn_low = ffn_low_ref[...]
    cotangent = cotangent_ref[...]

    out = after
    grad_normed = jnp.zeros_like(after)
    for part in chunks(0, inner, 256):
        act, slope = gated(low(dot(ffn_low, ffn_in_ref[:, part])))
        act_ref[:, part] = low(act)
        grad_act = low(dot_back(cotangent, ffn_out_ref[part]))
        grad_inner_ref[:, part] = low(grad_act * slope)
    out = after + dot(act_ref[...], ffn_out_ref[...])
    out_ref[...] = low(out)
    grad_normed = dot_back(grad_inner_ref[...], ffn_in_ref[...])
    ffn_gain_grad_ref[...] += jnp.sum(grad_normed * unit_values, axis=0, keepdims=True)
    grad_after = cotangent.astype(jnp.float32) + norm_backward(
        grad_normed * ffn_gain_ref[...], unit_values, scale
    )
    grad_change = grad_after * update_gate
    grad_proj = low(grad_change * candidate_slope)
    grad_proj_ref[...] = grad_proj
    grad_main_ref[:, vdim : vdim + width] = low(grad_change * change * (1.0 - update_gate))
    grad_main_ref[:, vdim + width :] = grad_proj
    for part in chunks(0, vdim, 256):
        grad_product = low(dot_back(grad_proj, output_weight_ref[part]))
        grad_attended_ref[:, part] = low(grad_product * reset_ref[:, part])
        grad_main_ref[:, part] = low(grad_product * reset_slope_ref[:, part])

    grad_gains = jnp.zeros(grad_gains_ref.shape, jnp.float32)
    for block in chunks(0, length, GROUP):
        probs = probs_ref[block]
        probs_low = low(probs)
        grad_probs = dot_back(grad_attended_ref[block], value_ref[block])
        for part in chunks(0, vdim, 512):
            grad_value = dot_outer(probs_low, grad_attended_ref[block, part])
            grad_vpre_ref[block, part] = low(low(grad_value) * value_slope_ref[block, part])
        total = jnp.sum(grad_probs * probs, axis=-1, keepdims=True)
        grad_raw = low(probs * (grad_probs - total) * zdim**-0.5)
        grad_query = dot(grad_raw, key_ref[block])
        grad_key = dot_outer(grad_raw, query_ref[block])
        shared = shared_ref[block]
        grad_gains = grad_gains + jnp.concatenate(
            [
                jnp.sum(value, axis=0, keepdims=True)
                for value in (grad_query * shared, grad_key * shared, grad_query, grad_key)
            ],
            axis=0,
        )
        grad_shared = grad_query * gains_ref[0:1] + grad_key * gains_ref[1:2]
        grad_shared_ref[block] = low(grad_shared * shared_slope_ref[block])
    grad_gains_ref[...] += grad_gains
    residual_ref[...] = low(grad_after - grad_change)


def row_spec(length, width):
    return pl.BlockSpec((None, length, width), lambda row: (row, 0, 0))


def once_spec(shape):
    return pl.BlockSpec(shape, lambda row: (0,) * len(shape), pipeline_mode=pl.Buffered(1))


def forward_call(
    counts,
    tokens,
    cotangent,
    average,
    normed,
    value,
    value_slope,
    omega,
    base_weight,
    gains,
    biases,
    output_weight,
    ffn_gain,
    ffn_in,
    ffn_out,
):
    rows, length, width = tokens.shape
    zdim, vdim, inner = gains.shape[1], value.shape[2], ffn_in.shape[1]
    half, full = jnp.bfloat16, jnp.float32
    outs = [
        (width, half),
        (width, half),
        (width, half),
        (vdim, half),
        (width, half),
        (inner, half),
        (inner, half),
        (width, half),
        (vdim + 2 * width, half),
        (zdim, half),
        (vdim, half),
        (width, half),
    ]
    tied = [
        omega,
        base_weight,
        gains,
        biases,
        output_weight,
        ffn_gain,
        ffn_in,
        ffn_out,
    ]
    return pl.pallas_call(
        forward_body,
        grid=(rows,),
        in_specs=[pl.BlockSpec(memory_space=pltpu.SMEM)]
        + [row_spec(length, width)] * 4
        + [row_spec(length, vdim)] * 2
        + [once_spec(weight.shape) for weight in tied],
        out_specs=[row_spec(length, size) for size, _ in outs]
        + [whole_spec((1, width)), whole_spec((4, zdim))],
        out_shape=[jax.ShapeDtypeStruct((rows, length, size), kind) for size, kind in outs]
        + [jax.ShapeDtypeStruct((1, width), full), jax.ShapeDtypeStruct((4, zdim), full)],
        scratch_shapes=[pltpu.VMEM((length, vdim), half)] * 3
        + [pltpu.VMEM((length, GROUP), full)]
        + [pltpu.VMEM((length, zdim), half)] * 2
        + [pltpu.VMEM((length, zdim), full)] * 2,
        compiler_params=front_params,
        cost_estimate=work_cost(18e9, 40e-6),
        name="dense_forward",
    )(counts, tokens, cotangent, average, normed, value, value_slope, *tied)


def backward_body(
    grad_main_ref,
    grad_shared_ref,
    grad_vpre_ref,
    normed_ref,
    mixed_slope_ref,
    omega_ref,
    value_weight_ref,
    base_weight_ref,
    grad_average_ref,
    part_ref,
    grad_omega_ref,
    grad_gain_ref,
):
    zdim = grad_shared_ref.shape[1]

    @pl.when(pl.program_id(0) == 0)
    def _():
        grad_omega_ref[...] = jnp.zeros_like(grad_omega_ref)
        grad_gain_ref[...] = jnp.zeros_like(grad_gain_ref)

    grad_average = dot_back(grad_main_ref[...], base_weight_ref[:, zdim:])
    grad_average = grad_average + dot_back(grad_shared_ref[...], base_weight_ref[:, :zdim])
    grad_average = grad_average * mixed_slope_ref[...].astype(jnp.float32)
    grad_average_ref[...] = grad_average
    part = dot_back(grad_vpre_ref[...], value_weight_ref[...]) + grad_average * omega_ref[...]
    part_ref[...] = part
    normed = normed_ref[...].astype(jnp.float32)
    grad_omega_ref[...] += jnp.sum(grad_average * normed, axis=0, keepdims=True)
    grad_gain_ref[...] += jnp.sum(part * normed, axis=0, keepdims=True)


def backward_call(inputs, tied_inputs):
    rows, length, _ = inputs[0].shape
    width = tied_inputs[0].shape[1]
    return pl.pallas_call(
        backward_body,
        grid=(rows,),
        in_specs=[row_spec(length, value.shape[2]) for value in inputs]
        + [once_spec(value.shape) for value in tied_inputs],
        out_specs=[row_spec(length, width)] * 2 + [whole_spec((1, width))] * 2,
        out_shape=[jax.ShapeDtypeStruct((rows, length, width), jnp.float32)] * 2
        + [jax.ShapeDtypeStruct((1, width), jnp.float32)] * 2,
        compiler_params=dense_params,
        cost_estimate=work_cost(7e9, 12e-6),
        name="dense_backward",
    )(*inputs, *tied_inputs)


def joined_body(*refs, widths, split):
    refs = refs[1:] if split else refs
    outs_per_chain = 2 if split else 1
    outs = refs[len(refs) - outs_per_chain * len(widths) :]
    at = 0
    for chain, parts in enumerate(widths):
        for side in range(outs_per_chain):
            column = 0
            for width in parts:
                total = refs[at][...] + refs[at + 1][...]
                outs[chain * outs_per_chain + side][:, column : column + width] = total
                column += width
                at += 2


def joined(chains):
    split = chains[0][2] is not None
    sides = 2 if split else 1
    widths = [[value.shape[1] for value in kept] for kept, _, _ in chains]
    sizes = [kept[0].shape[0] // sides for kept, _, _ in chains]
    steps = 4
    while any(size % (8 * steps) for size in sizes):
        steps //= 2
    operands, in_specs, out_specs, out_shape = [], [], [], []
    for chain, (kept, arrived, _) in enumerate(chains):
        block = sizes[chain] // steps
        for side in range(sides):

            def place(step, *held, chain=chain, side=side):
                if not held:
                    return step, 0
                mine = held[0][chain]
                return (1 - mine if side else mine) * steps + step, 0

            for pair in zip(kept, arrived):
                for value in pair:
                    operands.append(value)
                    in_specs.append(pl.BlockSpec((block, value.shape[1]), place))
            total = sum(widths[chain])
            out_specs.append(pl.BlockSpec((block, total), lambda step, *held: (step, 0)))
            out_shape.append(jax.ShapeDtypeStruct((sizes[chain], total), jnp.float32))
    if split:
        mine = [(device_place() // bit) % 2 for _, _, bit in chains]
        operands.insert(0, jnp.stack(mine).astype(jnp.int32))
    outs = pl.pallas_call(
        functools.partial(joined_body, widths=widths, split=split),
        grid_spec=pltpu.PrefetchScalarGridSpec(
            num_scalar_prefetch=1 if split else 0,
            grid=(steps,),
            in_specs=in_specs,
            out_specs=out_specs,
        ),
        out_shape=out_shape,
        compiler_params=scan_params,
        cost_estimate=work_cost(0.0, 2e-6),
        name="joined",
    )(*operands)
    return [tuple(outs[at : at + sides]) for at in range(0, len(outs), sides)]


def placed_body(*refs, copies, sources):
    mine, refs = refs[0], refs[1:]
    half = pl.program_id(0)
    for own, arrived, which, taken, result, column in copies:
        there = slice(column, column + taken.stop - taken.start)

        @pl.when(half == mine[which])
        def _(own=own, taken=taken, result=result, there=there):
            refs[sources + result][:, there] = refs[own][:, taken]

        @pl.when(half != mine[which])
        def _(arrived=arrived, taken=taken, result=result, there=there):
            refs[sources + result][:, there] = refs[arrived][:, taken]


def placed(values, bits, copies, shapes):
    steps = 4
    while any(value.shape[0] % (8 * steps) for value in values):
        steps //= 2
    in_specs = []
    for at, value in enumerate(values):

        def place(half, step, mine, which=at // 2, other=at % 2):
            wanted = (half == mine[which]) != bool(other)
            return jnp.where(wanted, step, jnp.where(half == 0, 0, steps - 1)), 0

        in_specs.append(pl.BlockSpec((value.shape[0] // steps, value.shape[1]), place))
    mine = jnp.stack([(device_place() // bit) % 2 for bit in bits]).astype(jnp.int32)
    return pl.pallas_call(
        functools.partial(placed_body, copies=copies, sources=len(values)),
        grid_spec=pltpu.PrefetchScalarGridSpec(
            num_scalar_prefetch=1,
            grid=(2, steps),
            in_specs=in_specs,
            out_specs=[
                pl.BlockSpec(
                    (shape[0] // (2 * steps), shape[1]),
                    lambda half, step, mine: (half * steps + step, 0),
                )
                for shape in shapes
            ],
        ),
        out_shape=[jax.ShapeDtypeStruct(shape, jnp.float32) for shape in shapes],
        compiler_params=scan_params,
        cost_estimate=work_cost(0.0, 2e-6),
        name="placed",
    )(mine, *values)


def gathered_body(*refs, bits, copies, results, others, per_row):
    sources = refs[: 2 * len(bits)]
    outs = refs[len(refs) - results - len(sources) - 2 : len(refs) - len(sources) - 2]
    held, (in_sems, out_sems) = refs[len(refs) - len(sources) - 2 : -2], refs[-2:]
    place = lax.axis_index("seq") * per_row + lax.axis_index("row")
    arriving = []
    for at, source in enumerate(sources):
        copy = pltpu.make_async_copy(source, held[at], in_sems.at[at])
        copy.start()
        arriving.append(copy)
    leaving = []
    for at, source in enumerate(sources):
        high_bit, low_bit = bits[at // 2]
        high = (place // high_bit) % 2
        low_side = (place // low_bit) % 2
        if others:
            high = 1 - high
        if at % 2:
            low_side = 1 - low_side
        rows = source.shape[0]
        there = pl.ds(pl.multiple_of((2 * high + low_side) * rows, 8), rows)
        arriving[at].wait()
        for chain, taken, result, column in copies:
            if chain == at // 2:
                copy = pltpu.make_async_copy(
                    held[at].at[:, taken],
                    outs[result].at[there, column : column + taken.stop - taken.start],
                    out_sems.at[len(leaving)],
                )
                copy.start()
                leaving.append(copy)
    for copy in leaving:
        copy.wait()


def gathered(chains, copies, shapes, before=None):
    values = []
    for one in chains:
        values += one.held if before is None else one.arrived
    anywhere = pl.BlockSpec(memory_space=pl.ANY)
    aliases = {}
    if before is not None:
        aliases = {len(values) + at: at for at in range(len(shapes))}
    return pl.pallas_call(
        functools.partial(
            gathered_body,
            bits=[one.order[:2] for one in chains],
            copies=copies,
            results=len(shapes),
            others=before is not None,
            per_row=lax.axis_size("row"),
        ),
        in_specs=[anywhere] * (len(values) + len(aliases)),
        out_specs=[anywhere] * len(shapes),
        out_shape=[jax.ShapeDtypeStruct(shape, jnp.float32) for shape in shapes],
        input_output_aliases=aliases,
        scratch_shapes=[pltpu.VMEM(value.shape, jnp.float32) for value in values]
        + [
            pltpu.SemaphoreType.DMA((len(values),)),
            pltpu.SemaphoreType.DMA((2 * len(copies),)),
        ],
        compiler_params=scan_params,
        cost_estimate=work_cost(0.0, 6e-6),
        name="gathered",
    )(*values, *(before or ()))


class Chain:
    def __init__(self, order, sent, kept):
        self.order, self.at = order, 0
        self.sent, self.kept, self.arrived = list(sent), list(kept), []

    def state(self):
        return self.sent, self.kept, self.arrived

    def set_state(self, state):
        self.sent, self.kept, self.arrived = state

    def send(self):
        total = len(self.order)
        bit = self.order[self.at if self.at < total else 2 * total - 1 - self.at]
        self.arrived = [swapped(value, bit) for value in self.sent]

    def give(self):
        self.held = self.sent + self.arrived
        self.arrived = [swapped(value, self.order[0]) for value in self.held]

    def pieces(self):
        return self.held + self.arrived


def join(*chains):
    total = len(chains[0].order)
    if chains[0].at < total:
        last = chains[0].at == total - 1
        results = joined(
            [
                (one.kept, one.arrived, None if last else one.order[one.at + 1])
                for one in chains
            ]
        )
        for one, result in zip(chains, results):
            if last:
                one.sent, one.kept = [result[0]], []
            else:
                one.sent, one.kept = [result[1]], [result[0]]
    else:
        values, copies, shapes = [], [], []
        for at, one in enumerate(chains):
            rows, columns = one.sent[0].shape
            values += [one.sent[0], one.arrived[0]]
            copies.append((2 * at, 2 * at + 1, at, slice(0, columns), at, 0))
            shapes.append((2 * rows, columns))
        bits = [one.order[2 * total - 1 - one.at] for one in chains]
        for one, result in zip(chains, placed(values, bits, copies, shapes)):
            one.sent = [result]
    for one in chains:
        one.arrived = []
        one.at += 1


def tied(value, *chains):
    value, states = lax.optimization_barrier((value, [one.state() for one in chains]))
    for one, state in zip(chains, states):
        one.set_state(state)
    return value


def weight_halves(first_op, second_op, bit):
    first_op = first_op.reshape(-1, first_op.shape[-1])
    second_op = second_op.reshape(-1, second_op.shape[-1])
    half = first_op.shape[1] // 2
    mine = (device_place() // bit) % 2
    return [
        dot_outer(lax.dynamic_slice_in_dim(first_op, which * half, half, 1), second_op)
        for which in (1 - mine, mine)
    ]


def weight_grad(first_op, second_op):
    return dot_outer(
        first_op.reshape(-1, first_op.shape[-1]), second_op.reshape(-1, second_op.shape[-1])
    )


def per_device(
    tokens,
    valid_count,
    norm_gain,
    value_weight,
    ema_forget,
    ema_beta,
    ema_eta,
    ema_omega,
    base_weight,
    qk_gain,
    qk_bias,
    output_weight,
    ffn_gain,
    ffn_in,
    ffn_out,
    cotangent,
):
    length, width = tokens.shape[1:]
    counts = valid_count - lax.axis_index("seq") * length
    norm_gain = norm_gain.astype(jnp.float32)[None]
    ffn_gain = ffn_gain.astype(jnp.float32)[None]
    omega = ema_omega[None]
    gains, biases = qk_gain.astype(jnp.float32), qk_bias.astype(jnp.float32)
    forget, beta, eta = ema_forget.T, ema_beta.T, ema_eta.T
    retain = 1.0 - forget
    gate = jnp.sqrt(forget * (2.0 - forget))
    inflow = beta * gate
    mix = eta * inflow
    span_decay = power_of(retain, length)[:, None, :]

    normed, turned, device_end = enter_call(counts, tokens, norm_gain, retain)
    ahead = Exchange(device_end, span_decay, "seq", False)
    ahead.share()
    ahead.cross()
    value, value_slope = value_call(normed, value_weight)
    ahead.start, value, value_slope = lax.optimization_barrier((ahead.start, value, value_slope))
    incoming = ahead.give()
    state_end, average = average_call(turned, retain, mix, incoming)
    unit_decay = power_of(retain, LAG)
    (
        block_out,
        mixed,
        mixed_slope,
        product,
        ffn_low,
        act,
        grad_inner,
        grad_proj,
        grad_main,
        grad_shared,
        grad_vpre,
        residual,
        grad_ffn_gain,
        grad_query_key,
    ) = forward_call(
        counts,
        tokens,
        cotangent,
        average,
        normed,
        value,
        value_slope,
        omega,
        base_weight,
        gains,
        biases,
        output_weight,
        ffn_gain,
        ffn_in,
        ffn_out,
    )
    orders = link_orders()
    core = orders[0][0]
    chained = device_total() == 32
    chains = []
    back_inputs = [grad_main, grad_shared, grad_vpre, normed, mixed_slope]
    if chained:
        products = [
            [(act, cotangent), (product, grad_proj)],
            [(mixed, grad_main)],
            [(ffn_low, grad_inner), (normed, grad_vpre), (mixed, grad_shared)],
        ]
        halves = [[weight_halves(*pair, core) for pair in pairs] for pairs in products]
        for order, pairs in zip(orders, halves):
            chains.append(Chain(order, [pair[0] for pair in pairs], [pair[1] for pair in pairs]))
            chains[-1].send()
        join(*chains)
        back_inputs = tied(back_inputs, *chains)
        for one in chains:
            one.send()
    grad_average, part, grad_omega, grad_gain = backward_call(
        back_inputs, [omega, value_weight, base_weight]
    )

    def halve(value):
        if chained:
            value = tied(value, *chains)
            join(*chains)
            value = tied(value, *chains)
            for one in chains:
                one.send()
        return value

    grad_turned, device_start = return_call(grad_average, retain)
    behind = Exchange(device_start, span_decay, "seq", True)
    behind.share()
    behind.pair = halve(behind.pair)
    behind.cross()
    behind.start = halve(behind.start)
    later = behind.give()
    states = retain.shape[0]
    carried = [
        jnp.stack([later, state_end, jnp.zeros_like(later), jnp.zeros_like(later)]),
        jnp.zeros((LAG,) + later.shape[1:], jnp.float32),
    ]
    parts = length // STEPS
    inverse = 1.0 / retain
    ends = [at * STEPS // 8 for at in (8 * parts, 5 * parts, 2 * parts, 0)]
    ends = [at // STEPS * STEPS for at in ends]
    for high_end, low_end in zip(ends, ends[1:]):
        carried = halve(carried)
        carried = sums_call(
            low_end, high_end, grad_turned, turned, [retain, inverse, unit_decay], carried
        )
    carry, lags = carried
    ends = [at * STEPS for at in (parts, 5 * parts // 8, 0)]
    left = [later]
    for high_end, low_end in zip(ends, ends[1:]):
        left, carry, lags = halve((left, carry, lags))
        left = leave_call(
            low_end,
            high_end,
            counts,
            tokens,
            norm_gain,
            part,
            residual,
            grad_turned,
            retain,
            mix,
            left,
        )
    left, carry, lags = lax.optimization_barrier((left, carry, lags))
    cross, border = jnp.sum(carry[2:], axis=2)
    lags = jnp.sum(lags, axis=1)
    paired = retain * border
    decay = jnp.ones_like(retain)
    for lag in range(LAG):
        paired = paired + decay * lags[lag]
        decay = decay * retain
    small = jnp.concatenate(
        [
            paired,
            cross,
            grad_gain,
            grad_omega,
            grad_ffn_gain,
            grad_query_key.reshape(-1, width),
        ],
        axis=0,
    )
    used = small.shape[0]
    small = jnp.pad(small, ((0, -used % 8), (0, 0)))
    grad_tokens = left[1]
    vdim = value_weight.shape[1]
    if chained:
        small = tied(small, *chains)
        small = small + swapped(small, core)
        for one in chains:
            one.give()
        zdim, main_end, inner_dim = gains.shape[1], grad_main.shape[-1], ffn_in.shape[1]
        copies = [
            (0, slice(0, width), 0, 0),
            (0, slice(width, 2 * width), 1, 0),
            (1, slice(0, main_end), 2, zdim),
            (2, slice(inner_dim + vdim, inner_dim + vdim + zdim), 2, 0),
            (2, slice(0, inner_dim), 3, 0),
            (2, slice(inner_dim, inner_dim + vdim), 4, 0),
        ]
        shapes = [
            ffn_out.shape,
            output_weight.shape,
            base_weight.shape,
            ffn_in.shape,
            value_weight.shape,
        ]
        first = gathered(chains, copies, shapes)
        small, first = lax.optimization_barrier((small, first))
        small = paired_sum(small, orders[0][1:3])
        small = paired_sum(small, orders[0][3:5])
    else:
        small = small_sum(small)
    paired, cross = small[:states], small[states : 2 * states]
    grad_gain, grad_omega, grad_ffn_gain = (small[2 * states + at] for at in range(3))
    grad_norm_gain = (grad_gain + jnp.sum(mix * paired, axis=0)) / norm_gain[0]
    grad_query_key = small[2 * states + 3 : used].reshape(grad_query_key.shape)
    grad_eta = (inflow * paired).T
    grad_beta = (eta * paired * gate).T
    grad_forget = (eta * paired * beta * (1.0 - forget) / gate - mix * cross).T
    vdim = value_weight.shape[1]
    if chained:
        (
            grad_ffn_out,
            grad_output_weight,
            grad_base_weight,
            grad_ffn_in,
            grad_value_weight,
        ) = gathered(chains, copies, shapes, first)
    else:
        grad_base = jnp.concatenate([grad_shared, grad_main], axis=-1)
        (
            grad_ffn_out,
            grad_output_weight,
            grad_base_weight,
            grad_ffn_in,
            grad_value_weight,
        ) = summed_everywhere(
            [
                weight_grad(act, cotangent),
                weight_grad(product, grad_proj),
                weight_grad(mixed, grad_base),
                weight_grad(ffn_low, grad_inner),
                weight_grad(normed, grad_vpre),
            ]
        )
    return (
        block_out,
        grad_tokens,
        grad_norm_gain,
        grad_value_weight,
        grad_forget,
        grad_beta,
        grad_eta,
        grad_omega,
        grad_base_weight,
        grad_query_key[:2],
        grad_query_key[2:],
        grad_output_weight,
        grad_ffn_gain,
        grad_ffn_in,
        grad_ffn_out,
    )


def solution(mesh):
    return jax.shard_map(
        per_device,
        mesh=mesh,
        in_specs=(
            P("row", "seq", None),
            P("row"),
            P(),
            P(),
            P(),
            P(),
            P(),
            P(),
            P(),
            P(),
            P(),
            P(),
            P(),
            P(),
            P(),
            P("row", "seq", None),
        ),
        out_specs=(
            P("row", "seq", None),
            P("row", "seq", None),
            P(),
            P(),
            P(),
            P(),
            P(),
            P(),
            P(),
            P(),
            P(),
            P(),
            P(),
            P(),
            P(),
        ),
        check_vma=False,
    )
```

```python
import functools

import jax
import jax.numpy as jnp
from jax import lax
from jax.experimental import pallas as pl
from jax.experimental.pallas import tpu as pltpu
from jax.sharding import PartitionSpec as P

GROUP = 128
STEPS = 32
LAG = 8
LANES = 128

epsilon = 1e-05
very_low = -1e30
scan_params = pltpu.CompilerParams(vmem_limit_bytes=20 * 2**20)
front_params = pltpu.CompilerParams(vmem_limit_bytes=52 * 2**20)
dense_params = pltpu.CompilerParams(vmem_limit_bytes=36 * 2**20)


def work_cost(flops, seconds):
    return pl.CostEstimate(flops=int(flops), bytes_accessed=int(seconds * 3.0e12), transcendentals=0)


def sigmoid(value):
    return 0.5 * jnp.tanh(0.5 * value) + 0.5


def unit_norm(values):
    centered = values - jnp.mean(values, axis=-1, keepdims=True)
    spread = jnp.mean(centered * centered, axis=-1, keepdims=True)
    scale = lax.rsqrt(spread + epsilon)
    return centered * scale, scale


def norm_backward(grad, unit_values, scale):
    along = jnp.mean(grad * unit_values, axis=-1, keepdims=True)
    return scale * (grad - jnp.mean(grad, axis=-1, keepdims=True) - unit_values * along)


def whole_spec(shape):
    return pl.BlockSpec(shape, lambda step: (0,) * len(shape))


def lane_slices(width):
    return [slice(low, low + LANES) for low in range(0, width, LANES)]


def spread_rows(ref, index, lanes, rows):
    return jnp.broadcast_to(ref[index : index + 1, lanes], (rows, LANES))


def add_all(parts):
    while len(parts) > 1:
        parts = [
            parts[at] + parts[at + 1] if at + 1 < len(parts) else parts[at]
            for at in range(0, len(parts), 2)
        ]
    return parts[0]


def enter_body(count_ref, tokens_ref, gain_ref, retain_ref, low_ref, turned_ref, end_ref, state):
    step = pl.program_id(0)
    rows, steps, width = tokens_ref.shape
    states = retain_ref.shape[0]

    @pl.when(step == 0)
    def _():
        state[...] = jnp.zeros_like(state)

    values = tokens_ref[...].astype(jnp.float32)
    centered = values - jnp.mean(values, axis=-1, keepdims=True)
    spread = jnp.mean(centered * centered, axis=-1, keepdims=True)
    normed = centered * lax.rsqrt(spread + epsilon) * gain_ref[...]
    low_ref[...] = normed.astype(jnp.bfloat16)
    places = step * steps + lax.broadcasted_iota(jnp.int32, (steps, 1), 0)
    kept = jnp.stack([jnp.where(places < count_ref[row], normed[row], 0.0) for row in range(rows)])
    for lanes in lane_slices(width):
        for unit in range(steps // LAG):
            part = slice(unit * LAG, (unit + 1) * LAG)
            turned_ref[part, :, lanes] = jnp.swapaxes(kept[:, part, lanes], 0, 1)
    for lanes in lane_slices(width):
        retain = [spread_rows(retain_ref, j, lanes, rows) for j in range(states)]

        def unit_step(unit, hidden):
            for within in range(LAG):
                entry = turned_ref[unit * LAG + within, :, lanes]
                hidden = [retain[j] * hidden[j] + entry for j in range(states)]
            return hidden

        hidden = lax.fori_loop(
            0, steps // LAG, unit_step, [state[j, :, lanes] for j in range(states)]
        )
        for j in range(states):
            state[j, :, lanes] = hidden[j]

    @pl.when(step == pl.num_programs(0) - 1)
    def _():
        end_ref[...] = state[...]


def enter_call(counts, tokens, gain, retain):
    rows, length, width = tokens.shape
    states = retain.shape[0]
    natural = pl.BlockSpec((rows, STEPS, width), lambda step: (0, step, 0))
    return pl.pallas_call(
        enter_body,
        grid=(length // STEPS,),
        in_specs=[
            pl.BlockSpec(memory_space=pltpu.SMEM),
            natural,
            whole_spec((1, width)),
            whole_spec((states, width)),
        ],
        out_specs=(
            natural,
            pl.BlockSpec((STEPS, rows, width), lambda step: (step, 0, 0)),
            whole_spec((states, rows, width)),
        ),
        out_shape=(
            jax.ShapeDtypeStruct(tokens.shape, jnp.bfloat16),
            jax.ShapeDtypeStruct((length, rows, width), jnp.float32),
            jax.ShapeDtypeStruct((states, rows, width), jnp.float32),
        ),
        scratch_shapes=[pltpu.VMEM((states, rows, width), jnp.float32)],
        compiler_params=front_params,
        cost_estimate=work_cost(0.0, 9e-6),
        name="enter",
    )(counts, tokens, gain, retain)


def average_body(turned_ref, retain_ref, mix_ref, held_ref, state, out_ref):
    step = pl.program_id(0)
    steps, rows, width = turned_ref.shape
    states = retain_ref.shape[0]

    @pl.when(step == 0)
    def _():
        state[...] = held_ref[...]

    for lanes in lane_slices(width):
        retain = [spread_rows(retain_ref, j, lanes, rows) for j in range(states)]
        mix = [spread_rows(mix_ref, j, lanes, rows) for j in range(states)]

        def unit_step(unit, hidden):
            sums = []
            for within in range(LAG):
                entry = turned_ref[unit * LAG + within, :, lanes]
                hidden = [retain[j] * hidden[j] + entry for j in range(states)]
                sums.append(add_all([mix[j] * hidden[j] for j in range(states)]))
            out_ref[:, pl.ds(unit * LAG, LAG), lanes] = jnp.swapaxes(jnp.stack(sums), 0, 1)
            return hidden

        hidden = lax.fori_loop(
            0, steps // LAG, unit_step, [state[j, :, lanes] for j in range(states)]
        )
        for j in range(states):
            state[j, :, lanes] = hidden[j]


def average_call(turned, retain, mix, start):
    length, rows, width = turned.shape
    states = retain.shape[0]
    held = (states, rows, width)
    return pl.pallas_call(
        average_body,
        grid=(length // STEPS,),
        in_specs=[
            pl.BlockSpec((STEPS, rows, width), lambda step: (step, 0, 0)),
            whole_spec((states, width)),
            whole_spec((states, width)),
            whole_spec(held),
        ],
        out_specs=(
            whole_spec(held),
            pl.BlockSpec((rows, STEPS, width), lambda step: (0, step, 0)),
        ),
        out_shape=(
            jax.ShapeDtypeStruct(held, jnp.float32),
            jax.ShapeDtypeStruct((rows, length, width), jnp.float32),
        ),
        compiler_params=front_params,
        cost_estimate=work_cost(0.0, 12e-6),
        name="average",
    )(turned, retain, mix, start)


def return_body(grad_ref, retain_ref, turned_ref, end_ref, state):
    step = pl.program_id(0)
    rows, steps, width = grad_ref.shape
    states = retain_ref.shape[0]

    @pl.when(step == 0)
    def _():
        state[...] = jnp.zeros_like(state)

    for lanes in lane_slices(width):
        retain = [spread_rows(retain_ref, j, lanes, rows) for j in range(states)]

        def unit_step(unit, hidden):
            part = pl.ds((steps // LAG - 1 - unit) * LAG, LAG)
            turned = jnp.swapaxes(grad_ref[:, part, lanes], 0, 1)
            turned_ref[part, :, lanes] = turned
            for within in reversed(range(LAG)):
                hidden = [retain[j] * hidden[j] + turned[within] for j in range(states)]
            return hidden

        hidden = lax.fori_loop(
            0, steps // LAG, unit_step, [state[j, :, lanes] for j in range(states)]
        )
        for j in range(states):
            state[j, :, lanes] = hidden[j]

    @pl.when(step == pl.num_programs(0) - 1)
    def _():
        end_ref[...] = state[...]


def return_call(grad, retain):
    rows, length, width = grad.shape
    states = retain.shape[0]
    last = length // STEPS - 1
    return pl.pallas_call(
        return_body,
        grid=(length // STEPS,),
        in_specs=[
            pl.BlockSpec((rows, STEPS, width), lambda step: (0, last - step, 0)),
            whole_spec((states, width)),
        ],
        out_specs=(
            pl.BlockSpec((STEPS, rows, width), lambda step: (last - step, 0, 0)),
            whole_spec((states, rows, width)),
        ),
        out_shape=(
            jax.ShapeDtypeStruct((length, rows, width), jnp.float32),
            jax.ShapeDtypeStruct((states, rows, width), jnp.float32),
        ),
        scratch_shapes=[pltpu.VMEM((states, rows, width), jnp.float32)],
        compiler_params=scan_params,
        cost_estimate=work_cost(0.0, 8e-6),
        name="back_enter",
    )(grad, retain)


def sums_body(
    grad_ref,
    turned_ref,
    retain_ref,
    inverse_ref,
    unit_ref,
    held_ref,
    lag_in_ref,
    carry_ref,
    lag_ref,
):
    step = pl.program_id(0)
    steps, rows, width = grad_ref.shape
    states = retain_ref.shape[0]
    half = states // 2
    units = steps // LAG

    @pl.when(step == 0)
    def _():
        carry_ref[...] = held_ref[...]
        lag_ref[...] = lag_in_ref[...]

    for lanes in lane_slices(width):
        for first in range(0, states, half):
            chosen = range(first, first + half)
            retain = [spread_rows(retain_ref, j, lanes, rows) for j in chosen]
            inverse = [spread_rows(inverse_ref, j, lanes, rows) for j in chosen]

            def unit_step(unit, carried):
                after, hidden, cross = carried
                unit = units - 1 - unit
                later = after
                for within in reversed(range(LAG)):
                    place = unit * LAG + within
                    entry = turned_ref[place, :, lanes]
                    grad = grad_ref[place, :, lanes]
                    after = [retain[m] * after[m] + grad for m in range(half)]
                    hidden = [(hidden[m] - entry) * inverse[m] for m in range(half)]
                    cross = [cross[m] + after[m] * hidden[m] for m in range(half)]
                for m, j in enumerate(chosen):
                    unit_decay = spread_rows(unit_ref, j, lanes, rows)
                    carry_ref[3, j, :, lanes] += hidden[m] * (after[m] - unit_decay * later[m])
                return after, hidden, cross

            results = lax.fori_loop(
                0,
                units,
                unit_step,
                tuple([carry_ref[kind, j, :, lanes] for j in chosen] for kind in range(3)),
            )
            for kind in range(3):
                for m, j in enumerate(chosen):
                    carry_ref[kind, j, :, lanes] = results[kind][m]

        def lag_step(unit, lags):
            entries = [turned_ref[unit * LAG + at, :, lanes] for at in range(LAG)]
            grads = [grad_ref[unit * LAG + at, :, lanes] for at in range(LAG)]
            return [
                lags[lag] + add_all([grads[at] * entries[at - lag] for at in range(lag, LAG)])
                for lag in range(LAG)
            ]

        lags = lax.fori_loop(0, units, lag_step, [lag_ref[at, :, lanes] for at in range(LAG)])
        for at in range(LAG):
            lag_ref[at, :, lanes] = lags[at]


def sums_call(low_end, high_end, grad, turned, params, carried):
    rows, width = grad.shape[1:]
    states = params[0].shape[0]
    last = high_end // STEPS - 1
    turned_spec = pl.BlockSpec((STEPS, rows, width), lambda step: (last - step, 0, 0))
    carried_specs = [whole_spec(value.shape) for value in carried]
    return pl.pallas_call(
        sums_body,
        grid=((high_end - low_end) // STEPS,),
        in_specs=[turned_spec] * 2 + [whole_spec((states, width))] * 3 + carried_specs,
        out_specs=carried_specs,
        out_shape=[jax.ShapeDtypeStruct(value.shape, jnp.float32) for value in carried],
        compiler_params=scan_params,
        cost_estimate=work_cost(0.0, 8e-6),
        name="adjoint_sums",
    )(grad, turned, *params, *carried)


def leave_body(
    count_ref,
    tokens_ref,
    gain_ref,
    part_ref,
    residual_ref,
    grad_ref,
    retain_ref,
    mix_ref,
    held_ref,
    *others,
    places_before,
):
    carry_ref, out_ref, path = others[-3:]
    step = pl.program_id(0)
    steps, rows, width = grad_ref.shape
    states = retain_ref.shape[0]
    units = steps // LAG

    @pl.when(step == 0)
    def _():
        carry_ref[...] = held_ref[...]

    for lanes in lane_slices(width):
        retain = [spread_rows(retain_ref, j, lanes, rows) for j in range(states)]
        mix = [spread_rows(mix_ref, j, lanes, rows) for j in range(states)]

        def unit_step(unit, after):
            unit = units - 1 - unit
            sums = []
            for within in reversed(range(LAG)):
                grad = grad_ref[unit * LAG + within, :, lanes]
                after = [retain[j] * after[j] + grad for j in range(states)]
                sums.append(add_all([mix[j] * after[j] for j in range(states)]))
            path[:, pl.ds(unit * LAG, LAG), lanes] = jnp.swapaxes(jnp.stack(sums[::-1]), 0, 1)
            return after

        after = lax.fori_loop(
            0, units, unit_step, [carry_ref[j, :, lanes] for j in range(states)]
        )
        for j in range(states):
            carry_ref[j, :, lanes] = after[j]

    first_place = places_before + (pl.num_programs(0) - 1 - step) * steps
    places = first_place + lax.broadcasted_iota(jnp.int32, (steps, 1), 0)
    gain = gain_ref[...]
    for row in range(rows):
        unit_values, scale = unit_norm(tokens_ref[row].astype(jnp.float32))
        grad = part_ref[row].astype(jnp.float32)
        grad = grad + jnp.where(places < count_ref[row], path[row], 0.0)
        out = norm_backward(grad * gain, unit_values, scale)
        out_ref[row] = (out + residual_ref[row].astype(jnp.float32)).astype(jnp.bfloat16)


def leave_call(
    low_end, high_end, counts, tokens, gain, part, residual, grad, retain, mix, carried
):
    rows, length, width = tokens.shape
    held = carried[0].shape
    last = high_end // STEPS - 1
    going_on = len(carried) > 1
    natural = pl.BlockSpec((rows, STEPS, width), lambda step: (0, last - step, 0))
    return pl.pallas_call(
        functools.partial(leave_body, places_before=low_end),
        grid=((high_end - low_end) // STEPS,),
        in_specs=[
            pl.BlockSpec(memory_space=pltpu.SMEM),
            natural,
            whole_spec((1, width)),
            natural,
            natural,
            pl.BlockSpec((STEPS, rows, width), lambda step: (last - step, 0, 0)),
            whole_spec(retain.shape),
            whole_spec(mix.shape),
            whole_spec(held),
        ]
        + [pl.BlockSpec(memory_space=pl.ANY)] * going_on,
        out_specs=[whole_spec(held), natural],
        out_shape=[
            jax.ShapeDtypeStruct(held, jnp.float32),
            jax.ShapeDtypeStruct((rows, length, width), jnp.bfloat16),
        ],
        input_output_aliases={9: 1} if going_on else {},
        scratch_shapes=[pltpu.VMEM((rows, STEPS, width), jnp.float32)],
        compiler_params=scan_params,
        cost_estimate=work_cost(0.0, 8e-6),
        name="leave",
    )(counts, tokens, gain, part, residual, grad, retain, mix, *carried)


class Exchange:
    def __init__(self, local, decay, axis, backward):
        self.axis, self.backward = axis, backward
        self.count = lax.axis_size(axis)
        place = lax.axis_index(axis)
        self.place = self.count - 1 - place if backward else place
        self.low = self.place % 2
        self.half = local.shape[-1] // 2
        self.local = local
        self.decay = self.part(decay, self.low)

    def part(self, value, which):
        return lax.dynamic_slice_in_dim(value, which * self.half, self.half, value.ndim - 1)

    def moved(self, value, pairs):
        last = self.count - 1
        if self.backward:
            pairs = [(last - source, last - target) for source, target in pairs]
        return lax.ppermute(value, self.axis, pairs)

    def swapped(self, value):
        return self.moved(value, [(at, at ^ 1) for at in range(self.count)])

    def later(self, value, hop):
        return self.moved(value, [(at, at + 2 * hop) for at in range(self.count - 2 * hop)])

    def share(self):
        own = self.part(self.local, self.low)
        other = self.swapped(self.part(self.local, 1 - self.low))
        self.first = jnp.where(self.low == 0, own, other)
        self.pair = self.decay * self.first + jnp.where(self.low == 0, other, own)

    def cross(self):
        pairs = self.count // 2
        decay = self.decay * self.decay
        if pairs <= 4:
            arrived = [self.later(self.pair, hop) for hop in range(1, pairs)]
            total = arrived[-1]
            for value in arrived[-2::-1]:
                total = decay * total + value
        else:
            total, hop = self.later(self.pair, 1), 1
            while hop < pairs - 1:
                total = total + decay * self.later(total, hop)
                decay = decay * decay
                hop *= 2
        self.start = total

    def give(self):
        second = self.decay * self.start + self.first
        kept = jnp.where(self.low == 0, self.start, second)
        got = self.swapped(jnp.where(self.low == 0, second, self.start))
        return jnp.concatenate(
            [jnp.where(self.low == 0, kept, got), jnp.where(self.low == 0, got, kept)], axis=-1
        )


mesh_axes = ("seq", "row")


def device_total():
    return lax.axis_size("seq") * lax.axis_size("row")


def device_place():
    return lax.axis_index("seq") * lax.axis_size("row") + lax.axis_index("row")


def swapped(value, bit):
    return lax.ppermute(value, mesh_axes, [(at, at ^ bit) for at in range(device_total())])


def half_summed(value, bit):
    half = value.shape[0] // 2
    mine = (device_place() // bit) % 2
    sent = lax.dynamic_slice_in_dim(value, (1 - mine) * half, half, 0)
    kept = lax.dynamic_slice_in_dim(value, mine * half, half, 0)
    return kept + swapped(sent, bit)


def both_halves(value, bit):
    mine = (device_place() // bit) % 2 == 1
    other = swapped(value, bit)
    return jnp.concatenate([jnp.where(mine, other, value), jnp.where(mine, value, other)], axis=0)


def link_orders():
    total = device_total()
    bits = [1 << at for at in range(total.bit_length() - 1)]
    if (lax.axis_size("seq"), lax.axis_size("row")) == (8, 4):
        core, x, y, z_low, z_high = bits
        return (
            (core, x, y, z_low, z_high),
            (core, y, z_low, x, z_high),
            (core, z_low, x, y, z_high),
        )
    third = len(bits) // 3
    return tuple(bits[turn * third :] + bits[: turn * third] for turn in range(3))


def summed_everywhere(values):
    orders = link_orders()
    for at in range(len(orders[0])):
        values = [half_summed(v, orders[n % 3][at]) for n, v in enumerate(values)]
    for at in reversed(range(len(orders[0]))):
        values = [both_halves(v, orders[n % 3][at]) for n, v in enumerate(values)]
    return values


def paired_sum(value, group):
    partners = [group[0]] if len(group) == 1 else [group[0], group[1], group[0] + group[1]]
    arrived = [swapped(value, partner) for partner in partners]
    if len(arrived) == 1:
        return value + arrived[0]
    return (value + arrived[0]) + (arrived[1] + arrived[2])


def small_sum(value):
    bits = [1 << at for at in range(device_total().bit_length() - 1)]
    for at in range(0, len(bits), 2):
        value = paired_sum(value, bits[at : at + 2])
    return value


def power_of(value, exponent):
    result = None
    while exponent:
        if exponent & 1:
            result = value if result is None else result * value
        value = value * value
        exponent >>= 1
    return result


def dot(first_op, second_op):
    return jnp.dot(first_op, second_op, preferred_element_type=jnp.float32)


def dot_back(first_op, second_op):
    return lax.dot_general(
        first_op, second_op, (((1,), (1,)), ((), ())), preferred_element_type=jnp.float32
    )


def dot_outer(first_op, second_op):
    return lax.dot_general(
        first_op, second_op, (((0,), (0,)), ((), ())), preferred_element_type=jnp.float32
    )


def low(value):
    return value.astype(jnp.bfloat16)


def chunks(low_end, high_end, size):
    return [slice(at, min(at + size, high_end)) for at in range(low_end, high_end, size)]


def gated(value):
    half = 0.5 * value
    turn = jnp.tanh(half)
    gate = 0.5 * turn + 0.5
    act = half * turn + half
    return act, gate + act * (1.0 - gate)


def value_body(normed_ref, value_weight_ref, value_ref, value_slope_ref):
    for part in chunks(0, value_ref.shape[1], 256):
        value, slope = gated(low(dot(normed_ref[...], value_weight_ref[:, part])))
        value_ref[:, part] = low(value)
        value_slope_ref[:, part] = low(slope)


def value_call(normed, value_weight):
    rows, length, width = normed.shape
    vdim = value_weight.shape[1]
    return pl.pallas_call(
        value_body,
        grid=(rows,),
        in_specs=[row_spec(length, width), once_spec(value_weight.shape)],
        out_specs=[row_spec(length, vdim)] * 2,
        out_shape=[jax.ShapeDtypeStruct((rows, length, vdim), jnp.bfloat16)] * 2,
        compiler_params=front_params,
        cost_estimate=work_cost(2e9, 5e-6),
        name="value",
    )(normed, value_weight)


def forward_body(
    count_ref,
    tokens_ref,
    cotangent_ref,
    average_ref,
    normed_ref,
    value_ref,
    value_slope_ref,
    omega_ref,
    base_weight_ref,
    gains_ref,
    biases_ref,
    output_weight_ref,
    ffn_gain_ref,
    ffn_in_ref,
    ffn_out_ref,
    out_ref,
    mixed_ref,
    mixed_slope_ref,
    product_ref,
    ffn_low_ref,
    act_ref,
    grad_inner_ref,
    grad_proj_ref,
    grad_main_ref,
    grad_shared_ref,
    grad_vpre_ref,
    residual_ref,
    ffn_gain_grad_ref,
    grad_gains_ref,
    reset_ref,
    reset_slope_ref,
    grad_attended_ref,
    probs_ref,
    query_ref,
    key_ref,
    shared_ref,
    shared_slope_ref,
):
    row = pl.program_id(0)
    length, width = tokens_ref.shape
    zdim = query_ref.shape[1]
    vdim = value_ref.shape[1]
    inner = act_ref.shape[1]

    @pl.when(row == 0)
    def _():
        ffn_gain_grad_ref[...] = jnp.zeros_like(ffn_gain_grad_ref)
        grad_gains_ref[...] = jnp.zeros_like(grad_gains_ref)

    normed = normed_ref[...]
    sums = average_ref[...] + omega_ref[...] * normed.astype(jnp.float32)
    gate = sigmoid(sums)
    mixed = sums * gate
    mixed_ref[...] = low(mixed)
    mixed_slope_ref[...] = low(gate + mixed * (1.0 - gate))
    mixed_low = mixed_ref[...]

    shared = dot(mixed_low, base_weight_ref[:, :zdim])
    gate = sigmoid(shared)
    shared_act = shared * gate
    shared_ref[...] = shared_act
    shared_slope_ref[...] = gate + shared_act * (1.0 - gate)
    query_ref[...] = low(shared_act * gains_ref[0:1] + biases_ref[0:1])
    key_ref[...] = low(shared_act * gains_ref[1:2] + biases_ref[1:2])

    to_place = lax.broadcasted_iota(jnp.int32, (GROUP, GROUP), 0)
    from_place = lax.broadcasted_iota(jnp.int32, (GROUP, GROUP), 1)
    for block in chunks(0, length, GROUP):
        allowed = (from_place <= to_place) & (
            (from_place < count_ref[row] - block.start) | (from_place == to_place)
        )
        scores = dot_back(query_ref[block], key_ref[block]) * zdim**-0.5
        scores = jnp.where(allowed, scores, very_low)
        weights = jnp.exp(scores - jnp.max(scores, axis=-1, keepdims=True))
        weights = jnp.where(allowed, weights, 0.0)
        probs_ref[block] = weights / jnp.sum(weights, axis=-1, keepdims=True)

    for part in chunks(0, vdim, 256):
        base_part = slice(zdim + part.start, zdim + part.stop)
        reset_act, reset_slope = gated(low(dot(mixed_low, base_weight_ref[:, base_part])))
        reset_ref[:, part] = low(reset_act)
        for block in chunks(0, length, GROUP):
            attended = low(dot(low(probs_ref[block]), value_ref[block, part]))
            product_ref[block, part] = low(attended * reset_act[block])
            reset_slope_ref[block, part] = low(attended * reset_slope[block])

    update_gate = sigmoid(dot(mixed_low, base_weight_ref[:, zdim + vdim : zdim + vdim + width]))
    candidate = dot(mixed_low, base_weight_ref[:, zdim + vdim + width :])
    candidate = candidate + dot(product_ref[...], output_weight_ref[...])
    candidate_gate = sigmoid(candidate)
    candidate_act = candidate * candidate_gate
    candidate_slope = candidate_gate + candidate_act * (1.0 - candidate_gate)
    tokens = tokens_ref[...].astype(jnp.float32)
    change = candidate_act - tokens
    after = tokens + update_gate * change
    unit_values, scale = unit_norm(after)
    ffn_low_ref[...] = low(unit_values * ffn_gain_ref[...])
    ffn_low = ffn_low_ref[...]
    cotangent = cotangent_ref[...]

    out = after
    grad_normed = jnp.zeros_like(after)
    for part in chunks(0, inner, 256):
        act, slope = gated(low(dot(ffn_low, ffn_in_ref[:, part])))
        act_ref[:, part] = low(act)
        grad_act = low(dot_back(cotangent, ffn_out_ref[part]))
        grad_inner_ref[:, part] = low(grad_act * slope)
    out = after + dot(act_ref[...], ffn_out_ref[...])
    out_ref[...] = low(out)
    grad_normed = dot_back(grad_inner_ref[...], ffn_in_ref[...])
    ffn_gain_grad_ref[...] += jnp.sum(grad_normed * unit_values, axis=0, keepdims=True)
    grad_after = cotangent.astype(jnp.float32) + norm_backward(
        grad_normed * ffn_gain_ref[...], unit_values, scale
    )
    grad_change = grad_after * update_gate
    grad_proj = low(grad_change * candidate_slope)
    grad_proj_ref[...] = grad_proj
    grad_main_ref[:, vdim : vdim + width] = low(grad_change * change * (1.0 - update_gate))
    grad_main_ref[:, vdim + width :] = grad_proj
    for part in chunks(0, vdim, 256):
        grad_product = low(dot_back(grad_proj, output_weight_ref[part]))
        grad_attended_ref[:, part] = low(grad_product * reset_ref[:, part])
        grad_main_ref[:, part] = low(grad_product * reset_slope_ref[:, part])

    grad_gains = jnp.zeros(grad_gains_ref.shape, jnp.float32)
    for block in chunks(0, length, GROUP):
        probs = probs_ref[block]
        probs_low = low(probs)
        grad_probs = dot_back(grad_attended_ref[block], value_ref[block])
        for part in chunks(0, vdim, 512):
            grad_value = dot_outer(probs_low, grad_attended_ref[block, part])
            grad_vpre_ref[block, part] = low(low(grad_value) * value_slope_ref[block, part])
        total = jnp.sum(grad_probs * probs, axis=-1, keepdims=True)
        grad_raw = low(probs * (grad_probs - total) * zdim**-0.5)
        grad_query = dot(grad_raw, key_ref[block])
        grad_key = dot_outer(grad_raw, query_ref[block])
        shared = shared_ref[block]
        grad_gains = grad_gains + jnp.concatenate(
            [
                jnp.sum(value, axis=0, keepdims=True)
                for value in (grad_query * shared, grad_key * shared, grad_query, grad_key)
            ],
            axis=0,
        )
        grad_shared = grad_query * gains_ref[0:1] + grad_key * gains_ref[1:2]
        grad_shared_ref[block] = low(grad_shared * shared_slope_ref[block])
    grad_gains_ref[...] += grad_gains
    residual_ref[...] = low(grad_after - grad_change)


def row_spec(length, width):
    return pl.BlockSpec((None, length, width), lambda row: (row, 0, 0))


def once_spec(shape):
    return pl.BlockSpec(shape, lambda row: (0,) * len(shape), pipeline_mode=pl.Buffered(1))


def forward_call(
    counts,
    tokens,
    cotangent,
    average,
    normed,
    value,
    value_slope,
    omega,
    base_weight,
    gains,
    biases,
    output_weight,
    ffn_gain,
    ffn_in,
    ffn_out,
):
    rows, length, width = tokens.shape
    zdim, vdim, inner = gains.shape[1], value.shape[2], ffn_in.shape[1]
    half, full = jnp.bfloat16, jnp.float32
    outs = [
        (width, half),
        (width, half),
        (width, half),
        (vdim, half),
        (width, half),
        (inner, half),
        (inner, half),
        (width, half),
        (vdim + 2 * width, half),
        (zdim, half),
        (vdim, half),
        (width, half),
    ]
    tied = [
        omega,
        base_weight,
        gains,
        biases,
        output_weight,
        ffn_gain,
        ffn_in,
        ffn_out,
    ]
    return pl.pallas_call(
        forward_body,
        grid=(rows,),
        in_specs=[pl.BlockSpec(memory_space=pltpu.SMEM)]
        + [row_spec(length, width)] * 4
        + [row_spec(length, vdim)] * 2
        + [once_spec(weight.shape) for weight in tied],
        out_specs=[row_spec(length, size) for size, _ in outs]
        + [whole_spec((1, width)), whole_spec((4, zdim))],
        out_shape=[jax.ShapeDtypeStruct((rows, length, size), kind) for size, kind in outs]
        + [jax.ShapeDtypeStruct((1, width), full), jax.ShapeDtypeStruct((4, zdim), full)],
        scratch_shapes=[pltpu.VMEM((length, vdim), half)] * 3
        + [pltpu.VMEM((length, GROUP), full)]
        + [pltpu.VMEM((length, zdim), half)] * 2
        + [pltpu.VMEM((length, zdim), full)] * 2,
        compiler_params=front_params,
        cost_estimate=work_cost(18e9, 40e-6),
        name="dense_forward",
    )(counts, tokens, cotangent, average, normed, value, value_slope, *tied)


def backward_body(
    grad_main_ref,
    grad_shared_ref,
    grad_vpre_ref,
    normed_ref,
    mixed_slope_ref,
    omega_ref,
    value_weight_ref,
    base_weight_ref,
    grad_average_ref,
    part_ref,
    grad_omega_ref,
    grad_gain_ref,
):
    zdim = grad_shared_ref.shape[1]

    @pl.when(pl.program_id(0) == 0)
    def _():
        grad_omega_ref[...] = jnp.zeros_like(grad_omega_ref)
        grad_gain_ref[...] = jnp.zeros_like(grad_gain_ref)

    grad_average = dot_back(grad_main_ref[...], base_weight_ref[:, zdim:])
    grad_average = grad_average + dot_back(grad_shared_ref[...], base_weight_ref[:, :zdim])
    grad_average = grad_average * mixed_slope_ref[...].astype(jnp.float32)
    grad_average_ref[...] = grad_average
    part = dot_back(grad_vpre_ref[...], value_weight_ref[...]) + grad_average * omega_ref[...]
    part_ref[...] = part
    normed = normed_ref[...].astype(jnp.float32)
    grad_omega_ref[...] += jnp.sum(grad_average * normed, axis=0, keepdims=True)
    grad_gain_ref[...] += jnp.sum(part * normed, axis=0, keepdims=True)


def backward_call(inputs, tied_inputs):
    rows, length, _ = inputs[0].shape
    width = tied_inputs[0].shape[1]
    return pl.pallas_call(
        backward_body,
        grid=(rows,),
        in_specs=[row_spec(length, value.shape[2]) for value in inputs]
        + [once_spec(value.shape) for value in tied_inputs],
        out_specs=[row_spec(length, width)] * 2 + [whole_spec((1, width))] * 2,
        out_shape=[jax.ShapeDtypeStruct((rows, length, width), jnp.float32)] * 2
        + [jax.ShapeDtypeStruct((1, width), jnp.float32)] * 2,
        compiler_params=dense_params,
        cost_estimate=work_cost(7e9, 12e-6),
        name="dense_backward",
    )(*inputs, *tied_inputs)


def joined_body(*refs, widths, split):
    refs = refs[1:] if split else refs
    outs_per_chain = 2 if split else 1
    outs = refs[len(refs) - outs_per_chain * len(widths) :]
    at = 0
    for chain, parts in enumerate(widths):
        for side in range(outs_per_chain):
            column = 0
            for width in parts:
                total = refs[at][...] + refs[at + 1][...]
                outs[chain * outs_per_chain + side][:, column : column + width] = total
                column += width
                at += 2


def joined(chains):
    split = chains[0][2] is not None
    sides = 2 if split else 1
    widths = [[value.shape[1] for value in kept] for kept, _, _ in chains]
    sizes = [kept[0].shape[0] // sides for kept, _, _ in chains]
    steps = 4
    while any(size % (8 * steps) for size in sizes):
        steps //= 2
    operands, in_specs, out_specs, out_shape = [], [], [], []
    for chain, (kept, arrived, _) in enumerate(chains):
        block = sizes[chain] // steps
        for side in range(sides):

            def place(step, *held, chain=chain, side=side):
                if not held:
                    return step, 0
                mine = held[0][chain]
                return (1 - mine if side else mine) * steps + step, 0

            for pair in zip(kept, arrived):
                for value in pair:
                    operands.append(value)
                    in_specs.append(pl.BlockSpec((block, value.shape[1]), place))
            total = sum(widths[chain])
            out_specs.append(pl.BlockSpec((block, total), lambda step, *held: (step, 0)))
            out_shape.append(jax.ShapeDtypeStruct((sizes[chain], total), jnp.float32))
    if split:
        mine = [(device_place() // bit) % 2 for _, _, bit in chains]
        operands.insert(0, jnp.stack(mine).astype(jnp.int32))
    outs = pl.pallas_call(
        functools.partial(joined_body, widths=widths, split=split),
        grid_spec=pltpu.PrefetchScalarGridSpec(
            num_scalar_prefetch=1 if split else 0,
            grid=(steps,),
            in_specs=in_specs,
            out_specs=out_specs,
        ),
        out_shape=out_shape,
        compiler_params=scan_params,
        cost_estimate=work_cost(0.0, 2e-6),
        name="joined",
    )(*operands)
    return [tuple(outs[at : at + sides]) for at in range(0, len(outs), sides)]


def placed_body(*refs, copies, sources):
    mine, refs = refs[0], refs[1:]
    half = pl.program_id(0)
    for own, arrived, which, taken, result, column in copies:
        there = slice(column, column + taken.stop - taken.start)

        @pl.when(half == mine[which])
        def _(own=own, taken=taken, result=result, there=there):
            refs[sources + result][:, there] = refs[own][:, taken]

        @pl.when(half != mine[which])
        def _(arrived=arrived, taken=taken, result=result, there=there):
            refs[sources + result][:, there] = refs[arrived][:, taken]


def placed(values, bits, copies, shapes):
    steps = 4
    while any(value.shape[0] % (8 * steps) for value in values):
        steps //= 2
    in_specs = []
    for at, value in enumerate(values):

        def place(half, step, mine, which=at // 2, other=at % 2):
            wanted = (half == mine[which]) != bool(other)
            return jnp.where(wanted, step, jnp.where(half == 0, 0, steps - 1)), 0

        in_specs.append(pl.BlockSpec((value.shape[0] // steps, value.shape[1]), place))
    mine = jnp.stack([(device_place() // bit) % 2 for bit in bits]).astype(jnp.int32)
    return pl.pallas_call(
        functools.partial(placed_body, copies=copies, sources=len(values)),
        grid_spec=pltpu.PrefetchScalarGridSpec(
            num_scalar_prefetch=1,
            grid=(2, steps),
            in_specs=in_specs,
            out_specs=[
                pl.BlockSpec(
                    (shape[0] // (2 * steps), shape[1]),
                    lambda half, step, mine: (half * steps + step, 0),
                )
                for shape in shapes
            ],
        ),
        out_shape=[jax.ShapeDtypeStruct(shape, jnp.float32) for shape in shapes],
        compiler_params=scan_params,
        cost_estimate=work_cost(0.0, 2e-6),
        name="placed",
    )(mine, *values)


def gathered_body(*refs, bits, copies, results, others, per_row):
    sources = refs[: 2 * len(bits)]
    outs = refs[len(refs) - results - len(sources) - 2 : len(refs) - len(sources) - 2]
    held, (in_sems, out_sems) = refs[len(refs) - len(sources) - 2 : -2], refs[-2:]
    place = lax.axis_index("seq") * per_row + lax.axis_index("row")
    arriving = []
    for at, source in enumerate(sources):
        copy = pltpu.make_async_copy(source, held[at], in_sems.at[at])
        copy.start()
        arriving.append(copy)
    leaving = []
    for at, source in enumerate(sources):
        high_bit, low_bit = bits[at // 2]
        high = (place // high_bit) % 2
        low_side = (place // low_bit) % 2
        if others:
            high = 1 - high
        if at % 2:
            low_side = 1 - low_side
        rows = source.shape[0]
        there = pl.ds(pl.multiple_of((2 * high + low_side) * rows, 8), rows)
        arriving[at].wait()
        for chain, taken, result, column in copies:
            if chain == at // 2:
                copy = pltpu.make_async_copy(
                    held[at].at[:, taken],
                    outs[result].at[there, column : column + taken.stop - taken.start],
                    out_sems.at[len(leaving)],
                )
                copy.start()
                leaving.append(copy)
    for copy in leaving:
        copy.wait()


def gathered(chains, copies, shapes, before=None):
    values = []
    for one in chains:
        values += one.held if before is None else one.arrived
    anywhere = pl.BlockSpec(memory_space=pl.ANY)
    aliases = {}
    if before is not None:
        aliases = {len(values) + at: at for at in range(len(shapes))}
    return pl.pallas_call(
        functools.partial(
            gathered_body,
            bits=[one.order[:2] for one in chains],
            copies=copies,
            results=len(shapes),
            others=before is not None,
            per_row=lax.axis_size("row"),
        ),
        in_specs=[anywhere] * (len(values) + len(aliases)),
        out_specs=[anywhere] * len(shapes),
        out_shape=[jax.ShapeDtypeStruct(shape, jnp.float32) for shape in shapes],
        input_output_aliases=aliases,
        scratch_shapes=[pltpu.VMEM(value.shape, jnp.float32) for value in values]
        + [
            pltpu.SemaphoreType.DMA((len(values),)),
            pltpu.SemaphoreType.DMA((2 * len(copies),)),
        ],
        compiler_params=scan_params,
        cost_estimate=work_cost(0.0, 6e-6),
        name="gathered",
    )(*values, *(before or ()))


class Chain:
    def __init__(self, order, sent, kept):
        self.order, self.at = order, 0
        self.sent, self.kept, self.arrived = list(sent), list(kept), []

    def state(self):
        return self.sent, self.kept, self.arrived

    def set_state(self, state):
        self.sent, self.kept, self.arrived = state

    def send(self):
        total = len(self.order)
        bit = self.order[self.at if self.at < total else 2 * total - 1 - self.at]
        self.arrived = [swapped(value, bit) for value in self.sent]

    def give(self):
        self.held = self.sent + self.arrived
        self.arrived = [swapped(value, self.order[0]) for value in self.held]

    def pieces(self):
        return self.held + self.arrived


def join(*chains):
    total = len(chains[0].order)
    if chains[0].at < total:
        last = chains[0].at == total - 1
        results = joined(
            [
                (one.kept, one.arrived, None if last else one.order[one.at + 1])
                for one in chains
            ]
        )
        for one, result in zip(chains, results):
            if last:
                one.sent, one.kept = [result[0]], []
            else:
                one.sent, one.kept = [result[1]], [result[0]]
    else:
        values, copies, shapes = [], [], []
        for at, one in enumerate(chains):
            rows, columns = one.sent[0].shape
            values += [one.sent[0], one.arrived[0]]
            copies.append((2 * at, 2 * at + 1, at, slice(0, columns), at, 0))
            shapes.append((2 * rows, columns))
        bits = [one.order[2 * total - 1 - one.at] for one in chains]
        for one, result in zip(chains, placed(values, bits, copies, shapes)):
            one.sent = [result]
    for one in chains:
        one.arrived = []
        one.at += 1


def tied(value, *chains):
    value, states = lax.optimization_barrier((value, [one.state() for one in chains]))
    for one, state in zip(chains, states):
        one.set_state(state)
    return value


def weight_halves(first_op, second_op, bit):
    first_op = first_op.reshape(-1, first_op.shape[-1])
    second_op = second_op.reshape(-1, second_op.shape[-1])
    half = first_op.shape[1] // 2
    mine = (device_place() // bit) % 2
    return [
        dot_outer(lax.dynamic_slice_in_dim(first_op, which * half, half, 1), second_op)
        for which in (1 - mine, mine)
    ]


def weight_grad(first_op, second_op):
    return dot_outer(
        first_op.reshape(-1, first_op.shape[-1]), second_op.reshape(-1, second_op.shape[-1])
    )


def per_device(
    tokens,
    valid_count,
    norm_gain,
    value_weight,
    ema_forget,
    ema_beta,
    ema_eta,
    ema_omega,
    base_weight,
    qk_gain,
    qk_bias,
    output_weight,
    ffn_gain,
    ffn_in,
    ffn_out,
    cotangent,
):
    length, width = tokens.shape[1:]
    counts = valid_count - lax.axis_index("seq") * length
    norm_gain = norm_gain.astype(jnp.float32)[None]
    ffn_gain = ffn_gain.astype(jnp.float32)[None]
    omega = ema_omega[None]
    gains, biases = qk_gain.astype(jnp.float32), qk_bias.astype(jnp.float32)
    forget, beta, eta = ema_forget.T, ema_beta.T, ema_eta.T
    retain = 1.0 - forget
    gate = jnp.sqrt(forget * (2.0 - forget))
    inflow = beta * gate
    mix = eta * inflow
    span_decay = power_of(retain, length)[:, None, :]

    normed, turned, device_end = enter_call(counts, tokens, norm_gain, retain)
    ahead = Exchange(device_end, span_decay, "seq", False)
    ahead.share()
    ahead.cross()
    value, value_slope = value_call(normed, value_weight)
    ahead.start, value, value_slope = lax.optimization_barrier((ahead.start, value, value_slope))
    incoming = ahead.give()
    state_end, average = average_call(turned, retain, mix, incoming)
    unit_decay = power_of(retain, LAG)
    (
        block_out,
        mixed,
        mixed_slope,
        product,
        ffn_low,
        act,
        grad_inner,
        grad_proj,
        grad_main,
        grad_shared,
        grad_vpre,
        residual,
        grad_ffn_gain,
        grad_query_key,
    ) = forward_call(
        counts,
        tokens,
        cotangent,
        average,
        normed,
        value,
        value_slope,
        omega,
        base_weight,
        gains,
        biases,
        output_weight,
        ffn_gain,
        ffn_in,
        ffn_out,
    )
    orders = link_orders()
    core = orders[0][0]
    chained = device_total() == 32
    chains = []
    back_inputs = [grad_main, grad_shared, grad_vpre, normed, mixed_slope]
    if chained:
        products = [
            [(act, cotangent), (product, grad_proj)],
            [(mixed, grad_main)],
            [(ffn_low, grad_inner), (normed, grad_vpre), (mixed, grad_shared)],
        ]
        halves = [[weight_halves(*pair, core) for pair in pairs] for pairs in products]
        for order, pairs in zip(orders, halves):
            chains.append(Chain(order, [pair[0] for pair in pairs], [pair[1] for pair in pairs]))
            chains[-1].send()
        join(*chains)
        back_inputs = tied(back_inputs, *chains)
        for one in chains:
            one.send()
    grad_average, part, grad_omega, grad_gain = backward_call(
        back_inputs, [omega, value_weight, base_weight]
    )

    def halve(value):
        if chained:
            value = tied(value, *chains)
            join(*chains)
            value = tied(value, *chains)
            for one in chains:
                one.send()
        return value

    grad_turned, device_start = return_call(grad_average, retain)
    behind = Exchange(device_start, span_decay, "seq", True)
    behind.share()
    behind.pair = halve(behind.pair)
    behind.cross()
    behind.start = halve(behind.start)
    later = behind.give()
    states = retain.shape[0]
    carried = [
        jnp.stack([later, state_end, jnp.zeros_like(later), jnp.zeros_like(later)]),
        jnp.zeros((LAG,) + later.shape[1:], jnp.float32),
    ]
    parts = length // STEPS
    inverse = 1.0 / retain
    ends = [at * STEPS // 8 for at in (8 * parts, 4 * parts, 2 * parts, 0)]
    ends = [at // STEPS * STEPS for at in ends]
    for high_end, low_end in zip(ends, ends[1:]):
        carried = halve(carried)
        carried = sums_call(
            low_end, high_end, grad_turned, turned, [retain, inverse, unit_decay], carried
        )
    carry, lags = carried
    ends = [at * STEPS for at in (parts, parts // 2, 0)]
    left = [later]
    for high_end, low_end in zip(ends, ends[1:]):
        left, carry, lags = halve((left, carry, lags))
        left = leave_call(
            low_end,
            high_end,
            counts,
            tokens,
            norm_gain,
            part,
            residual,
            grad_turned,
            retain,
            mix,
            left,
        )
    left, carry, lags = lax.optimization_barrier((left, carry, lags))
    cross, border = jnp.sum(carry[2:], axis=2)
    lags = jnp.sum(lags, axis=1)
    paired = retain * border
    decay = jnp.ones_like(retain)
    for lag in range(LAG):
        paired = paired + decay * lags[lag]
        decay = decay * retain
    small = jnp.concatenate(
        [
            paired,
            cross,
            grad_gain,
            grad_omega,
            grad_ffn_gain,
            grad_query_key.reshape(-1, width),
        ],
        axis=0,
    )
    used = small.shape[0]
    small = jnp.pad(small, ((0, -used % 8), (0, 0)))
    grad_tokens = left[1]
    vdim = value_weight.shape[1]
    if chained:
        small = tied(small, *chains)
        small = small + swapped(small, core)
        for one in chains:
            one.give()
        zdim, main_end, inner_dim = gains.shape[1], grad_main.shape[-1], ffn_in.shape[1]
        copies = [
            (0, slice(0, width), 0, 0),
            (0, slice(width, 2 * width), 1, 0),
            (1, slice(0, main_end), 2, zdim),
            (2, slice(inner_dim + vdim, inner_dim + vdim + zdim), 2, 0),
            (2, slice(0, inner_dim), 3, 0),
            (2, slice(inner_dim, inner_dim + vdim), 4, 0),
        ]
        shapes = [
            ffn_out.shape,
            output_weight.shape,
            base_weight.shape,
            ffn_in.shape,
            value_weight.shape,
        ]
        first = gathered(chains, copies, shapes)
        small = paired_sum(small, orders[0][1:3])
        small, first = tied((small, first), *chains)
        small = paired_sum(small, orders[0][3:5])
    else:
        small = small_sum(small)
    paired, cross = small[:states], small[states : 2 * states]
    grad_gain, grad_omega, grad_ffn_gain = (small[2 * states + at] for at in range(3))
    grad_norm_gain = (grad_gain + jnp.sum(mix * paired, axis=0)) / norm_gain[0]
    grad_query_key = small[2 * states + 3 : used].reshape(grad_query_key.shape)
    grad_eta = (inflow * paired).T
    grad_beta = (eta * paired * gate).T
    grad_forget = (eta * paired * beta * (1.0 - forget) / gate - mix * cross).T
    vdim = value_weight.shape[1]
    if chained:
        (
            grad_ffn_out,
            grad_output_weight,
            grad_base_weight,
            grad_ffn_in,
            grad_value_weight,
        ) = gathered(chains, copies, shapes, first)
    else:
        grad_base = jnp.concatenate([grad_shared, grad_main], axis=-1)
        (
            grad_ffn_out,
            grad_output_weight,
            grad_base_weight,
            grad_ffn_in,
            grad_value_weight,
        ) = summed_everywhere(
            [
                weight_grad(act, cotangent),
                weight_grad(product, grad_proj),
                weight_grad(mixed, grad_base),
                weight_grad(ffn_low, grad_inner),
                weight_grad(normed, grad_vpre),
            ]
        )
    return (
        block_out,
        grad_tokens,
        grad_norm_gain,
        grad_value_weight,
        grad_forget,
        grad_beta,
        grad_eta,
        grad_omega,
        grad_base_weight,
        grad_query_key[:2],
        grad_query_key[2:],
        grad_output_weight,
        grad_ffn_gain,
        grad_ffn_in,
        grad_ffn_out,
    )


def solution(mesh):
    return jax.shard_map(
        per_device,
        mesh=mesh,
        in_specs=(
            P("row", "seq", None),
            P("row"),
            P(),
            P(),
            P(),
            P(),
            P(),
            P(),
            P(),
            P(),
            P(),
            P(),
            P(),
            P(),
            P(),
            P("row", "seq", None),
        ),
        out_specs=(
            P("row", "seq", None),
            P("row", "seq", None),
            P(),
            P(),
            P(),
            P(),
            P(),
            P(),
            P(),
            P(),
            P(),
            P(),
            P(),
            P(),
            P(),
        ),
        check_vma=False,
    )
```

```python
import functools

import jax
import jax.numpy as jnp
from jax import lax
from jax.experimental import pallas as pl
from jax.experimental.pallas import tpu as pltpu
from jax.sharding import PartitionSpec as P

GROUP = 128
STEPS = 32
LAG = 8
LANES = 128

epsilon = 1e-05
very_low = -1e30
scan_params = pltpu.CompilerParams(vmem_limit_bytes=14 * 2**20)
front_params = pltpu.CompilerParams(vmem_limit_bytes=52 * 2**20)
dense_params = pltpu.CompilerParams(vmem_limit_bytes=30 * 2**20)


def work_cost(flops, seconds):
    return pl.CostEstimate(flops=int(flops), bytes_accessed=int(seconds * 3.0e12), transcendentals=0)


def sigmoid(value):
    return 0.5 * jnp.tanh(0.5 * value) + 0.5


def unit_norm(values):
    centered = values - jnp.mean(values, axis=-1, keepdims=True)
    spread = jnp.mean(centered * centered, axis=-1, keepdims=True)
    scale = lax.rsqrt(spread + epsilon)
    return centered * scale, scale


def norm_backward(grad, unit_values, scale):
    along = jnp.mean(grad * unit_values, axis=-1, keepdims=True)
    return scale * (grad - jnp.mean(grad, axis=-1, keepdims=True) - unit_values * along)


def whole_spec(shape):
    return pl.BlockSpec(shape, lambda step: (0,) * len(shape))


def lane_slices(width):
    return [slice(low, low + LANES) for low in range(0, width, LANES)]


def spread_rows(ref, index, lanes, rows):
    return jnp.broadcast_to(ref[index : index + 1, lanes], (rows, LANES))


def add_all(parts):
    while len(parts) > 1:
        parts = [
            parts[at] + parts[at + 1] if at + 1 < len(parts) else parts[at]
            for at in range(0, len(parts), 2)
        ]
    return parts[0]


def enter_body(count_ref, tokens_ref, gain_ref, retain_ref, low_ref, turned_ref, end_ref, state):
    step = pl.program_id(0)
    rows, steps, width = tokens_ref.shape
    states = retain_ref.shape[0]

    @pl.when(step == 0)
    def _():
        state[...] = jnp.zeros_like(state)

    values = tokens_ref[...].astype(jnp.float32)
    centered = values - jnp.mean(values, axis=-1, keepdims=True)
    spread = jnp.mean(centered * centered, axis=-1, keepdims=True)
    normed = centered * lax.rsqrt(spread + epsilon) * gain_ref[...]
    low_ref[...] = normed.astype(jnp.bfloat16)
    places = step * steps + lax.broadcasted_iota(jnp.int32, (steps, 1), 0)
    kept = jnp.stack([jnp.where(places < count_ref[row], normed[row], 0.0) for row in range(rows)])
    for lanes in lane_slices(width):
        for unit in range(steps // LAG):
            part = slice(unit * LAG, (unit + 1) * LAG)
            turned_ref[part, :, lanes] = jnp.swapaxes(kept[:, part, lanes], 0, 1)
    for lanes in lane_slices(width):
        retain = [spread_rows(retain_ref, j, lanes, rows) for j in range(states)]

        def unit_step(unit, hidden):
            for within in range(LAG):
                entry = turned_ref[unit * LAG + within, :, lanes]
                hidden = [retain[j] * hidden[j] + entry for j in range(states)]
            return hidden

        hidden = lax.fori_loop(
            0, steps // LAG, unit_step, [state[j, :, lanes] for j in range(states)]
        )
        for j in range(states):
            state[j, :, lanes] = hidden[j]

    @pl.when(step == pl.num_programs(0) - 1)
    def _():
        end_ref[...] = state[...]


def enter_call(counts, tokens, gain, retain):
    rows, length, width = tokens.shape
    states = retain.shape[0]
    natural = pl.BlockSpec((rows, STEPS, width), lambda step: (0, step, 0))
    return pl.pallas_call(
        enter_body,
        grid=(length // STEPS,),
        in_specs=[
            pl.BlockSpec(memory_space=pltpu.SMEM),
            natural,
            whole_spec((1, width)),
            whole_spec((states, width)),
        ],
        out_specs=(
            natural,
            pl.BlockSpec((STEPS, rows, width), lambda step: (step, 0, 0)),
            whole_spec((states, rows, width)),
        ),
        out_shape=(
            jax.ShapeDtypeStruct(tokens.shape, jnp.bfloat16),
            jax.ShapeDtypeStruct((length, rows, width), jnp.float32),
            jax.ShapeDtypeStruct((states, rows, width), jnp.float32),
        ),
        scratch_shapes=[pltpu.VMEM((states, rows, width), jnp.float32)],
        compiler_params=front_params,
        cost_estimate=work_cost(0.0, 9e-6),
        name="enter",
    )(counts, tokens, gain, retain)


def average_body(turned_ref, retain_ref, mix_ref, held_ref, state, out_ref):
    step = pl.program_id(0)
    steps, rows, width = turned_ref.shape
    states = retain_ref.shape[0]

    @pl.when(step == 0)
    def _():
        state[...] = held_ref[...]

    for lanes in lane_slices(width):
        retain = [spread_rows(retain_ref, j, lanes, rows) for j in range(states)]
        mix = [spread_rows(mix_ref, j, lanes, rows) for j in range(states)]

        def unit_step(unit, hidden):
            sums = []
            for within in range(LAG):
                entry = turned_ref[unit * LAG + within, :, lanes]
                hidden = [retain[j] * hidden[j] + entry for j in range(states)]
                sums.append(add_all([mix[j] * hidden[j] for j in range(states)]))
            out_ref[:, pl.ds(unit * LAG, LAG), lanes] = jnp.swapaxes(jnp.stack(sums), 0, 1)
            return hidden

        hidden = lax.fori_loop(
            0, steps // LAG, unit_step, [state[j, :, lanes] for j in range(states)]
        )
        for j in range(states):
            state[j, :, lanes] = hidden[j]


def average_call(turned, retain, mix, start):
    length, rows, width = turned.shape
    states = retain.shape[0]
    held = (states, rows, width)
    return pl.pallas_call(
        average_body,
        grid=(length // STEPS,),
        in_specs=[
            pl.BlockSpec((STEPS, rows, width), lambda step: (step, 0, 0)),
            whole_spec((states, width)),
            whole_spec((states, width)),
            whole_spec(held),
        ],
        out_specs=(
            whole_spec(held),
            pl.BlockSpec((rows, STEPS, width), lambda step: (0, step, 0)),
        ),
        out_shape=(
            jax.ShapeDtypeStruct(held, jnp.float32),
            jax.ShapeDtypeStruct((rows, length, width), jnp.float32),
        ),
        compiler_params=front_params,
        cost_estimate=work_cost(0.0, 12e-6),
        name="average",
    )(turned, retain, mix, start)


def return_body(grad_ref, retain_ref, turned_ref, end_ref, state):
    step = pl.program_id(0)
    rows, steps, width = grad_ref.shape
    states = retain_ref.shape[0]

    @pl.when(step == 0)
    def _():
        state[...] = jnp.zeros_like(state)

    for lanes in lane_slices(width):
        retain = [spread_rows(retain_ref, j, lanes, rows) for j in range(states)]

        def unit_step(unit, hidden):
            part = pl.ds((steps // LAG - 1 - unit) * LAG, LAG)
            turned = jnp.swapaxes(grad_ref[:, part, lanes], 0, 1)
            turned_ref[part, :, lanes] = turned
            for within in reversed(range(LAG)):
                hidden = [retain[j] * hidden[j] + turned[within] for j in range(states)]
            return hidden

        hidden = lax.fori_loop(
            0, steps // LAG, unit_step, [state[j, :, lanes] for j in range(states)]
        )
        for j in range(states):
            state[j, :, lanes] = hidden[j]

    @pl.when(step == pl.num_programs(0) - 1)
    def _():
        end_ref[...] = state[...]


def return_call(grad, retain):
    rows, length, width = grad.shape
    states = retain.shape[0]
    last = length // STEPS - 1
    return pl.pallas_call(
        return_body,
        grid=(length // STEPS,),
        in_specs=[
            pl.BlockSpec((rows, STEPS, width), lambda step: (0, last - step, 0)),
            whole_spec((states, width)),
        ],
        out_specs=(
            pl.BlockSpec((STEPS, rows, width), lambda step: (last - step, 0, 0)),
            whole_spec((states, rows, width)),
        ),
        out_shape=(
            jax.ShapeDtypeStruct((length, rows, width), jnp.float32),
            jax.ShapeDtypeStruct((states, rows, width), jnp.float32),
        ),
        scratch_shapes=[pltpu.VMEM((states, rows, width), jnp.float32)],
        compiler_params=scan_params,
        cost_estimate=work_cost(0.0, 8e-6),
        name="back_enter",
    )(grad, retain)


def sums_body(
    grad_ref,
    turned_ref,
    retain_ref,
    inverse_ref,
    unit_ref,
    held_ref,
    lag_in_ref,
    carry_ref,
    lag_ref,
):
    step = pl.program_id(0)
    steps, rows, width = grad_ref.shape
    states = retain_ref.shape[0]
    half = states // 2
    units = steps // LAG

    @pl.when(step == 0)
    def _():
        carry_ref[...] = held_ref[...]
        lag_ref[...] = lag_in_ref[...]

    for lanes in lane_slices(width):
        for first in range(0, states, half):
            chosen = range(first, first + half)
            retain = [spread_rows(retain_ref, j, lanes, rows) for j in chosen]
            inverse = [spread_rows(inverse_ref, j, lanes, rows) for j in chosen]

            def unit_step(unit, carried):
                after, hidden, cross = carried
                unit = units - 1 - unit
                later = after
                for within in reversed(range(LAG)):
                    place = unit * LAG + within
                    entry = turned_ref[place, :, lanes]
                    grad = grad_ref[place, :, lanes]
                    after = [retain[m] * after[m] + grad for m in range(half)]
                    hidden = [(hidden[m] - entry) * inverse[m] for m in range(half)]
                    cross = [cross[m] + after[m] * hidden[m] for m in range(half)]
                for m, j in enumerate(chosen):
                    unit_decay = spread_rows(unit_ref, j, lanes, rows)
                    carry_ref[3, j, :, lanes] += hidden[m] * (after[m] - unit_decay * later[m])
                return after, hidden, cross

            results = lax.fori_loop(
                0,
                units,
                unit_step,
                tuple([carry_ref[kind, j, :, lanes] for j in chosen] for kind in range(3)),
            )
            for kind in range(3):
                for m, j in enumerate(chosen):
                    carry_ref[kind, j, :, lanes] = results[kind][m]

        def lag_step(unit, lags):
            entries = [turned_ref[unit * LAG + at, :, lanes] for at in range(LAG)]
            grads = [grad_ref[unit * LAG + at, :, lanes] for at in range(LAG)]
            return [
                lags[lag] + add_all([grads[at] * entries[at - lag] for at in range(lag, LAG)])
                for lag in range(LAG)
            ]

        lags = lax.fori_loop(0, units, lag_step, [lag_ref[at, :, lanes] for at in range(LAG)])
        for at in range(LAG):
            lag_ref[at, :, lanes] = lags[at]


def sums_call(low_end, high_end, grad, turned, params, carried):
    rows, width = grad.shape[1:]
    states = params[0].shape[0]
    last = high_end // STEPS - 1
    turned_spec = pl.BlockSpec((STEPS, rows, width), lambda step: (last - step, 0, 0))
    carried_specs = [whole_spec(value.shape) for value in carried]
    return pl.pallas_call(
        sums_body,
        grid=((high_end - low_end) // STEPS,),
        in_specs=[turned_spec] * 2 + [whole_spec((states, width))] * 3 + carried_specs,
        out_specs=carried_specs,
        out_shape=[jax.ShapeDtypeStruct(value.shape, jnp.float32) for value in carried],
        compiler_params=scan_params,
        cost_estimate=work_cost(0.0, 8e-6),
        name="adjoint_sums",
    )(grad, turned, *params, *carried)


def leave_body(
    count_ref,
    tokens_ref,
    gain_ref,
    part_ref,
    residual_ref,
    grad_ref,
    retain_ref,
    mix_ref,
    held_ref,
    *others,
    places_before,
):
    carry_ref, out_ref, path = others[-3:]
    step = pl.program_id(0)
    steps, rows, width = grad_ref.shape
    states = retain_ref.shape[0]
    units = steps // LAG

    @pl.when(step == 0)
    def _():
        carry_ref[...] = held_ref[...]

    for lanes in lane_slices(width):
        retain = [spread_rows(retain_ref, j, lanes, rows) for j in range(states)]
        mix = [spread_rows(mix_ref, j, lanes, rows) for j in range(states)]

        def unit_step(unit, after):
            unit = units - 1 - unit
            sums = []
            for within in reversed(range(LAG)):
                grad = grad_ref[unit * LAG + within, :, lanes]
                after = [retain[j] * after[j] + grad for j in range(states)]
                sums.append(add_all([mix[j] * after[j] for j in range(states)]))
            path[:, pl.ds(unit * LAG, LAG), lanes] = jnp.swapaxes(jnp.stack(sums[::-1]), 0, 1)
            return after

        after = lax.fori_loop(
            0, units, unit_step, [carry_ref[j, :, lanes] for j in range(states)]
        )
        for j in range(states):
            carry_ref[j, :, lanes] = after[j]

    first_place = places_before + (pl.num_programs(0) - 1 - step) * steps
    places = first_place + lax.broadcasted_iota(jnp.int32, (steps, 1), 0)
    gain = gain_ref[...]
    for row in range(rows):
        unit_values, scale = unit_norm(tokens_ref[row].astype(jnp.float32))
        grad = part_ref[row].astype(jnp.float32)
        grad = grad + jnp.where(places < count_ref[row], path[row], 0.0)
        out = norm_backward(grad * gain, unit_values, scale)
        out_ref[row] = (out + residual_ref[row].astype(jnp.float32)).astype(jnp.bfloat16)


def leave_call(
    low_end, high_end, counts, tokens, gain, part, residual, grad, retain, mix, carried
):
    rows, length, width = tokens.shape
    held = carried[0].shape
    last = high_end // STEPS - 1
    going_on = len(carried) > 1
    natural = pl.BlockSpec((rows, STEPS, width), lambda step: (0, last - step, 0))
    return pl.pallas_call(
        functools.partial(leave_body, places_before=low_end),
        grid=((high_end - low_end) // STEPS,),
        in_specs=[
            pl.BlockSpec(memory_space=pltpu.SMEM),
            natural,
            whole_spec((1, width)),
            natural,
            natural,
            pl.BlockSpec((STEPS, rows, width), lambda step: (last - step, 0, 0)),
            whole_spec(retain.shape),
            whole_spec(mix.shape),
            whole_spec(held),
        ]
        + [pl.BlockSpec(memory_space=pl.ANY)] * going_on,
        out_specs=[whole_spec(held), natural],
        out_shape=[
            jax.ShapeDtypeStruct(held, jnp.float32),
            jax.ShapeDtypeStruct((rows, length, width), jnp.bfloat16),
        ],
        input_output_aliases={9: 1} if going_on else {},
        scratch_shapes=[pltpu.VMEM((rows, STEPS, width), jnp.float32)],
        compiler_params=scan_params,
        cost_estimate=work_cost(0.0, 8e-6),
        name="leave",
    )(counts, tokens, gain, part, residual, grad, retain, mix, *carried)


class Exchange:
    def __init__(self, local, decay, axis, backward):
        self.axis, self.backward = axis, backward
        self.count = lax.axis_size(axis)
        place = lax.axis_index(axis)
        self.place = self.count - 1 - place if backward else place
        self.low = self.place % 2
        self.half = local.shape[-1] // 2
        self.local = local
        self.decay = self.part(decay, self.low)

    def part(self, value, which):
        return lax.dynamic_slice_in_dim(value, which * self.half, self.half, value.ndim - 1)

    def moved(self, value, pairs):
        last = self.count - 1
        if self.backward:
            pairs = [(last - source, last - target) for source, target in pairs]
        return lax.ppermute(value, self.axis, pairs)

    def swapped(self, value):
        return self.moved(value, [(at, at ^ 1) for at in range(self.count)])

    def later(self, value, hop):
        return self.moved(value, [(at, at + 2 * hop) for at in range(self.count - 2 * hop)])

    def share(self):
        own = self.part(self.local, self.low)
        other = self.swapped(self.part(self.local, 1 - self.low))
        self.first = jnp.where(self.low == 0, own, other)
        self.pair = self.decay * self.first + jnp.where(self.low == 0, other, own)

    def cross(self):
        pairs = self.count // 2
        decay = self.decay * self.decay
        if pairs <= 4:
            arrived = [self.later(self.pair, hop) for hop in range(1, pairs)]
            total = arrived[-1]
            for value in arrived[-2::-1]:
                total = decay * total + value
        else:
            total, hop = self.later(self.pair, 1), 1
            while hop < pairs - 1:
                total = total + decay * self.later(total, hop)
                decay = decay * decay
                hop *= 2
        self.start = total

    def give(self):
        second = self.decay * self.start + self.first
        kept = jnp.where(self.low == 0, self.start, second)
        got = self.swapped(jnp.where(self.low == 0, second, self.start))
        return jnp.concatenate(
            [jnp.where(self.low == 0, kept, got), jnp.where(self.low == 0, got, kept)], axis=-1
        )


mesh_axes = ("seq", "row")


def device_total():
    return lax.axis_size("seq") * lax.axis_size("row")


def device_place():
    return lax.axis_index("seq") * lax.axis_size("row") + lax.axis_index("row")


def swapped(value, bit):
    return lax.ppermute(value, mesh_axes, [(at, at ^ bit) for at in range(device_total())])


def half_summed(value, bit):
    half = value.shape[0] // 2
    mine = (device_place() // bit) % 2
    sent = lax.dynamic_slice_in_dim(value, (1 - mine) * half, half, 0)
    kept = lax.dynamic_slice_in_dim(value, mine * half, half, 0)
    return kept + swapped(sent, bit)


def both_halves(value, bit):
    mine = (device_place() // bit) % 2 == 1
    other = swapped(value, bit)
    return jnp.concatenate([jnp.where(mine, other, value), jnp.where(mine, value, other)], axis=0)


def link_orders():
    total = device_total()
    bits = [1 << at for at in range(total.bit_length() - 1)]
    if (lax.axis_size("seq"), lax.axis_size("row")) == (8, 4):
        core, x, y, z_low, z_high = bits
        return (
            (core, x, y, z_low, z_high),
            (core, y, z_low, x, z_high),
            (core, z_low, x, y, z_high),
        )
    third = len(bits) // 3
    return tuple(bits[turn * third :] + bits[: turn * third] for turn in range(3))


def summed_everywhere(values):
    orders = link_orders()
    for at in range(len(orders[0])):
        values = [half_summed(v, orders[n % 3][at]) for n, v in enumerate(values)]
    for at in reversed(range(len(orders[0]))):
        values = [both_halves(v, orders[n % 3][at]) for n, v in enumerate(values)]
    return values


def paired_sum(value, group):
    partners = [group[0]] if len(group) == 1 else [group[0], group[1], group[0] + group[1]]
    arrived = [swapped(value, partner) for partner in partners]
    if len(arrived) == 1:
        return value + arrived[0]
    return (value + arrived[0]) + (arrived[1] + arrived[2])


def small_sum(value):
    bits = [1 << at for at in range(device_total().bit_length() - 1)]
    for at in range(0, len(bits), 2):
        value = paired_sum(value, bits[at : at + 2])
    return value


def power_of(value, exponent):
    result = None
    while exponent:
        if exponent & 1:
            result = value if result is None else result * value
        value = value * value
        exponent >>= 1
    return result


def dot(first_op, second_op):
    return jnp.dot(first_op, second_op, preferred_element_type=jnp.float32)


def dot_back(first_op, second_op):
    return lax.dot_general(
        first_op, second_op, (((1,), (1,)), ((), ())), preferred_element_type=jnp.float32
    )


def dot_outer(first_op, second_op):
    return lax.dot_general(
        first_op, second_op, (((0,), (0,)), ((), ())), preferred_element_type=jnp.float32
    )


def low(value):
    return value.astype(jnp.bfloat16)


def chunks(low_end, high_end, size):
    return [slice(at, min(at + size, high_end)) for at in range(low_end, high_end, size)]


def gated(value):
    half = 0.5 * value
    turn = jnp.tanh(half)
    gate = 0.5 * turn + 0.5
    act = half * turn + half
    return act, gate + act * (1.0 - gate)


def value_body(normed_ref, value_weight_ref, value_ref, value_slope_ref):
    for part in chunks(0, value_ref.shape[1], 256):
        value, slope = gated(low(dot(normed_ref[...], value_weight_ref[:, part])))
        value_ref[:, part] = low(value)
        value_slope_ref[:, part] = low(slope)


def value_call(normed, value_weight):
    rows, length, width = normed.shape
    vdim = value_weight.shape[1]
    return pl.pallas_call(
        value_body,
        grid=(rows,),
        in_specs=[row_spec(length, width), once_spec(value_weight.shape)],
        out_specs=[row_spec(length, vdim)] * 2,
        out_shape=[jax.ShapeDtypeStruct((rows, length, vdim), jnp.bfloat16)] * 2,
        compiler_params=front_params,
        cost_estimate=work_cost(2e9, 5e-6),
        name="value",
    )(normed, value_weight)


def forward_body(
    count_ref,
    tokens_ref,
    cotangent_ref,
    average_ref,
    normed_ref,
    value_ref,
    value_slope_ref,
    omega_ref,
    base_weight_ref,
    gains_ref,
    biases_ref,
    output_weight_ref,
    ffn_gain_ref,
    ffn_in_ref,
    ffn_out_ref,
    out_ref,
    mixed_ref,
    mixed_slope_ref,
    product_ref,
    ffn_low_ref,
    act_ref,
    grad_inner_ref,
    grad_proj_ref,
    grad_main_ref,
    grad_shared_ref,
    grad_vpre_ref,
    residual_ref,
    ffn_gain_grad_ref,
    grad_gains_ref,
    reset_ref,
    reset_slope_ref,
    grad_attended_ref,
    probs_ref,
    query_ref,
    key_ref,
    shared_ref,
    shared_slope_ref,
):
    row = pl.program_id(0)
    length, width = tokens_ref.shape
    zdim = query_ref.shape[1]
    vdim = value_ref.shape[1]
    inner = act_ref.shape[1]

    @pl.when(row == 0)
    def _():
        ffn_gain_grad_ref[...] = jnp.zeros_like(ffn_gain_grad_ref)
        grad_gains_ref[...] = jnp.zeros_like(grad_gains_ref)

    normed = normed_ref[...]
    sums = average_ref[...] + omega_ref[...] * normed.astype(jnp.float32)
    gate = sigmoid(sums)
    mixed = sums * gate
    mixed_ref[...] = low(mixed)
    mixed_slope_ref[...] = low(gate + mixed * (1.0 - gate))
    mixed_low = mixed_ref[...]

    shared = dot(mixed_low, base_weight_ref[:, :zdim])
    gate = sigmoid(shared)
    shared_act = shared * gate
    shared_ref[...] = shared_act
    shared_slope_ref[...] = gate + shared_act * (1.0 - gate)
    query_ref[...] = low(shared_act * gains_ref[0:1] + biases_ref[0:1])
    key_ref[...] = low(shared_act * gains_ref[1:2] + biases_ref[1:2])

    to_place = lax.broadcasted_iota(jnp.int32, (GROUP, GROUP), 0)
    from_place = lax.broadcasted_iota(jnp.int32, (GROUP, GROUP), 1)
    for block in chunks(0, length, GROUP):
        allowed = (from_place <= to_place) & (
            (from_place < count_ref[row] - block.start) | (from_place == to_place)
        )
        scores = dot_back(query_ref[block], key_ref[block]) * zdim**-0.5
        scores = jnp.where(allowed, scores, very_low)
        weights = jnp.exp(scores - jnp.max(scores, axis=-1, keepdims=True))
        weights = jnp.where(allowed, weights, 0.0)
        probs_ref[block] = weights / jnp.sum(weights, axis=-1, keepdims=True)

    for part in chunks(0, vdim, 256):
        base_part = slice(zdim + part.start, zdim + part.stop)
        reset_act, reset_slope = gated(low(dot(mixed_low, base_weight_ref[:, base_part])))
        reset_ref[:, part] = low(reset_act)
        for block in chunks(0, length, GROUP):
            attended = low(dot(low(probs_ref[block]), value_ref[block, part]))
            product_ref[block, part] = low(attended * reset_act[block])
            reset_slope_ref[block, part] = low(attended * reset_slope[block])

    update_gate = sigmoid(dot(mixed_low, base_weight_ref[:, zdim + vdim : zdim + vdim + width]))
    candidate = dot(mixed_low, base_weight_ref[:, zdim + vdim + width :])
    candidate = candidate + dot(product_ref[...], output_weight_ref[...])
    candidate_gate = sigmoid(candidate)
    candidate_act = candidate * candidate_gate
    candidate_slope = candidate_gate + candidate_act * (1.0 - candidate_gate)
    tokens = tokens_ref[...].astype(jnp.float32)
    change = candidate_act - tokens
    after = tokens + update_gate * change
    unit_values, scale = unit_norm(after)
    ffn_low_ref[...] = low(unit_values * ffn_gain_ref[...])
    ffn_low = ffn_low_ref[...]
    cotangent = cotangent_ref[...]

    out = after
    grad_normed = jnp.zeros_like(after)
    for part in chunks(0, inner, 256):
        act, slope = gated(low(dot(ffn_low, ffn_in_ref[:, part])))
        act_ref[:, part] = low(act)
        grad_act = low(dot_back(cotangent, ffn_out_ref[part]))
        grad_inner_ref[:, part] = low(grad_act * slope)
    out = after + dot(act_ref[...], ffn_out_ref[...])
    out_ref[...] = low(out)
    grad_normed = dot_back(grad_inner_ref[...], ffn_in_ref[...])
    ffn_gain_grad_ref[...] += jnp.sum(grad_normed * unit_values, axis=0, keepdims=True)
    grad_after = cotangent.astype(jnp.float32) + norm_backward(
        grad_normed * ffn_gain_ref[...], unit_values, scale
    )
    grad_change = grad_after * update_gate
    grad_proj = low(grad_change * candidate_slope)
    grad_proj_ref[...] = grad_proj
    grad_main_ref[:, vdim : vdim + width] = low(grad_change * change * (1.0 - update_gate))
    grad_main_ref[:, vdim + width :] = grad_proj
    for part in chunks(0, vdim, 256):
        grad_product = low(dot_back(grad_proj, output_weight_ref[part]))
        grad_attended_ref[:, part] = low(grad_product * reset_ref[:, part])
        grad_main_ref[:, part] = low(grad_product * reset_slope_ref[:, part])

    grad_gains = jnp.zeros(grad_gains_ref.shape, jnp.float32)
    for block in chunks(0, length, GROUP):
        probs = probs_ref[block]
        probs_low = low(probs)
        grad_probs = dot_back(grad_attended_ref[block], value_ref[block])
        for part in chunks(0, vdim, 512):
            grad_value = dot_outer(probs_low, grad_attended_ref[block, part])
            grad_vpre_ref[block, part] = low(low(grad_value) * value_slope_ref[block, part])
        total = jnp.sum(grad_probs * probs, axis=-1, keepdims=True)
        grad_raw = low(probs * (grad_probs - total) * zdim**-0.5)
        grad_query = dot(grad_raw, key_ref[block])
        grad_key = dot_outer(grad_raw, query_ref[block])
        shared = shared_ref[block]
        grad_gains = grad_gains + jnp.concatenate(
            [
                jnp.sum(value, axis=0, keepdims=True)
                for value in (grad_query * shared, grad_key * shared, grad_query, grad_key)
            ],
            axis=0,
        )
        grad_shared = grad_query * gains_ref[0:1] + grad_key * gains_ref[1:2]
        grad_shared_ref[block] = low(grad_shared * shared_slope_ref[block])
    grad_gains_ref[...] += grad_gains
    residual_ref[...] = low(grad_after - grad_change)


def row_spec(length, width):
    return pl.BlockSpec((None, length, width), lambda row: (row, 0, 0))


def once_spec(shape):
    return pl.BlockSpec(shape, lambda row: (0,) * len(shape), pipeline_mode=pl.Buffered(1))


def forward_call(
    counts,
    tokens,
    cotangent,
    average,
    normed,
    value,
    value_slope,
    omega,
    base_weight,
    gains,
    biases,
    output_weight,
    ffn_gain,
    ffn_in,
    ffn_out,
):
    rows, length, width = tokens.shape
    zdim, vdim, inner = gains.shape[1], value.shape[2], ffn_in.shape[1]
    half, full = jnp.bfloat16, jnp.float32
    outs = [
        (width, half),
        (width, half),
        (width, half),
        (vdim, half),
        (width, half),
        (inner, half),
        (inner, half),
        (width, half),
        (vdim + 2 * width, half),
        (zdim, half),
        (vdim, half),
        (width, half),
    ]
    tied = [
        omega,
        base_weight,
        gains,
        biases,
        output_weight,
        ffn_gain,
        ffn_in,
        ffn_out,
    ]
    return pl.pallas_call(
        forward_body,
        grid=(rows,),
        in_specs=[pl.BlockSpec(memory_space=pltpu.SMEM)]
        + [row_spec(length, width)] * 4
        + [row_spec(length, vdim)] * 2
        + [once_spec(weight.shape) for weight in tied],
        out_specs=[row_spec(length, size) for size, _ in outs]
        + [whole_spec((1, width)), whole_spec((4, zdim))],
        out_shape=[jax.ShapeDtypeStruct((rows, length, size), kind) for size, kind in outs]
        + [jax.ShapeDtypeStruct((1, width), full), jax.ShapeDtypeStruct((4, zdim), full)],
        scratch_shapes=[pltpu.VMEM((length, vdim), half)] * 3
        + [pltpu.VMEM((length, GROUP), full)]
        + [pltpu.VMEM((length, zdim), half)] * 2
        + [pltpu.VMEM((length, zdim), full)] * 2,
        compiler_params=front_params,
        cost_estimate=work_cost(18e9, 40e-6),
        name="dense_forward",
    )(counts, tokens, cotangent, average, normed, value, value_slope, *tied)


def backward_body(
    grad_main_ref,
    grad_shared_ref,
    grad_vpre_ref,
    normed_ref,
    mixed_slope_ref,
    omega_ref,
    value_weight_ref,
    base_weight_ref,
    grad_average_ref,
    part_ref,
    grad_omega_ref,
    grad_gain_ref,
):
    zdim = grad_shared_ref.shape[1]

    @pl.when(pl.program_id(0) == 0)
    def _():
        grad_omega_ref[...] = jnp.zeros_like(grad_omega_ref)
        grad_gain_ref[...] = jnp.zeros_like(grad_gain_ref)

    grad_average = dot_back(grad_main_ref[...], base_weight_ref[:, zdim:])
    grad_average = grad_average + dot_back(grad_shared_ref[...], base_weight_ref[:, :zdim])
    grad_average = grad_average * mixed_slope_ref[...].astype(jnp.float32)
    grad_average_ref[...] = grad_average
    part = dot_back(grad_vpre_ref[...], value_weight_ref[...]) + grad_average * omega_ref[...]
    part_ref[...] = part
    normed = normed_ref[...].astype(jnp.float32)
    grad_omega_ref[...] += jnp.sum(grad_average * normed, axis=0, keepdims=True)
    grad_gain_ref[...] += jnp.sum(part * normed, axis=0, keepdims=True)


def backward_call(inputs, tied_inputs):
    rows, length, _ = inputs[0].shape
    width = tied_inputs[0].shape[1]
    return pl.pallas_call(
        backward_body,
        grid=(rows,),
        in_specs=[row_spec(length, value.shape[2]) for value in inputs]
        + [once_spec(value.shape) for value in tied_inputs],
        out_specs=[row_spec(length, width)] * 2 + [whole_spec((1, width))] * 2,
        out_shape=[jax.ShapeDtypeStruct((rows, length, width), jnp.float32)] * 2
        + [jax.ShapeDtypeStruct((1, width), jnp.float32)] * 2,
        compiler_params=dense_params,
        cost_estimate=work_cost(7e9, 12e-6),
        name="dense_backward",
    )(*inputs, *tied_inputs)


def joined_body(*refs, widths, split):
    refs = refs[1:] if split else refs
    outs_per_chain = 2 if split else 1
    outs = refs[len(refs) - outs_per_chain * len(widths) :]
    at = 0
    for chain, parts in enumerate(widths):
        for side in range(outs_per_chain):
            column = 0
            for width in parts:
                total = refs[at][...] + refs[at + 1][...]
                outs[chain * outs_per_chain + side][:, column : column + width] = total
                column += width
                at += 2


def joined(chains):
    split = chains[0][2] is not None
    sides = 2 if split else 1
    widths = [[value.shape[1] for value in kept] for kept, _, _ in chains]
    sizes = [kept[0].shape[0] // sides for kept, _, _ in chains]
    steps = 4
    while any(size % (8 * steps) for size in sizes):
        steps //= 2
    operands, in_specs, out_specs, out_shape = [], [], [], []
    for chain, (kept, arrived, _) in enumerate(chains):
        block = sizes[chain] // steps
        for side in range(sides):

            def place(step, *held, chain=chain, side=side):
                if not held:
                    return step, 0
                mine = held[0][chain]
                return (1 - mine if side else mine) * steps + step, 0

            for pair in zip(kept, arrived):
                for value in pair:
                    operands.append(value)
                    in_specs.append(pl.BlockSpec((block, value.shape[1]), place))
            total = sum(widths[chain])
            out_specs.append(pl.BlockSpec((block, total), lambda step, *held: (step, 0)))
            out_shape.append(jax.ShapeDtypeStruct((sizes[chain], total), jnp.float32))
    if split:
        mine = [(device_place() // bit) % 2 for _, _, bit in chains]
        operands.insert(0, jnp.stack(mine).astype(jnp.int32))
    outs = pl.pallas_call(
        functools.partial(joined_body, widths=widths, split=split),
        grid_spec=pltpu.PrefetchScalarGridSpec(
            num_scalar_prefetch=1 if split else 0,
            grid=(steps,),
            in_specs=in_specs,
            out_specs=out_specs,
        ),
        out_shape=out_shape,
        compiler_params=scan_params,
        cost_estimate=work_cost(0.0, 2e-6),
        name="joined",
    )(*operands)
    return [tuple(outs[at : at + sides]) for at in range(0, len(outs), sides)]


def placed_body(*refs, copies, sources):
    mine, refs = refs[0], refs[1:]
    half = pl.program_id(0)
    for own, arrived, which, taken, result, column in copies:
        there = slice(column, column + taken.stop - taken.start)

        @pl.when(half == mine[which])
        def _(own=own, taken=taken, result=result, there=there):
            refs[sources + result][:, there] = refs[own][:, taken]

        @pl.when(half != mine[which])
        def _(arrived=arrived, taken=taken, result=result, there=there):
            refs[sources + result][:, there] = refs[arrived][:, taken]


def placed(values, bits, copies, shapes):
    steps = 4
    while any(value.shape[0] % (8 * steps) for value in values):
        steps //= 2
    in_specs = []
    for at, value in enumerate(values):

        def place(half, step, mine, which=at // 2, other=at % 2):
            wanted = (half == mine[which]) != bool(other)
            return jnp.where(wanted, step, jnp.where(half == 0, 0, steps - 1)), 0

        in_specs.append(pl.BlockSpec((value.shape[0] // steps, value.shape[1]), place))
    mine = jnp.stack([(device_place() // bit) % 2 for bit in bits]).astype(jnp.int32)
    return pl.pallas_call(
        functools.partial(placed_body, copies=copies, sources=len(values)),
        grid_spec=pltpu.PrefetchScalarGridSpec(
            num_scalar_prefetch=1,
            grid=(2, steps),
            in_specs=in_specs,
            out_specs=[
                pl.BlockSpec(
                    (shape[0] // (2 * steps), shape[1]),
                    lambda half, step, mine: (half * steps + step, 0),
                )
                for shape in shapes
            ],
        ),
        out_shape=[jax.ShapeDtypeStruct(shape, jnp.float32) for shape in shapes],
        compiler_params=scan_params,
        cost_estimate=work_cost(0.0, 2e-6),
        name="placed",
    )(mine, *values)


def gathered_body(*refs, bits, copies, results, others, per_row):
    sources = refs[: 2 * len(bits)]
    outs = refs[len(refs) - results - len(sources) - 2 : len(refs) - len(sources) - 2]
    held, (in_sems, out_sems) = refs[len(refs) - len(sources) - 2 : -2], refs[-2:]
    place = lax.axis_index("seq") * per_row + lax.axis_index("row")
    arriving = []
    for at, source in enumerate(sources):
        copy = pltpu.make_async_copy(source, held[at], in_sems.at[at])
        copy.start()
        arriving.append(copy)
    leaving = []
    for at, source in enumerate(sources):
        high_bit, low_bit = bits[at // 2]
        high = (place // high_bit) % 2
        low_side = (place // low_bit) % 2
        if others:
            high = 1 - high
        if at % 2:
            low_side = 1 - low_side
        rows = source.shape[0]
        there = pl.ds(pl.multiple_of((2 * high + low_side) * rows, 8), rows)
        arriving[at].wait()
        for chain, taken, result, column in copies:
            if chain == at // 2:
                copy = pltpu.make_async_copy(
                    held[at].at[:, taken],
                    outs[result].at[there, column : column + taken.stop - taken.start],
                    out_sems.at[len(leaving)],
                )
                copy.start()
                leaving.append(copy)
    for copy in leaving:
        copy.wait()


def gathered(chains, copies, shapes, before=None):
    values = []
    for one in chains:
        values += one.held if before is None else one.arrived
    anywhere = pl.BlockSpec(memory_space=pl.ANY)
    aliases = {}
    if before is not None:
        aliases = {len(values) + at: at for at in range(len(shapes))}
    return pl.pallas_call(
        functools.partial(
            gathered_body,
            bits=[one.order[:2] for one in chains],
            copies=copies,
            results=len(shapes),
            others=before is not None,
            per_row=lax.axis_size("row"),
        ),
        in_specs=[anywhere] * (len(values) + len(aliases)),
        out_specs=[anywhere] * len(shapes),
        out_shape=[jax.ShapeDtypeStruct(shape, jnp.float32) for shape in shapes],
        input_output_aliases=aliases,
        scratch_shapes=[pltpu.VMEM(value.shape, jnp.float32) for value in values]
        + [
            pltpu.SemaphoreType.DMA((len(values),)),
            pltpu.SemaphoreType.DMA((2 * len(copies),)),
        ],
        compiler_params=scan_params,
        cost_estimate=work_cost(0.0, 6e-6),
        name="gathered",
    )(*values, *(before or ()))


class Chain:
    def __init__(self, order, sent, kept):
        self.order, self.at = order, 0
        self.sent, self.kept, self.arrived = list(sent), list(kept), []

    def state(self):
        return self.sent, self.kept, self.arrived

    def set_state(self, state):
        self.sent, self.kept, self.arrived = state

    def send(self):
        total = len(self.order)
        bit = self.order[self.at if self.at < total else 2 * total - 1 - self.at]
        self.arrived = [swapped(value, bit) for value in self.sent]

    def give(self):
        self.held = self.sent + self.arrived
        self.arrived = [swapped(value, self.order[0]) for value in self.held]

    def pieces(self):
        return self.held + self.arrived


def join(*chains):
    total = len(chains[0].order)
    if chains[0].at < total:
        last = chains[0].at == total - 1
        results = joined(
            [
                (one.kept, one.arrived, None if last else one.order[one.at + 1])
                for one in chains
            ]
        )
        for one, result in zip(chains, results):
            if last:
                one.sent, one.kept = [result[0]], []
            else:
                one.sent, one.kept = [result[1]], [result[0]]
    else:
        values, copies, shapes = [], [], []
        for at, one in enumerate(chains):
            rows, columns = one.sent[0].shape
            values += [one.sent[0], one.arrived[0]]
            copies.append((2 * at, 2 * at + 1, at, slice(0, columns), at, 0))
            shapes.append((2 * rows, columns))
        bits = [one.order[2 * total - 1 - one.at] for one in chains]
        for one, result in zip(chains, placed(values, bits, copies, shapes)):
            one.sent = [result]
    for one in chains:
        one.arrived = []
        one.at += 1


def tied(value, *chains):
    value, states = lax.optimization_barrier((value, [one.state() for one in chains]))
    for one, state in zip(chains, states):
        one.set_state(state)
    return value


def weight_halves(first_op, second_op, bit):
    first_op = first_op.reshape(-1, first_op.shape[-1])
    second_op = second_op.reshape(-1, second_op.shape[-1])
    half = first_op.shape[1] // 2
    mine = (device_place() // bit) % 2
    return [
        dot_outer(lax.dynamic_slice_in_dim(first_op, which * half, half, 1), second_op)
        for which in (1 - mine, mine)
    ]


def weight_grad(first_op, second_op):
    return dot_outer(
        first_op.reshape(-1, first_op.shape[-1]), second_op.reshape(-1, second_op.shape[-1])
    )


def per_device(
    tokens,
    valid_count,
    norm_gain,
    value_weight,
    ema_forget,
    ema_beta,
    ema_eta,
    ema_omega,
    base_weight,
    qk_gain,
    qk_bias,
    output_weight,
    ffn_gain,
    ffn_in,
    ffn_out,
    cotangent,
):
    length, width = tokens.shape[1:]
    counts = valid_count - lax.axis_index("seq") * length
    norm_gain = norm_gain.astype(jnp.float32)[None]
    ffn_gain = ffn_gain.astype(jnp.float32)[None]
    omega = ema_omega[None]
    gains, biases = qk_gain.astype(jnp.float32), qk_bias.astype(jnp.float32)
    forget, beta, eta = ema_forget.T, ema_beta.T, ema_eta.T
    retain = 1.0 - forget
    gate = jnp.sqrt(forget * (2.0 - forget))
    inflow = beta * gate
    mix = eta * inflow
    span_decay = power_of(retain, length)[:, None, :]

    normed, turned, device_end = enter_call(counts, tokens, norm_gain, retain)
    ahead = Exchange(device_end, span_decay, "seq", False)
    ahead.share()
    ahead.cross()
    value, value_slope = value_call(normed, value_weight)
    ahead.start, value, value_slope = lax.optimization_barrier((ahead.start, value, value_slope))
    incoming = ahead.give()
    state_end, average = average_call(turned, retain, mix, incoming)
    unit_decay = power_of(retain, LAG)
    (
        block_out,
        mixed,
        mixed_slope,
        product,
        ffn_low,
        act,
        grad_inner,
        grad_proj,
        grad_main,
        grad_shared,
        grad_vpre,
        residual,
        grad_ffn_gain,
        grad_query_key,
    ) = forward_call(
        counts,
        tokens,
        cotangent,
        average,
        normed,
        value,
        value_slope,
        omega,
        base_weight,
        gains,
        biases,
        output_weight,
        ffn_gain,
        ffn_in,
        ffn_out,
    )
    orders = link_orders()
    core = orders[0][0]
    chained = device_total() == 32
    chains = []
    back_inputs = [grad_main, grad_shared, grad_vpre, normed, mixed_slope]
    if chained:
        products = [
            [(act, cotangent), (product, grad_proj)],
            [(mixed, grad_main)],
            [(ffn_low, grad_inner), (normed, grad_vpre), (mixed, grad_shared)],
        ]
        halves = [[weight_halves(*pair, core) for pair in pairs] for pairs in products]
        for order, pairs in zip(orders, halves):
            chains.append(Chain(order, [pair[0] for pair in pairs], [pair[1] for pair in pairs]))
            chains[-1].send()
        join(*chains)
        back_inputs = tied(back_inputs, *chains)
        for one in chains:
            one.send()
    grad_average, part, grad_omega, grad_gain = backward_call(
        back_inputs, [omega, value_weight, base_weight]
    )

    def halve(value):
        if chained:
            value = tied(value, *chains)
            join(*chains)
            value = tied(value, *chains)
            for one in chains:
                one.send()
        return value

    grad_turned, device_start = return_call(grad_average, retain)
    behind = Exchange(device_start, span_decay, "seq", True)
    behind.share()
    behind.pair = halve(behind.pair)
    behind.cross()
    behind.start = halve(behind.start)
    later = behind.give()
    states = retain.shape[0]
    carried = [
        jnp.stack([later, state_end, jnp.zeros_like(later), jnp.zeros_like(later)]),
        jnp.zeros((LAG,) + later.shape[1:], jnp.float32),
    ]
    parts = length // STEPS
    inverse = 1.0 / retain
    ends = [at * STEPS // 8 for at in (8 * parts, 4 * parts, 2 * parts, 0)]
    ends = [at // STEPS * STEPS for at in ends]
    for high_end, low_end in zip(ends, ends[1:]):
        carried = halve(carried)
        carried = sums_call(
            low_end, high_end, grad_turned, turned, [retain, inverse, unit_decay], carried
        )
    carry, lags = carried
    ends = [at * STEPS for at in (parts, parts // 2, 0)]
    left = [later]
    for high_end, low_end in zip(ends, ends[1:]):
        left, carry, lags = halve((left, carry, lags))
        left = leave_call(
            low_end,
            high_end,
            counts,
            tokens,
            norm_gain,
            part,
            residual,
            grad_turned,
            retain,
            mix,
            left,
        )
    left, carry, lags = lax.optimization_barrier((left, carry, lags))
    cross, border = jnp.sum(carry[2:], axis=2)
    lags = jnp.sum(lags, axis=1)
    paired = retain * border
    decay = jnp.ones_like(retain)
    for lag in range(LAG):
        paired = paired + decay * lags[lag]
        decay = decay * retain
    small = jnp.concatenate(
        [
            paired,
            cross,
            grad_gain,
            grad_omega,
            grad_ffn_gain,
            grad_query_key.reshape(-1, width),
        ],
        axis=0,
    )
    used = small.shape[0]
    small = jnp.pad(small, ((0, -used % 8), (0, 0)))
    grad_tokens = left[1]
    vdim = value_weight.shape[1]
    if chained:
        small = tied(small, *chains)
        small = small + swapped(small, core)
        for one in chains:
            one.give()
        zdim, main_end, inner_dim = gains.shape[1], grad_main.shape[-1], ffn_in.shape[1]
        copies = [
            (0, slice(0, width), 0, 0),
            (0, slice(width, 2 * width), 1, 0),
            (1, slice(0, main_end), 2, zdim),
            (2, slice(inner_dim + vdim, inner_dim + vdim + zdim), 2, 0),
            (2, slice(0, inner_dim), 3, 0),
            (2, slice(inner_dim, inner_dim + vdim), 4, 0),
        ]
        shapes = [
            ffn_out.shape,
            output_weight.shape,
            base_weight.shape,
            ffn_in.shape,
            value_weight.shape,
        ]
        first = gathered(chains, copies, shapes)
        small = paired_sum(small, orders[0][1:3])
        small, first = tied((small, first), *chains)
        small = paired_sum(small, orders[0][3:5])
    else:
        small = small_sum(small)
    paired, cross = small[:states], small[states : 2 * states]
    grad_gain, grad_omega, grad_ffn_gain = (small[2 * states + at] for at in range(3))
    grad_norm_gain = (grad_gain + jnp.sum(mix * paired, axis=0)) / norm_gain[0]
    grad_query_key = small[2 * states + 3 : used].reshape(grad_query_key.shape)
    grad_eta = (inflow * paired).T
    grad_beta = (eta * paired * gate).T
    grad_forget = (eta * paired * beta * (1.0 - forget) / gate - mix * cross).T
    vdim = value_weight.shape[1]
    if chained:
        (
            grad_ffn_out,
            grad_output_weight,
            grad_base_weight,
            grad_ffn_in,
            grad_value_weight,
        ) = gathered(chains, copies, shapes, first)
    else:
        grad_base = jnp.concatenate([grad_shared, grad_main], axis=-1)
        (
            grad_ffn_out,
            grad_output_weight,
            grad_base_weight,
            grad_ffn_in,
            grad_value_weight,
        ) = summed_everywhere(
            [
                weight_grad(act, cotangent),
                weight_grad(product, grad_proj),
                weight_grad(mixed, grad_base),
                weight_grad(ffn_low, grad_inner),
                weight_grad(normed, grad_vpre),
            ]
        )
    return (
        block_out,
        grad_tokens,
        grad_norm_gain,
        grad_value_weight,
        grad_forget,
        grad_beta,
        grad_eta,
        grad_omega,
        grad_base_weight,
        grad_query_key[:2],
        grad_query_key[2:],
        grad_output_weight,
        grad_ffn_gain,
        grad_ffn_in,
        grad_ffn_out,
    )


def solution(mesh):
    return jax.shard_map(
        per_device,
        mesh=mesh,
        in_specs=(
            P("row", "seq", None),
            P("row"),
            P(),
            P(),
            P(),
            P(),
            P(),
            P(),
            P(),
            P(),
            P(),
            P(),
            P(),
            P(),
            P(),
            P("row", "seq", None),
        ),
        out_specs=(
            P("row", "seq", None),
            P("row", "seq", None),
            P(),
            P(),
            P(),
            P(),
            P(),
            P(),
            P(),
            P(),
            P(),
            P(),
            P(),
            P(),
            P(),
        ),
        check_vma=False,
    )
```
